32 devices in a mesh: dp: 2 (over x), expert: 16 (over z, y, core).
Axes of the slice: x: 2, y: 2, z: 4, core: 2. Of those that a mesh axis runs over, the one named last changes fastest.
Arguments:
- tokens: bfloat16 [2, 1024, 2048], P(None, 'expert', 'dp'), may hold values from -6 to 6
- cotangent: bfloat16 [2, 1024, 2048], P(None, 'expert', 'dp'), may hold values from -6 to 6
- routes: int32 [2, 1024, 2], P(None, 'expert'), may hold values from 0 to 15, all different within a row; in each aligned block of 64 rows (0 to 63, 64 to 127, ..., all dimensions but the last counted through in order) at most 12 rows name the same one
- gates: float32 [2, 1024, 2], P(None, 'expert'), may hold values from 0.25 to 1
- source: int32 [16], replicated, may hold values from 0 to 15, as said below
- w_gate_up: bfloat16 [16, 2048, 2, 1024], P('expert', None, None, 'dp'), may hold values from -0.125 to 0.125
- w_down: bfloat16 [16, 1024, 2048], P('expert', 'dp'), may hold values from -0.1875 to 0.1875
- moment_first: bfloat16 [16, 1024, 2048], P('expert', 'dp'), may hold values from -6 to 6
- moment_second: bfloat16 [16, 1024, 2048], P('expert', 'dp'), may hold values from 0.25 to 4
Outputs:
- layer_out: bfloat16 [2, 1024, 2048], P(None, 'expert', 'dp')
- token_grad: bfloat16 [2, 1024, 2048], P(None, 'expert', 'dp')
- update_dir: bfloat16 [16, 1024, 2048], P('expert', 'dp')
- new_first: bfloat16 [16, 1024, 2048], P('expert', 'dp')
- new_second: bfloat16 [16, 1024, 2048], P('expert', 'dp')
The draws below stay inside these ranges and needn't reach their ends.
Inputs may be any that keep to these rules, and one draw needn't show every extreme that they name: `routes`: in each micro-batch, the 64 tokens of one index of expert name no expert more than 12 times, a bound that some block reaches. source[source[s]] = s for every slot; 8 slots take another slot's expert.
All inputs are finite; a program needn't handle non-finite values.
Results may differ from the reference program's by a relative error of at most 0.018.
Values may be sent and summed in bfloat16 or wider, within the bound.
No kernel may reach another device: no remote copies, remote signals or barrier semaphores. Data moves between devices by JAX's collectives and lax.ppermute only.
A program may use at most 128 MiB of HBM per device.

```python
import math
import jax
import jax.numpy as jnp
import numpy as np
from jax import lax

D = 2048
FF = 1024
TOP = 2
MB = 2
TOK_MB = 64
EXPERTS = 16
TOKENS = 1024
CAP = 12
N_DP = 2


def draw_source(key, part):
    order = jax.random.permutation(key, EXPERTS).astype(jnp.int32)
    pair_count = EXPERTS // 4
    first_half = order[0:2 * pair_count:2]
    second = order[1:2 * pair_count:2]
    mapping = jnp.arange(EXPERTS, dtype=jnp.int32)
    mapping = mapping.at[first_half].set(second).at[second].set(first_half)
    return mapping


def shard_levels(rng, shape, pieces, low, largest):
    level, own = 1.0, jax.random.fold_in(rng, 6)
    for dim, blocks in pieces:
        heights = jnp.exp(jax.random.uniform(jax.random.fold_in(own, dim), (blocks,), jnp.float32, low / len(pieces), largest / len(pieces)))
        level = level * jnp.repeat(heights, shape[dim] // blocks).reshape([-1 if axis == dim else 1 for axis in range(len(shape))])
    return level


def shared_out(own_key, own, number, rows, amount, top, most, skew):
    ranking = jax.random.permutation(own_key, amount)
    heavy_load, ordinary = shares(amount, rows * top, most, skew, True), shares(amount, rows * top, most, skew, False)
    places = jnp.arange(amount)

    def named(lengths, offset_by):
        used = int((lengths > 0).sum())
        fixed = max(1, used // 4)
        shifted = fixed + (places - fixed + offset_by * (used - fixed)) % max(1, amount - fixed)
        return jnp.zeros((amount,), jnp.int32).at[ranking[jnp.where(places < fixed, places, shifted)]].set(jnp.asarray(lengths, jnp.int32))

    lengths = jnp.where(number % 4 == 0, named(heavy_load, number // 4), named(ordinary, number - number // 4 - 1))
    mixed = jax.random.permutation(jax.random.fold_in(own, 3), amount)
    source_of, sink = mixed[0:amount // 2 * 2:2], mixed[1:amount // 2 * 2:2]
    room = jnp.minimum(lengths[source_of] - 1, most - lengths[sink]) // 2
    room = jnp.where((source_of == ranking[0]) | (sink == ranking[0]) | (lengths[sink] == 0), 0, jnp.maximum(room, 0))
    shifted = jax.random.randint(jax.random.fold_in(own, 4), (amount // 2,), 0, 1 << 20) % (room + 1)
    lengths = lengths.at[source_of].add(-shifted).at[sink].add(shifted)
    members = jnp.searchsorted(jnp.cumsum(lengths), jnp.arange(rows * top), side="right").astype(jnp.int32)
    grid = members.reshape(top, rows).T
    grid = grid[jax.random.permutation(jax.random.fold_in(own, 1), rows)]
    offset_by = jax.random.randint(jax.random.fold_in(own, 2), (rows, 1), 0, top)
    return jnp.take_along_axis(grid, (jnp.arange(top)[None, :] + offset_by) % top, axis=1)


def shares(count, total, limit, lean, full):
    weights = [(1 << 20) // math.isqrt(rank ** lean) + 1 for rank in range(1, count + 1)]
    largest = limit if full else min(limit, max(-(-total // count), total * weights[0] // sum(weights)))
    least = 1 if total - largest >= count - 1 else 0
    holding, rest = [largest] + [least] * (count - 1), total - largest - least * (count - 1)
    while rest > 0:
        candidates = [i for i in range(1, count) if holding[i] < largest] or [i for i in range(1, count) if holding[i] < limit]
        whole, budget = sum([weights[i] for i in candidates]), rest
        for i in candidates:
            extra = min(limit - holding[i], max(1, budget * weights[i] // whole), rest)
            holding[i] = holding[i] + extra
            rest = rest - extra
    return np.array(holding)


def gaussian(stream_key, extent, spread, most, shards=(), held_as=jnp.bfloat16):
    entries = spread * jax.random.normal(stream_key, extent, jnp.float32)
    if shards:
        entries = entries * shard_levels(stream_key, extent, shards, -0.22, 0.18)
    return jnp.clip(entries, -most, most).astype(held_as)


def setup_inputs(seed: int = 0) -> dict:
    streams_of = jax.random.split(jax.random.key(seed), 10)
    tokens = gaussian(streams_of[0], (MB, TOKENS, D), 1.0, 6.0, ((1, 16), (2, 2)))
    cotangent = gaussian(streams_of[1], (MB, TOKENS, D), 1.0, 6.0, ((1, 16), (2, 2)))
    routes_keys = jax.random.split(jax.random.fold_in(streams_of[2], 1), MB * TOKENS // TOK_MB)
    routes_turns = jax.random.permutation(jax.random.fold_in(streams_of[2], 3), MB * TOKENS // TOK_MB)
    routes = jax.vmap(lambda own, number: shared_out(jax.random.fold_in(streams_of[2], 2), own, number, TOK_MB, EXPERTS, TOP, CAP, 2))(routes_keys, routes_turns).reshape((MB, TOKENS, TOP))
    gates = jnp.clip(0.25 + 0.75 * jax.random.uniform(streams_of[3], (MB, TOKENS, TOP), jnp.float32) ** shard_levels(streams_of[3], (MB, TOKENS, TOP), ((1, 16),), -0.2, 0.2), 0.25, 1.0)
    source = draw_source(jax.random.fold_in(streams_of[9], 71), 0)
    w_gate_up = gaussian(streams_of[5], (EXPERTS, D, 2, FF), D ** -0.5, 0.125, ((0, 16), (3, 2)))
    w_down = gaussian(streams_of[6], (EXPERTS, FF, D), FF ** -0.5, 0.1875, ((0, 16), (1, 2)))
    moment_first = gaussian(streams_of[7], (EXPERTS, FF, D), 1.0, 6.0, ((0, 16), (1, 2)))
    moment_second = jnp.clip(jnp.exp(math.log(4.0) - 2.7725887 * jax.random.uniform(streams_of[8], (EXPERTS, FF, D), jnp.float32) ** shard_levels(streams_of[8], (EXPERTS, FF, D), ((0, 16), (1, 2)), -0.2, 0.2)), 0.25, 4.0).astype(jnp.bfloat16)
    return dict(tokens=tokens, cotangent=cotangent, routes=routes, gates=gates, source=source, w_gate_up=w_gate_up, w_down=w_down, moment_first=moment_first, moment_second=moment_second)


def expert_pass(inputs):
    row_tokens, row_grads, gate_up, down, moment_one, moment_two = inputs
    group_width = FF // N_DP
    down_grad = jnp.zeros((FF, D), jnp.float32)
    outputs = []
    input_grads = []
    gate_up_flat = gate_up.reshape(D, 2 * FF)
    for micro in range(MB):
        expert_in = row_tokens[micro]
        grad_in = row_grads[micro]
        both = jnp.dot(expert_in, gate_up_flat, preferred_element_type=jnp.float32).reshape(-1, 2, FF)
        gate_pre = both[:, 0]
        up_pre = both[:, 1]
        gate_sig = jax.nn.sigmoid(gate_pre)
        hidden = (gate_pre * gate_sig * up_pre).astype(jnp.bfloat16)
        partial_out = jnp.einsum('rgf,gfd->grd', hidden.reshape(-1, N_DP, group_width).astype(jnp.float32), down.reshape(N_DP, group_width, D).astype(jnp.float32))
        partial_out = lax.optimization_barrier(partial_out.astype(jnp.bfloat16)).astype(jnp.float32)
        outputs.append(lax.optimization_barrier(jnp.sum(partial_out, axis=0)).astype(jnp.bfloat16))
        hidden_grad = jnp.dot(grad_in, down.T, preferred_element_type=jnp.float32)
        down_grad = down_grad + jnp.dot(hidden.T, grad_in, preferred_element_type=jnp.float32)
        gate_grad = hidden_grad * up_pre * gate_sig * (1.0 + gate_pre * (1.0 - gate_sig))
        up_grad = hidden_grad * gate_pre * gate_sig
        both_grad = jnp.stack([gate_grad, up_grad], axis=1).astype(jnp.bfloat16)
        partial_in = jnp.einsum('rcgf,dcgf->grd', both_grad.reshape(-1, 2, N_DP, group_width).astype(jnp.float32), gate_up.reshape(D, 2, N_DP, group_width).astype(jnp.float32))
        partial_in = lax.optimization_barrier(partial_in.astype(jnp.bfloat16)).astype(jnp.float32)
        input_grads.append(lax.optimization_barrier(jnp.sum(partial_in, axis=0)).astype(jnp.bfloat16))
    first = 0.9 * moment_one.astype(jnp.float32) + 0.1 * down_grad
    second = 0.999 * moment_two.astype(jnp.float32) + 0.001 * down_grad * down_grad
    update = first / (jnp.sqrt(second) + 1e-08)
    return (jnp.stack(outputs), jnp.stack(input_grads), update.astype(jnp.bfloat16), first.astype(jnp.bfloat16), second.astype(jnp.bfloat16))

def reference(tokens, cotangent, routes, gates, source, w_gate_up, w_down, moment_first, moment_second):
    pair_rows = TOK_MB * TOP
    target = source[routes]
    blocks = target.reshape(MB, EXPERTS, pair_rows)
    onehot = (blocks[..., None] == jnp.arange(EXPERTS, dtype=jnp.int32)).astype(jnp.int32)
    position = lax.optimization_barrier(jnp.sum((jnp.cumsum(onehot, axis=2) - onehot) * onehot, axis=-1)).astype(jnp.int32)
    source_idx = jnp.arange(EXPERTS, dtype=jnp.int32)[None, :, None]
    micro_idx = jnp.arange(MB, dtype=jnp.int32)[:, None, None]
    token_rep = jnp.repeat(tokens.reshape(MB, EXPERTS, TOK_MB, D), TOP, axis=2)
    gate_flat = gates.reshape(MB, EXPERTS, pair_rows)
    grad_rep = (jnp.repeat(cotangent.reshape(MB, EXPERTS, TOK_MB, D).astype(jnp.float32), TOP, axis=2) * gate_flat[..., None]).astype(jnp.bfloat16)
    empty = jnp.zeros((MB, EXPERTS, EXPERTS, CAP, D), jnp.bfloat16)
    token_buf = empty.at[micro_idx, blocks, source_idx, position].set(token_rep)
    grad_buf = empty.at[micro_idx, blocks, source_idx, position].set(grad_rep)
    token_buf = jnp.transpose(token_buf.reshape(MB, EXPERTS, EXPERTS * CAP, D), (1, 0, 2, 3))
    grad_buf = jnp.transpose(grad_buf.reshape(MB, EXPERTS, EXPERTS * CAP, D), (1, 0, 2, 3))
    expert_out, rows_grad, update_dir, new_first, new_second = lax.map(expert_pass, (token_buf, grad_buf, w_gate_up[source], w_down[source], moment_first[source], moment_second[source]))
    expert_out = expert_out.reshape(EXPERTS, MB, EXPERTS, CAP, D)
    rows_grad = rows_grad.reshape(EXPERTS, MB, EXPERTS, CAP, D)
    picked_out = expert_out[blocks, micro_idx, source_idx, position].astype(jnp.float32)
    picked_grad = rows_grad[blocks, micro_idx, source_idx, position].astype(jnp.float32)
    picked_out = picked_out.reshape(MB, EXPERTS, TOK_MB, TOP, D) * gates.reshape(MB, EXPERTS, TOK_MB, TOP)[..., None]
    layer_out = lax.optimization_barrier(jnp.sum(picked_out, axis=3)).astype(jnp.bfloat16).reshape(MB, TOKENS, D)
    token_grad = lax.optimization_barrier(jnp.sum(picked_grad.reshape(MB, EXPERTS, TOK_MB, TOP, D), axis=3)).astype(jnp.bfloat16).reshape(MB, TOKENS, D)
    return (layer_out, token_grad, update_dir, new_first, new_second)
```

```python
import jax
import jax.numpy as jnp
from jax import lax
from jax.experimental import pallas as pl
from jax.experimental.pallas import tpu as pltpu
from jax.sharding import PartitionSpec as P

contract_first = (((0,), (0,)), ((), ()))
contract_second = (((1,), (1,)), ((), ()))


def exchange(blocks):
    return lax.all_to_all(blocks, "expert", split_axis=0, concat_axis=0, tiled=True)


def copy_block(order_ref, block_ref, out_ref):
    out_ref[...] = block_ref[...]


def reorder(blocks, order):
    count, rows, width = blocks.shape
    return pl.pallas_call(
        copy_block,
        out_shape=jax.ShapeDtypeStruct(blocks.shape, blocks.dtype),
        grid_spec=pltpu.PrefetchScalarGridSpec(
            num_scalar_prefetch=1,
            grid=(count,),
            in_specs=[pl.BlockSpec((1, rows, width), lambda s, order_ref: (order_ref[s], 0, 0))],
            out_specs=pl.BlockSpec((1, rows, width), lambda s, order_ref: (s, 0, 0)),
        ),
        name="reorder",
    )(order, blocks)


def gather_features(rows):
    parts = lax.axis_size("dp")
    if parts == 2:
        other = lax.ppermute(rows, "dp", ((0, 1), (1, 0)))
        first = lax.axis_index("dp") == 0
        return [jnp.where(first, rows, other), jnp.where(first, other, rows)]
    whole = lax.all_gather(rows, "dp", axis=0, tiled=False)
    return [whole[part] for part in range(parts)]


def scatter_sum(partial):
    parts = lax.axis_size("dp")
    if parts == 2:
        half = partial.shape[1] // 2
        low, high = partial[:, :half], partial[:, half:]
        first = lax.axis_index("dp") == 0
        keep, send = jnp.where(first, low, high), jnp.where(first, high, low)
        other = lax.ppermute(send, "dp", ((0, 1), (1, 0)))
        return (keep.astype(jnp.float32) + other.astype(jnp.float32)).astype(jnp.bfloat16)
    return lax.psum_scatter(partial, "dp", scatter_dimension=1, tiled=True)


def relocate(array, source, experts):
    blocks = array.reshape(experts, array.shape[1] // experts, array.shape[2])
    return exchange(reorder(exchange(blocks), source)).reshape(array.shape[1:])


def per_device(
    tokens, cotangent, routes, gates, source, w_gate_up, w_down, moment_first, moment_second
):
    experts = lax.axis_size("expert")
    micro_count, token_count, part_width = tokens.shape
    model_width = w_gate_up.shape[1]
    hidden_part = w_gate_up.shape[3]
    top_count = routes.shape[2]
    capacity = max(2, 3 * token_count * top_count // (2 * experts))
    per_expert = micro_count * capacity
    slots = experts * per_expert
    all_tokens = micro_count * token_count

    pairs = token_count * top_count
    chosen = routes.reshape(micro_count, pairs)
    same = chosen[:, :, None] == chosen[:, None, :]
    order = jnp.arange(pairs, dtype=jnp.int32)
    earlier = order[None, :] < order[:, None]
    position = jnp.sum((same & earlier).astype(jnp.int32), axis=2)
    micro_ids = jnp.arange(micro_count, dtype=jnp.int32)[:, None]
    place = (chosen * per_expert + micro_ids * capacity + position).reshape(all_tokens, top_count)
    slot_ids = jnp.arange(slots, dtype=jnp.int32)
    flat_gates = gates.reshape(all_tokens, top_count)
    matches = [place[:, k][:, None] == slot_ids for k in range(top_count)]
    picks = [match.astype(jnp.bfloat16) for match in matches]
    plain = sum(picks[1:], picks[0])
    slot_gate = sum(
        jnp.sum(jnp.where(matches[k], flat_gates[:, k : k + 1], 0.0), axis=0)
        for k in range(top_count)
    )

    row_tokens = lax.dot_general(
        plain,
        tokens.reshape(all_tokens, part_width),
        contract_first,
        preferred_element_type=jnp.float32,
    ).astype(jnp.bfloat16)
    row_grads = (
        lax.dot_general(
            plain,
            cotangent.reshape(all_tokens, part_width),
            contract_first,
            preferred_element_type=jnp.float32,
        )
        * slot_gate[:, None]
    ).astype(jnp.bfloat16)
    grad_blocks = row_grads.reshape(experts, per_expert, part_width)
    here_tokens = exchange(row_tokens.reshape(experts, per_expert, part_width))
    here_grads = exchange(grad_blocks)
    token_parts = gather_features(here_tokens.reshape(slots, part_width))
    grad_parts = gather_features(here_grads.reshape(slots, part_width))

    gate_up = w_gate_up.reshape(model_width, 2 * hidden_part)
    down = w_down.reshape(hidden_part, model_width)

    expert_in = jnp.concatenate(token_parts, axis=1)
    grad_in = jnp.concatenate(grad_parts, axis=1)
    both = jnp.dot(expert_in, gate_up, preferred_element_type=jnp.float32).reshape(
        slots, 2, hidden_part
    )
    gate_pre = both[:, 0]
    up_pre = both[:, 1]
    gate_sig = jax.nn.sigmoid(gate_pre)
    hidden = (gate_pre * gate_sig * up_pre).astype(jnp.bfloat16)
    partial_out = jnp.dot(hidden, down, preferred_element_type=jnp.float32).astype(jnp.bfloat16)
    summed_out = scatter_sum(partial_out)
    back = exchange(
        jnp.concatenate([summed_out, hidden], axis=1).reshape(experts, per_expert, -1)
    )
    back_out = back[:, :, :part_width].reshape(slots, part_width)
    back_hidden = back[:, :, part_width:]
    layer_out = sum(
        flat_gates[:, k : k + 1] * jnp.dot(picks[k], back_out, preferred_element_type=jnp.float32)
        for k in range(top_count)
    )

    there = exchange(reorder(jnp.concatenate([back_hidden, grad_blocks], axis=2), source))
    there = there.reshape(slots, hidden_part + part_width)
    there_hidden = there[:, :hidden_part]
    there_grads = jnp.concatenate(gather_features(there[:, hidden_part:]), axis=1)

    hidden_grad = lax.dot_general(
        grad_in, down, contract_second, preferred_element_type=jnp.float32
    )
    gate_grad = hidden_grad * up_pre * gate_sig * (1.0 + gate_pre * (1.0 - gate_sig))
    up_grad = hidden_grad * gate_pre * gate_sig
    both_grad = (
        jnp.stack([gate_grad, up_grad], axis=1)
        .astype(jnp.bfloat16)
        .reshape(slots, 2 * hidden_part)
    )
    partial_in = lax.dot_general(
        both_grad, gate_up, contract_second, preferred_element_type=jnp.float32
    ).astype(jnp.bfloat16)
    summed_in = scatter_sum(partial_in)
    back_in = exchange(summed_in.reshape(experts, per_expert, part_width))
    token_grad = jnp.dot(
        plain, back_in.reshape(slots, part_width), preferred_element_type=jnp.float32
    )

    old_first = relocate(moment_first, source, experts)
    old_second = relocate(moment_second, source, experts)
    down_grad = lax.dot_general(
        there_hidden, there_grads, contract_first, preferred_element_type=jnp.float32
    )
    first = 0.9 * old_first.astype(jnp.float32) + 0.1 * down_grad
    second = 0.999 * old_second.astype(jnp.float32) + 0.001 * down_grad * down_grad
    update = first / (jnp.sqrt(second) + 1e-08)
    shape = moment_first.shape
    return (
        layer_out.astype(jnp.bfloat16).reshape(tokens.shape),
        token_grad.astype(jnp.bfloat16).reshape(tokens.shape),
        update.astype(jnp.bfloat16).reshape(shape),
        first.astype(jnp.bfloat16).reshape(shape),
        second.astype(jnp.bfloat16).reshape(shape),
    )


def solution(mesh):
    placed = (
        P(None, "expert", "dp"),
        P(None, "expert", "dp"),
        P(None, "expert", None),
        P(None, "expert", None),
        P(),
        P("expert", None, None, "dp"),
        P("expert", "dp", None),
        P("expert", "dp", None),
        P("expert", "dp", None),
    )
    return jax.shard_map(
        per_device,
        mesh=mesh,
        in_specs=placed,
        out_specs=(
            P(None, "expert", "dp"),
            P(None, "expert", "dp"),
            P("expert", "dp", None),
            P("expert", "dp", None),
            P("expert", "dp", None),
        ),
        check_vma=False,
    )
```

```python
import functools

import jax
import jax.numpy as jnp
from jax import lax
from jax.experimental import pallas as pl
from jax.experimental.pallas import tpu as pltpu
from jax.sharding import PartitionSpec as P

contract_first = (((0,), (0,)), ((), ()))
contract_second = (((1,), (1,)), ((), ()))


def exchange(blocks):
    return lax.all_to_all(blocks, "expert", split_axis=0, concat_axis=0, tiled=True)


def copy_block(order_ref, block_ref, out_ref):
    out_ref[...] = block_ref[...]


def reorder(blocks, order):
    count, rows, width = blocks.shape
    return pl.pallas_call(
        copy_block,
        out_shape=jax.ShapeDtypeStruct(blocks.shape, blocks.dtype),
        grid_spec=pltpu.PrefetchScalarGridSpec(
            num_scalar_prefetch=1,
            grid=(count,),
            in_specs=[pl.BlockSpec((1, rows, width), lambda s, order_ref: (order_ref[s], 0, 0))],
            out_specs=pl.BlockSpec((1, rows, width), lambda s, order_ref: (s, 0, 0)),
        ),
        name="reorder",
    )(order, blocks)


def gather_features(rows):
    parts = lax.axis_size("dp")
    if parts == 2:
        other = lax.ppermute(rows, "dp", ((0, 1), (1, 0)))
        first = lax.axis_index("dp") == 0
        return [jnp.where(first, rows, other), jnp.where(first, other, rows)]
    whole = lax.all_gather(rows, "dp", axis=0, tiled=False)
    return [whole[part] for part in range(parts)]


def scatter_sum(partial):
    parts = lax.axis_size("dp")
    if parts == 2:
        half = partial.shape[1] // 2
        low, high = partial[:, :half], partial[:, half:]
        first = lax.axis_index("dp") == 0
        keep, send = jnp.where(first, low, high), jnp.where(first, high, low)
        other = lax.ppermute(send, "dp", ((0, 1), (1, 0)))
        return (keep.astype(jnp.float32) + other.astype(jnp.float32)).astype(jnp.bfloat16)
    return lax.psum_scatter(partial, "dp", scatter_dimension=1, tiled=True)


def relocate_spread(arrays, source, experts):
    outputs = []
    for array in arrays:
        blocks = array.reshape(experts, array.shape[1] // experts, array.shape[2])
        outputs.append(exchange(reorder(exchange(blocks), source)).reshape(array.shape[1:]))
    return outputs


PLANES = 4
GROUP = 4
KINDS = (((0, 1), (1, 2), (2, 3)), ((0, 2), (2, 3)), ((0, 1), (1, 3)), ((0, 3),))
KIND_ROW, UP_ROW, DOWN_ROW, FINAL_ROW = 0, 4, 8, 12


def plan_kernel(where_ref, source_ref, plan_ref, ends_ref):
    plane = where_ref[0]
    member = where_ref[1]
    for index in range(PLANES):
        plan_ref[KIND_ROW + index] = 0
        plan_ref[UP_ROW + index] = GROUP
        plan_ref[DOWN_ROW + index] = GROUP
        ends_ref[index] = 0
    for slot in range(PLANES * GROUP):
        low = slot // GROUP
        other = source_ref[slot]
        high = other // GROUP
        offset = (slot % GROUP) ^ member

        @pl.when(jnp.logical_and(high == low, plane == low))
        def _():
            plan_ref[FINAL_ROW + offset] = (other % GROUP) ^ member

        @pl.when(high > low)
        def _():
            turn = jnp.int32(PLANES - 1)
            for index in reversed(range(PLANES - 1)):
                turn = jnp.where(ends_ref[index] <= low, index, turn)
            ends_ref[turn] = high
            span = high - low
            kind = jnp.where(span == 3, 4, jnp.where(span == 2, 2 + low, 1))
            plan_ref[KIND_ROW + turn] = jnp.maximum(plan_ref[KIND_ROW + turn], kind)

            @pl.when(plane == low)
            def _():
                plan_ref[UP_ROW + turn] = offset
                plan_ref[FINAL_ROW + offset] = GROUP + 2 * turn + 1

            @pl.when(plane == high)
            def _():
                there = (other % GROUP) ^ member
                plan_ref[DOWN_ROW + turn] = there
                plan_ref[FINAL_ROW + there] = GROUP + 2 * turn


def make_plan(source, plane, member):
    smem = pl.BlockSpec(memory_space=pltpu.SMEM)
    return pl.pallas_call(
        plan_kernel,
        out_shape=jax.ShapeDtypeStruct((16,), jnp.int32),
        in_specs=[smem, smem],
        out_specs=smem,
        scratch_shapes=[pltpu.SMEM((PLANES,), jnp.int32)],
        name="plan",
    )(jnp.stack([plane, member]), source)


def cut_kernel(member_ref, *refs):
    arrays, outs, sems = refs[:2], refs[2 : 2 + GROUP], refs[-1]
    rows = outs[0].shape[1]
    copies = []
    for offset in range(GROUP):
        begin = pl.multiple_of((member_ref[0] ^ offset) * rows, rows)
        for which in range(2):
            copies.append(
                pltpu.make_async_copy(
                    arrays[which].at[pl.ds(begin, rows)],
                    outs[offset].at[which],
                    sems.at[offset, which],
                )
            )
    for copy in copies:
        copy.start()
    for copy in copies:
        copy.wait()


def cut(first, second, member):
    rows, width = first.shape
    anywhere = pl.BlockSpec(memory_space=pl.ANY)
    piece = jax.ShapeDtypeStruct((2, rows // GROUP, width), first.dtype)
    return pl.pallas_call(
        cut_kernel,
        out_shape=[piece] * GROUP,
        in_specs=[pl.BlockSpec(memory_space=pltpu.SMEM), anywhere, anywhere],
        out_specs=[anywhere] * GROUP,
        scratch_shapes=[pltpu.SemaphoreType.DMA((GROUP, 2))],
        name="cut",
    )(member[None], first, second)


def choose_kernel(count, choice_ref, *refs):
    options, outs, sems = refs[:count], refs[count:-1], refs[-1]
    for place, out in enumerate(outs):
        for index, option in enumerate(options):

            @pl.when(choice_ref[place] == index)
            def _():
                pltpu.make_async_copy(option, out, sems.at[place]).start()

    for place, out in enumerate(outs):

        @pl.when(choice_ref[place] < count)
        def _():
            pltpu.make_async_copy(options[0], out, sems.at[place]).wait()


def choose(choice, options):
    anywhere = pl.BlockSpec(memory_space=pl.ANY)
    piece = jax.ShapeDtypeStruct(options[0].shape, options[0].dtype)
    return pl.pallas_call(
        functools.partial(choose_kernel, len(options)),
        out_shape=[piece] * choice.shape[0],
        in_specs=[pl.BlockSpec(memory_space=pltpu.SMEM)] + [anywhere] * len(options),
        out_specs=[anywhere] * choice.shape[0],
        scratch_shapes=[pltpu.SemaphoreType.DMA((choice.shape[0],))],
        name="choose",
    )(choice, *options)


def within_plane(offset):
    return [(index, index ^ offset) for index in range(PLANES * GROUP)]


def between_planes(moves):
    return [(GROUP * a + index, GROUP * b + index) for a, b in moves for index in range(GROUP)]


def swap_round(moves):
    def run(up, down):
        return (
            lax.ppermute(up, "expert", between_planes(moves)),
            lax.ppermute(down, "expert", between_planes([(b, a) for a, b in moves])),
        )

    return run


def relocate_swaps(first, second, source):
    index = lax.axis_index("expert")
    plane, member = index // GROUP, index % GROUP
    plan = make_plan(source, plane, member)
    pieces = cut(first, second, member)
    held = [pieces[0]] + [
        lax.ppermute(pieces[offset], "expert", within_plane(offset)) for offset in range(1, GROUP)
    ]
    ways = choose(plan[UP_ROW:FINAL_ROW], held)
    arrived = []
    for turn in range(PLANES):
        arrived += lax.switch(
            plan[KIND_ROW + turn],
            [lambda up, down: (up, down)] + [swap_round(moves) for moves in KINDS],
            ways[turn],
            ways[PLANES + turn],
        )
    ready = choose(plan[FINAL_ROW:], held + arrived)
    own = [ready[0]] + [
        lax.ppermute(ready[offset], "expert", within_plane(offset)) for offset in range(1, GROUP)
    ]
    for bit in (1, 2):
        swap = (member & bit) != 0
        own = [jnp.where(swap, own[offset ^ bit], own[offset]) for offset in range(GROUP)]
    return [jnp.concatenate([piece[which] for piece in own], axis=0) for which in range(2)]


def per_device(
    tokens, cotangent, routes, gates, source, w_gate_up, w_down, moment_first, moment_second
):
    experts = lax.axis_size("expert")
    micro_count, token_count, part_width = tokens.shape
    model_width = w_gate_up.shape[1]
    hidden_part = w_gate_up.shape[3]
    top_count = routes.shape[2]
    capacity = max(2, 3 * token_count * top_count // (2 * experts))
    per_expert = micro_count * capacity
    slots = experts * per_expert
    all_tokens = micro_count * token_count

    pairs = token_count * top_count
    chosen = routes.reshape(micro_count, pairs)
    same = chosen[:, :, None] == chosen[:, None, :]
    order = jnp.arange(pairs, dtype=jnp.int32)
    earlier = order[None, :] < order[:, None]
    position = jnp.sum((same & earlier).astype(jnp.int32), axis=2)
    micro_ids = jnp.arange(micro_count, dtype=jnp.int32)[:, None]
    place = (chosen * per_expert + micro_ids * capacity + position).reshape(all_tokens, top_count)
    slot_ids = jnp.arange(slots, dtype=jnp.int32)
    flat_gates = gates.reshape(all_tokens, top_count)
    matches = [place[:, k][:, None] == slot_ids for k in range(top_count)]
    picks = [match.astype(jnp.bfloat16) for match in matches]
    plain = sum(picks[1:], picks[0])
    slot_gate = sum(
        jnp.sum(jnp.where(matches[k], flat_gates[:, k : k + 1], 0.0), axis=0)
        for k in range(top_count)
    )

    row_tokens = lax.dot_general(
        plain,
        tokens.reshape(all_tokens, part_width),
        contract_first,
        preferred_element_type=jnp.float32,
    ).astype(jnp.bfloat16)
    row_grads = (
        lax.dot_general(
            plain,
            cotangent.reshape(all_tokens, part_width),
            contract_first,
            preferred_element_type=jnp.float32,
        )
        * slot_gate[:, None]
    ).astype(jnp.bfloat16)
    grad_blocks = row_grads.reshape(experts, per_expert, part_width)
    here_tokens = exchange(row_tokens.reshape(experts, per_expert, part_width))
    here_grads = exchange(grad_blocks)
    token_parts = gather_features(here_tokens.reshape(slots, part_width))
    grad_parts = gather_features(here_grads.reshape(slots, part_width))

    gate_up = w_gate_up.reshape(model_width, 2 * hidden_part)
    down = w_down.reshape(hidden_part, model_width)

    expert_in = jnp.concatenate(token_parts, axis=1)
    grad_in = jnp.concatenate(grad_parts, axis=1)
    both = jnp.dot(expert_in, gate_up, preferred_element_type=jnp.float32).reshape(
        slots, 2, hidden_part
    )
    gate_pre = both[:, 0]
    up_pre = both[:, 1]
    gate_sig = jax.nn.sigmoid(gate_pre)
    hidden = (gate_pre * gate_sig * up_pre).astype(jnp.bfloat16)
    partial_out = jnp.dot(hidden, down, preferred_element_type=jnp.float32).astype(jnp.bfloat16)
    summed_out = scatter_sum(partial_out)
    back = exchange(
        jnp.concatenate([summed_out, hidden], axis=1).reshape(experts, per_expert, -1)
    )
    back_out = back[:, :, :part_width].reshape(slots, part_width)
    back_hidden = back[:, :, part_width:]
    layer_out = sum(
        flat_gates[:, k : k + 1] * jnp.dot(picks[k], back_out, preferred_element_type=jnp.float32)
        for k in range(top_count)
    )

    there = exchange(reorder(jnp.concatenate([back_hidden, grad_blocks], axis=2), source))
    there = there.reshape(slots, hidden_part + part_width)
    there_hidden = there[:, :hidden_part]
    there_grads = jnp.concatenate(gather_features(there[:, hidden_part:]), axis=1)

    hidden_grad = lax.dot_general(
        grad_in, down, contract_second, preferred_element_type=jnp.float32
    )
    gate_grad = hidden_grad * up_pre * gate_sig * (1.0 + gate_pre * (1.0 - gate_sig))
    up_grad = hidden_grad * gate_pre * gate_sig
    both_grad = (
        jnp.stack([gate_grad, up_grad], axis=1)
        .astype(jnp.bfloat16)
        .reshape(slots, 2 * hidden_part)
    )
    partial_in = lax.dot_general(
        both_grad, gate_up, contract_second, preferred_element_type=jnp.float32
    ).astype(jnp.bfloat16)
    summed_in = scatter_sum(partial_in)
    back_in = exchange(summed_in.reshape(experts, per_expert, part_width))
    token_grad = jnp.dot(
        plain, back_in.reshape(slots, part_width), preferred_element_type=jnp.float32
    )

    if experts == PLANES * GROUP:
        old_first, old_second = relocate_swaps(moment_first[0], moment_second[0], source)
    else:
        old_first, old_second = relocate_spread((moment_first, moment_second), source, experts)
    down_grad = lax.dot_general(
        there_hidden, there_grads, contract_first, preferred_element_type=jnp.float32
    )
    first = 0.9 * old_first.astype(jnp.float32) + 0.1 * down_grad
    second = 0.999 * old_second.astype(jnp.float32) + 0.001 * down_grad * down_grad
    update = first / (jnp.sqrt(second) + 1e-08)
    shape = moment_first.shape
    return (
        layer_out.astype(jnp.bfloat16).reshape(tokens.shape),
        token_grad.astype(jnp.bfloat16).reshape(tokens.shape),
        update.astype(jnp.bfloat16).reshape(shape),
        first.astype(jnp.bfloat16).reshape(shape),
        second.astype(jnp.bfloat16).reshape(shape),
    )


def solution(mesh):
    placed = (
        P(None, "expert", "dp"),
        P(None, "expert", "dp"),
        P(None, "expert", None),
        P(None, "expert", None),
        P(),
        P("expert", None, None, "dp"),
        P("expert", "dp", None),
        P("expert", "dp", None),
        P("expert", "dp", None),
    )
    return jax.shard_map(
        per_device,
        mesh=mesh,
        in_specs=placed,
        out_specs=(
            P(None, "expert", "dp"),
            P(None, "expert", "dp"),
            P("expert", "dp", None),
            P("expert", "dp", None),
            P("expert", "dp", None),
        ),
        check_vma=False,
    )
```

```python
import functools

import jax
import jax.numpy as jnp
from jax import lax
from jax.experimental import pallas as pl
from jax.experimental.pallas import tpu as pltpu
from jax.sharding import PartitionSpec as P

contract_first = (((0,), (0,)), ((), ()))
contract_second = (((1,), (1,)), ((), ()))
VMEM_BYTES = 32 * 1024 * 1024


def exchange(blocks):
    return lax.all_to_all(blocks, "expert", split_axis=0, concat_axis=0, tiled=True)


def reorder_kernel(order_ref, blocks_ref, out_ref):
    for place in range(out_ref.shape[0]):
        out_ref[place] = blocks_ref[order_ref[place]]


def reorder(blocks, order):
    whole = pl.BlockSpec(memory_space=pltpu.VMEM)
    return pl.pallas_call(
        reorder_kernel,
        out_shape=jax.ShapeDtypeStruct(blocks.shape, blocks.dtype),
        in_specs=[pl.BlockSpec(memory_space=pltpu.SMEM), whole],
        out_specs=whole,
        compiler_params=pltpu.CompilerParams(vmem_limit_bytes=VMEM_BYTES),
        name="reorder",
    )(order, blocks)


def gather_features(rows):
    parts = lax.axis_size("dp")
    if parts == 2:
        other = lax.ppermute(rows, "dp", ((0, 1), (1, 0)))
        first = lax.axis_index("dp") == 0
        return [jnp.where(first, rows, other), jnp.where(first, other, rows)]
    whole = lax.all_gather(rows, "dp", axis=0, tiled=False)
    return [whole[part] for part in range(parts)]


def scatter_sum(partial):
    parts = lax.axis_size("dp")
    if parts == 2:
        half = partial.shape[1] // 2
        low, high = partial[:, :half], partial[:, half:]
        first = lax.axis_index("dp") == 0
        keep, send = jnp.where(first, low, high), jnp.where(first, high, low)
        other = lax.ppermute(send, "dp", ((0, 1), (1, 0)))
        return (keep.astype(jnp.float32) + other.astype(jnp.float32)).astype(jnp.bfloat16)
    return lax.psum_scatter(partial, "dp", scatter_dimension=1, tiled=True)


def relocate_spread(arrays, source, experts):
    outputs = []
    for array in arrays:
        blocks = array.reshape(experts, array.shape[1] // experts, array.shape[2])
        outputs.append(exchange(reorder(exchange(blocks), source)).reshape(array.shape[1:]))
    return outputs


PLANES = 4
GROUP = 4
KINDS = (((0, 1), (1, 2), (2, 3)), ((0, 2), (2, 3)), ((0, 1), (1, 3)), ((0, 3),))
KIND_ROW, UP_ROW, DOWN_ROW, FINAL_ROW = 0, 4, 8, 12


def plan_kernel(where_ref, source_ref, plan_ref, ends_ref):
    plane = where_ref[0]
    member = where_ref[1]
    for index in range(PLANES):
        plan_ref[KIND_ROW + index] = 0
        plan_ref[UP_ROW + index] = GROUP
        plan_ref[DOWN_ROW + index] = GROUP
        ends_ref[index] = 0
    for slot in range(PLANES * GROUP):
        low = slot // GROUP
        other = source_ref[slot]
        high = other // GROUP
        offset = (slot % GROUP) ^ member

        @pl.when(jnp.logical_and(high == low, plane == low))
        def _():
            plan_ref[FINAL_ROW + offset] = (other % GROUP) ^ member

        @pl.when(high > low)
        def _():
            turn = jnp.int32(PLANES - 1)
            for index in reversed(range(PLANES - 1)):
                turn = jnp.where(ends_ref[index] <= low, index, turn)
            ends_ref[turn] = high
            span = high - low
            kind = jnp.where(span == 3, 4, jnp.where(span == 2, 2 + low, 1))
            plan_ref[KIND_ROW + turn] = jnp.maximum(plan_ref[KIND_ROW + turn], kind)

            @pl.when(plane == low)
            def _():
                plan_ref[UP_ROW + turn] = offset
                plan_ref[FINAL_ROW + offset] = GROUP + 2 * turn + 1

            @pl.when(plane == high)
            def _():
                there = (other % GROUP) ^ member
                plan_ref[DOWN_ROW + turn] = there
                plan_ref[FINAL_ROW + there] = GROUP + 2 * turn


def make_plan(source, plane, member):
    smem = pl.BlockSpec(memory_space=pltpu.SMEM)
    return pl.pallas_call(
        plan_kernel,
        out_shape=jax.ShapeDtypeStruct((16,), jnp.int32),
        in_specs=[smem, smem],
        out_specs=smem,
        scratch_shapes=[pltpu.SMEM((PLANES,), jnp.int32)],
        name="plan",
    )(jnp.stack([plane, member]), source)


def cut_kernel(member_ref, first_ref, second_ref, *refs):
    outs, staged, in_sems, out_sems = refs[:GROUP], *refs[GROUP:]
    rows = outs[0].shape[1]
    loads, stores = [], []
    for offset in (1, 2, 3, 0):
        begin = pl.multiple_of((member_ref[0] ^ offset) * rows, rows)
        for which, array in enumerate((first_ref, second_ref)):
            loads.append(
                pltpu.make_async_copy(
                    array.at[pl.ds(begin, rows)],
                    staged.at[offset, which],
                    in_sems.at[offset, which],
                )
            )
            stores.append(
                pltpu.make_async_copy(
                    staged.at[offset, which],
                    outs[offset].at[which],
                    out_sems.at[offset, which],
                )
            )
    for load in loads:
        load.start()
    for load, store in zip(loads, stores):
        load.wait()
        store.start()
    for store in stores:
        store.wait()


def cut(first, second, member):
    rows, width = first.shape
    anywhere = pl.BlockSpec(memory_space=pl.ANY)
    piece = (2, rows // GROUP, width)
    return pl.pallas_call(
        cut_kernel,
        out_shape=[jax.ShapeDtypeStruct(piece, first.dtype)] * GROUP,
        in_specs=[pl.BlockSpec(memory_space=pltpu.SMEM), anywhere, anywhere],
        out_specs=[anywhere] * GROUP,
        scratch_shapes=[
            pltpu.VMEM((GROUP, *piece), first.dtype),
            pltpu.SemaphoreType.DMA((GROUP, 2)),
            pltpu.SemaphoreType.DMA((GROUP, 2)),
        ],
        compiler_params=pltpu.CompilerParams(vmem_limit_bytes=VMEM_BYTES),
        name="cut",
    )(member[None], first, second)


def choose_kernel(count, choice_ref, *refs):
    options, outs = refs[:count], refs[count:-3]
    staged, in_sems, out_sems = refs[-3:]
    for place in range(len(outs)):
        for index, option in enumerate(options):

            @pl.when(choice_ref[place] == index)
            def _():
                pltpu.make_async_copy(option, staged.at[place], in_sems.at[place]).start()

    for place, out in enumerate(outs):

        @pl.when(choice_ref[place] < count)
        def _():
            pltpu.make_async_copy(options[0], staged.at[place], in_sems.at[place]).wait()
            pltpu.make_async_copy(staged.at[place], out, out_sems.at[place]).start()

    for place, out in enumerate(outs):

        @pl.when(choice_ref[place] < count)
        def _():
            pltpu.make_async_copy(staged.at[place], out, out_sems.at[place]).wait()


def choose(choice, options):
    anywhere = pl.BlockSpec(memory_space=pl.ANY)
    shape, dtype = options[0].shape, options[0].dtype
    amount = choice.shape[0]
    return pl.pallas_call(
        functools.partial(choose_kernel, len(options)),
        out_shape=[jax.ShapeDtypeStruct(shape, dtype)] * amount,
        in_specs=[pl.BlockSpec(memory_space=pltpu.SMEM)] + [anywhere] * len(options),
        out_specs=[anywhere] * amount,
        scratch_shapes=[
            pltpu.VMEM((amount, *shape), dtype),
            pltpu.SemaphoreType.DMA((amount,)),
            pltpu.SemaphoreType.DMA((amount,)),
        ],
        compiler_params=pltpu.CompilerParams(vmem_limit_bytes=VMEM_BYTES),
        name="choose",
    )(choice, *options)


def within_plane(offset):
    return [(index, index ^ offset) for index in range(PLANES * GROUP)]


def between_planes(moves):
    return [(GROUP * a + index, GROUP * b + index) for a, b in moves for index in range(GROUP)]


def swap_round(moves):
    def run(up, down):
        return (
            lax.ppermute(up, "expert", between_planes(moves)),
            lax.ppermute(down, "expert", between_planes([(b, a) for a, b in moves])),
        )

    return run


def spread_quarters(first, second, source):
    index = lax.axis_index("expert")
    plane, member = index // GROUP, index % GROUP
    return make_plan(source, plane, member), cut(first, second, member)


def hand_out(pieces):
    return [pieces[0]] + [
        lax.ppermute(pieces[offset], "expert", within_plane(offset)) for offset in range(1, GROUP)
    ]


def swap_quarters(plan, held):
    ways = choose(plan[UP_ROW:FINAL_ROW], held)
    arrived = []
    for turn in range(PLANES):
        arrived += lax.switch(
            plan[KIND_ROW + turn],
            [lambda up, down: (up, down)] + [swap_round(moves) for moves in KINDS],
            ways[turn],
            ways[PLANES + turn],
        )
    return choose(plan[FINAL_ROW:], held + arrived)


def join_quarters(ready):
    member = lax.axis_index("expert") % GROUP
    own = hand_out(ready)
    for bit in (1, 2):
        swap = (member & bit) != 0
        own = [jnp.where(swap, own[offset ^ bit], own[offset]) for offset in range(GROUP)]
    return [jnp.concatenate([piece[which] for piece in own], axis=0) for which in range(2)]


def per_device(
    tokens, cotangent, routes, gates, source, w_gate_up, w_down, moment_first, moment_second
):
    experts = lax.axis_size("expert")
    micro_count, token_count, part_width = tokens.shape
    model_width = w_gate_up.shape[1]
    hidden_part = w_gate_up.shape[3]
    top_count = routes.shape[2]
    capacity = max(2, 3 * token_count * top_count // (2 * experts))
    per_expert = micro_count * capacity
    slots = experts * per_expert
    all_tokens = micro_count * token_count

    swaps = experts == PLANES * GROUP
    if swaps:
        plan, pieces = spread_quarters(moment_first[0], moment_second[0], source)
        pieces, tokens = lax.optimization_barrier((pieces, tokens))
        held = hand_out(pieces)

    pairs = token_count * top_count
    chosen = routes.reshape(micro_count, pairs)
    same = chosen[:, :, None] == chosen[:, None, :]
    order = jnp.arange(pairs, dtype=jnp.int32)
    earlier = order[None, :] < order[:, None]
    position = jnp.sum((same & earlier).astype(jnp.int32), axis=2)
    micro_ids = jnp.arange(micro_count, dtype=jnp.int32)[:, None]
    place = (chosen * per_expert + micro_ids * capacity + position).reshape(all_tokens, top_count)
    slot_ids = jnp.arange(slots, dtype=jnp.int32)
    flat_gates = gates.reshape(all_tokens, top_count)
    matches = [place[:, k][:, None] == slot_ids for k in range(top_count)]
    picks = [match.astype(jnp.bfloat16) for match in matches]
    plain = sum(picks[1:], picks[0])
    slot_gate = sum(
        jnp.sum(jnp.where(matches[k], flat_gates[:, k : k + 1], 0.0), axis=0)
        for k in range(top_count)
    )

    row_tokens = lax.dot_general(
        plain,
        tokens.reshape(all_tokens, part_width),
        contract_first,
        preferred_element_type=jnp.float32,
    ).astype(jnp.bfloat16)
    row_grads = (
        lax.dot_general(
            plain,
            cotangent.reshape(all_tokens, part_width),
            contract_first,
            preferred_element_type=jnp.float32,
        )
        * slot_gate[:, None]
    ).astype(jnp.bfloat16)
    grad_blocks = row_grads.reshape(experts, per_expert, part_width)
    here_tokens = exchange(row_tokens.reshape(experts, per_expert, part_width))
    here_grads = exchange(grad_blocks)
    if swaps:
        held, here_grads = lax.optimization_barrier((held, here_grads))
        ready = swap_quarters(plan, held)
    token_parts = gather_features(here_tokens.reshape(slots, part_width))
    grad_parts = gather_features(here_grads.reshape(slots, part_width))

    gate_up = w_gate_up.reshape(model_width, 2 * hidden_part)
    down = w_down.reshape(hidden_part, model_width)

    expert_in = jnp.concatenate(token_parts, axis=1)
    grad_in = jnp.concatenate(grad_parts, axis=1)
    both = jnp.dot(expert_in, gate_up, preferred_element_type=jnp.float32).reshape(
        slots, 2, hidden_part
    )
    gate_pre = both[:, 0]
    up_pre = both[:, 1]
    gate_sig = jax.nn.sigmoid(gate_pre)
    hidden = (gate_pre * gate_sig * up_pre).astype(jnp.bfloat16)
    partial_out = jnp.dot(hidden, down, preferred_element_type=jnp.float32).astype(jnp.bfloat16)
    summed_out = scatter_sum(partial_out)
    if swaps:
        ready, summed_out = lax.optimization_barrier((ready, summed_out))
    back = exchange(
        jnp.concatenate([summed_out, hidden], axis=1).reshape(experts, per_expert, -1)
    )
    back_out = back[:, :, :part_width].reshape(slots, part_width)
    back_hidden = back[:, :, part_width:]
    layer_out = sum(
        flat_gates[:, k : k + 1] * jnp.dot(picks[k], back_out, preferred_element_type=jnp.float32)
        for k in range(top_count)
    )

    there = exchange(reorder(jnp.concatenate([back_hidden, grad_blocks], axis=2), source))
    there = there.reshape(slots, hidden_part + part_width)
    there_hidden = there[:, :hidden_part]
    there_grads = jnp.concatenate(gather_features(there[:, hidden_part:]), axis=1)

    hidden_grad = lax.dot_general(
        grad_in, down, contract_second, preferred_element_type=jnp.float32
    )
    gate_grad = hidden_grad * up_pre * gate_sig * (1.0 + gate_pre * (1.0 - gate_sig))
    up_grad = hidden_grad * gate_pre * gate_sig
    both_grad = (
        jnp.stack([gate_grad, up_grad], axis=1)
        .astype(jnp.bfloat16)
        .reshape(slots, 2 * hidden_part)
    )
    partial_in = lax.dot_general(
        both_grad, gate_up, contract_second, preferred_element_type=jnp.float32
    ).astype(jnp.bfloat16)
    summed_in = scatter_sum(partial_in)
    back_in = exchange(summed_in.reshape(experts, per_expert, part_width))
    token_grad = jnp.dot(
        plain, back_in.reshape(slots, part_width), preferred_element_type=jnp.float32
    )

    if swaps:
        old_first, old_second = join_quarters(ready)
    else:
        old_first, old_second = relocate_spread((moment_first, moment_second), source, experts)
    down_grad = lax.dot_general(
        there_hidden, there_grads, contract_first, preferred_element_type=jnp.float32
    )
    first = 0.9 * old_first.astype(jnp.float32) + 0.1 * down_grad
    second = 0.999 * old_second.astype(jnp.float32) + 0.001 * down_grad * down_grad
    update = first / (jnp.sqrt(second) + 1e-08)
    shape = moment_first.shape
    return (
        layer_out.astype(jnp.bfloat16).reshape(tokens.shape),
        token_grad.astype(jnp.bfloat16).reshape(tokens.shape),
        update.astype(jnp.bfloat16).reshape(shape),
        first.astype(jnp.bfloat16).reshape(shape),
        second.astype(jnp.bfloat16).reshape(shape),
    )


def solution(mesh):
    placed = (
        P(None, "expert", "dp"),
        P(None, "expert", "dp"),
        P(None, "expert", None),
        P(None, "expert", None),
        P(),
        P("expert", None, None, "dp"),
        P("expert", "dp", None),
        P("expert", "dp", None),
        P("expert", "dp", None),
    )
    return jax.shard_map(
        per_device,
        mesh=mesh,
        in_specs=placed,
        out_specs=(
            P(None, "expert", "dp"),
            P(None, "expert", "dp"),
            P("expert", "dp", None),
            P("expert", "dp", None),
            P("expert", "dp", None),
        ),
        check_vma=False,
    )
```

```python
import functools

import jax
import jax.numpy as jnp
from jax import lax
from jax.experimental import pallas as pl
from jax.experimental.pallas import tpu as pltpu
from jax.sharding import PartitionSpec as P

contract_first = (((0,), (0,)), ((), ()))
contract_second = (((1,), (1,)), ((), ()))
VMEM_BYTES = 32 * 1024 * 1024


def exchange(blocks):
    return lax.all_to_all(blocks, "expert", split_axis=0, concat_axis=0, tiled=True)


def reorder_kernel(order_ref, blocks_ref, out_ref):
    for place in range(out_ref.shape[0]):
        out_ref[place] = blocks_ref[order_ref[place]]


def reorder(blocks, order):
    whole = pl.BlockSpec(memory_space=pltpu.VMEM)
    return pl.pallas_call(
        reorder_kernel,
        out_shape=jax.ShapeDtypeStruct(blocks.shape, blocks.dtype),
        in_specs=[pl.BlockSpec(memory_space=pltpu.SMEM), whole],
        out_specs=whole,
        compiler_params=pltpu.CompilerParams(vmem_limit_bytes=VMEM_BYTES),
        name="reorder",
    )(order, blocks)


def gather_features(rows):
    parts = lax.axis_size("dp")
    if parts == 2:
        other = lax.ppermute(rows, "dp", ((0, 1), (1, 0)))
        first = lax.axis_index("dp") == 0
        return [jnp.where(first, rows, other), jnp.where(first, other, rows)]
    whole = lax.all_gather(rows, "dp", axis=0, tiled=False)
    return [whole[part] for part in range(parts)]


def scatter_sum(partial):
    parts = lax.axis_size("dp")
    if parts == 2:
        half = partial.shape[1] // 2
        low, high = partial[:, :half], partial[:, half:]
        first = lax.axis_index("dp") == 0
        keep, send = jnp.where(first, low, high), jnp.where(first, high, low)
        other = lax.ppermute(send, "dp", ((0, 1), (1, 0)))
        return (keep.astype(jnp.float32) + other.astype(jnp.float32)).astype(jnp.bfloat16)
    return lax.psum_scatter(partial, "dp", scatter_dimension=1, tiled=True)


def relocate_spread(arrays, source, experts):
    outputs = []
    for array in arrays:
        blocks = array.reshape(experts, array.shape[1] // experts, array.shape[2])
        outputs.append(exchange(reorder(exchange(blocks), source)).reshape(array.shape[1:]))
    return outputs


PLANES = 4
GROUP = 4
KINDS = (((0, 1), (1, 2), (2, 3)), ((0, 2), (2, 3)), ((0, 1), (1, 3)), ((0, 3),))
KIND_ROW, UP_ROW, DOWN_ROW, FINAL_ROW = 0, 4, 8, 12


def plan_kernel(where_ref, source_ref, plan_ref, ends_ref):
    plane = where_ref[0]
    member = where_ref[1]
    for index in range(PLANES):
        plan_ref[KIND_ROW + index] = 0
        plan_ref[UP_ROW + index] = GROUP
        plan_ref[DOWN_ROW + index] = GROUP
        ends_ref[index] = 0
    for slot in range(PLANES * GROUP):
        low = slot // GROUP
        other = source_ref[slot]
        high = other // GROUP
        offset = (slot % GROUP) ^ member

        @pl.when(jnp.logical_and(high == low, plane == low))
        def _():
            plan_ref[FINAL_ROW + offset] = (other % GROUP) ^ member

        @pl.when(high > low)
        def _():
            turn = jnp.int32(PLANES - 1)
            for index in reversed(range(PLANES - 1)):
                turn = jnp.where(ends_ref[index] <= low, index, turn)
            ends_ref[turn] = high
            span = high - low
            kind = jnp.where(span == 3, 4, jnp.where(span == 2, 2 + low, 1))
            plan_ref[KIND_ROW + turn] = jnp.maximum(plan_ref[KIND_ROW + turn], kind)

            @pl.when(plane == low)
            def _():
                plan_ref[UP_ROW + turn] = offset
                plan_ref[FINAL_ROW + offset] = GROUP + 2 * turn + 1

            @pl.when(plane == high)
            def _():
                there = (other % GROUP) ^ member
                plan_ref[DOWN_ROW + turn] = there
                plan_ref[FINAL_ROW + there] = GROUP + 2 * turn


def make_plan(source, plane, member):
    smem = pl.BlockSpec(memory_space=pltpu.SMEM)
    return pl.pallas_call(
        plan_kernel,
        out_shape=jax.ShapeDtypeStruct((16,), jnp.int32),
        in_specs=[smem, smem],
        out_specs=smem,
        scratch_shapes=[pltpu.SMEM((PLANES,), jnp.int32)],
        name="plan",
    )(jnp.stack([plane, member]), source)


def cut_kernel(member_ref, first_ref, second_ref, *refs):
    outs, staged, in_sems, out_sems = refs[:GROUP], *refs[GROUP:]
    rows = outs[0].shape[1]
    loads, stores = [], []
    for offset in (1, 2, 3, 0):
        begin = pl.multiple_of((member_ref[0] ^ offset) * rows, rows)
        for which, array in enumerate((first_ref, second_ref)):
            loads.append(
                pltpu.make_async_copy(
                    array.at[pl.ds(begin, rows)],
                    staged.at[offset, which],
                    in_sems.at[offset, which],
                )
            )
            stores.append(
                pltpu.make_async_copy(
                    staged.at[offset, which],
                    outs[offset].at[which],
                    out_sems.at[offset, which],
                )
            )
    for load in loads:
        load.start()
    for load, store in zip(loads, stores):
        load.wait()
        store.start()
    for store in stores:
        store.wait()


def cut(first, second, member):
    rows, width = first.shape
    anywhere = pl.BlockSpec(memory_space=pl.ANY)
    piece = (2, rows // GROUP, width)
    return pl.pallas_call(
        cut_kernel,
        out_shape=[jax.ShapeDtypeStruct(piece, first.dtype)] * GROUP,
        in_specs=[pl.BlockSpec(memory_space=pltpu.SMEM), anywhere, anywhere],
        out_specs=[anywhere] * GROUP,
        scratch_shapes=[
            pltpu.VMEM((GROUP, *piece), first.dtype),
            pltpu.SemaphoreType.DMA((GROUP, 2)),
            pltpu.SemaphoreType.DMA((GROUP, 2)),
        ],
        compiler_params=pltpu.CompilerParams(vmem_limit_bytes=VMEM_BYTES),
        name="cut",
    )(member[None], first, second)


def choose_kernel(count, choice_ref, *refs):
    options, outs = refs[:count], refs[count:-3]
    staged, in_sems, out_sems = refs[-3:]
    for place in range(len(outs)):
        for index, option in enumerate(options):

            @pl.when(choice_ref[place] == index)
            def _():
                pltpu.make_async_copy(option, staged.at[place], in_sems.at[place]).start()

    for place, out in enumerate(outs):

        @pl.when(choice_ref[place] < count)
        def _():
            pltpu.make_async_copy(options[0], staged.at[place], in_sems.at[place]).wait()
            pltpu.make_async_copy(staged.at[place], out, out_sems.at[place]).start()

    for place, out in enumerate(outs):

        @pl.when(choice_ref[place] < count)
        def _():
            pltpu.make_async_copy(staged.at[place], out, out_sems.at[place]).wait()


def choose(choice, options):
    anywhere = pl.BlockSpec(memory_space=pl.ANY)
    shape, dtype = options[0].shape, options[0].dtype
    amount = choice.shape[0]
    return pl.pallas_call(
        functools.partial(choose_kernel, len(options)),
        out_shape=[jax.ShapeDtypeStruct(shape, dtype)] * amount,
        in_specs=[pl.BlockSpec(memory_space=pltpu.SMEM)] + [anywhere] * len(options),
        out_specs=[anywhere] * amount,
        scratch_shapes=[
            pltpu.VMEM((amount, *shape), dtype),
            pltpu.SemaphoreType.DMA((amount,)),
            pltpu.SemaphoreType.DMA((amount,)),
        ],
        compiler_params=pltpu.CompilerParams(vmem_limit_bytes=VMEM_BYTES),
        name="choose",
    )(choice, *options)


def within_plane(offset):
    return [(index, index ^ offset) for index in range(PLANES * GROUP)]


def between_planes(moves):
    return [(GROUP * a + index, GROUP * b + index) for a, b in moves for index in range(GROUP)]


def swap_round(moves):
    def run(up, down):
        return (
            lax.ppermute(up, "expert", between_planes(moves)),
            lax.ppermute(down, "expert", between_planes([(b, a) for a, b in moves])),
        )

    return run


def spread_quarters(first, second, source):
    index = lax.axis_index("expert")
    plane, member = index // GROUP, index % GROUP
    return make_plan(source, plane, member), cut(first, second, member)


def hand_out(pieces):
    return [pieces[0]] + [
        lax.ppermute(pieces[offset], "expert", within_plane(offset)) for offset in range(1, GROUP)
    ]


def swap_quarters(plan, held):
    ways = choose(plan[UP_ROW:FINAL_ROW], held)
    arrived = []
    for turn in range(PLANES):
        arrived += lax.switch(
            plan[KIND_ROW + turn],
            [lambda up, down: (up, down)] + [swap_round(moves) for moves in KINDS],
            ways[turn],
            ways[PLANES + turn],
        )
    return choose(plan[FINAL_ROW:], held + arrived)


def join_quarters(ready):
    member = lax.axis_index("expert") % GROUP
    own = hand_out(ready)
    for bit in (1, 2):
        swap = (member & bit) != 0
        own = [jnp.where(swap, own[offset ^ bit], own[offset]) for offset in range(GROUP)]
    return [jnp.concatenate([piece[which] for piece in own], axis=0) for which in range(2)]


def per_device(
    tokens, cotangent, routes, gates, source, w_gate_up, w_down, moment_first, moment_second
):
    experts = lax.axis_size("expert")
    micro_count, token_count, part_width = tokens.shape
    model_width = w_gate_up.shape[1]
    hidden_part = w_gate_up.shape[3]
    top_count = routes.shape[2]
    capacity = max(2, 3 * token_count * top_count // (2 * experts))
    per_expert = micro_count * capacity
    slots = experts * per_expert
    all_tokens = micro_count * token_count

    swaps = experts == PLANES * GROUP
    if swaps:
        plan, pieces = spread_quarters(moment_first[0], moment_second[0], source)
        pieces, tokens = lax.optimization_barrier((pieces, tokens))
        held = hand_out(pieces)

    pairs = token_count * top_count
    chosen = routes.reshape(micro_count, pairs)
    same = chosen[:, :, None] == chosen[:, None, :]
    order = jnp.arange(pairs, dtype=jnp.int32)
    earlier = order[None, :] < order[:, None]
    position = jnp.sum((same & earlier).astype(jnp.int32), axis=2)
    micro_ids = jnp.arange(micro_count, dtype=jnp.int32)[:, None]
    place = (chosen * per_expert + micro_ids * capacity + position).reshape(all_tokens, top_count)
    slot_ids = jnp.arange(slots, dtype=jnp.int32)
    flat_gates = gates.reshape(all_tokens, top_count)
    matches = [place[:, k][:, None] == slot_ids for k in range(top_count)]
    picks = [match.astype(jnp.bfloat16) for match in matches]
    plain = sum(picks[1:], picks[0])
    slot_gate = sum(
        jnp.sum(jnp.where(matches[k], flat_gates[:, k : k + 1], 0.0), axis=0)
        for k in range(top_count)
    )

    row_tokens = lax.dot_general(
        plain,
        tokens.reshape(all_tokens, part_width),
        contract_first,
        preferred_element_type=jnp.float32,
    ).astype(jnp.bfloat16)
    row_grads = (
        lax.dot_general(
            plain,
            cotangent.reshape(all_tokens, part_width),
            contract_first,
            preferred_element_type=jnp.float32,
        )
        * slot_gate[:, None]
    ).astype(jnp.bfloat16)
    grad_blocks = row_grads.reshape(experts, per_expert, part_width)
    here_tokens = exchange(row_tokens.reshape(experts, per_expert, part_width))
    here_grads = exchange(grad_blocks)
    token_parts = gather_features(here_tokens.reshape(slots, part_width))
    grad_parts = gather_features(here_grads.reshape(slots, part_width))

    gate_up = w_gate_up.reshape(model_width, 2 * hidden_part)
    down = w_down.reshape(hidden_part, model_width)

    expert_in = jnp.concatenate(token_parts, axis=1)
    grad_in = jnp.concatenate(grad_parts, axis=1)
    both = jnp.dot(expert_in, gate_up, preferred_element_type=jnp.float32).reshape(
        slots, 2, hidden_part
    )
    gate_pre = both[:, 0]
    up_pre = both[:, 1]
    gate_sig = jax.nn.sigmoid(gate_pre)
    hidden = (gate_pre * gate_sig * up_pre).astype(jnp.bfloat16)
    partial_out = jnp.dot(hidden, down, preferred_element_type=jnp.float32).astype(jnp.bfloat16)
    summed_out = scatter_sum(partial_out)
    back = exchange(
        jnp.concatenate([summed_out, hidden], axis=1).reshape(experts, per_expert, -1)
    )
    back_out = back[:, :, :part_width].reshape(slots, part_width)
    back_hidden = back[:, :, part_width:]
    layer_out = sum(
        flat_gates[:, k : k + 1] * jnp.dot(picks[k], back_out, preferred_element_type=jnp.float32)
        for k in range(top_count)
    )

    hidden_grad = lax.dot_general(
        grad_in, down, contract_second, preferred_element_type=jnp.float32
    )
    gate_grad = hidden_grad * up_pre * gate_sig * (1.0 + gate_pre * (1.0 - gate_sig))
    up_grad = hidden_grad * gate_pre * gate_sig
    both_grad = (
        jnp.stack([gate_grad, up_grad], axis=1)
        .astype(jnp.bfloat16)
        .reshape(slots, 2 * hidden_part)
    )
    partial_in = lax.dot_general(
        both_grad, gate_up, contract_second, preferred_element_type=jnp.float32
    ).astype(jnp.bfloat16)

    if swaps:
        held, back_hidden, partial_in = lax.optimization_barrier((held, back_hidden, partial_in))
        ready = swap_quarters(plan, held)
        ready, back_hidden = lax.optimization_barrier((ready, back_hidden))
    there = exchange(reorder(jnp.concatenate([back_hidden, grad_blocks], axis=2), source))
    there = there.reshape(slots, hidden_part + part_width)
    there_hidden = there[:, :hidden_part]
    there_grads = jnp.concatenate(gather_features(there[:, hidden_part:]), axis=1)

    summed_in = scatter_sum(partial_in)
    if swaps:
        there, summed_in = lax.optimization_barrier((there, summed_in))
    back_in = exchange(summed_in.reshape(experts, per_expert, part_width))
    token_grad = jnp.dot(
        plain, back_in.reshape(slots, part_width), preferred_element_type=jnp.float32
    )

    if swaps:
        old_first, old_second = join_quarters(ready)
    else:
        old_first, old_second = relocate_spread((moment_first, moment_second), source, experts)
    down_grad = lax.dot_general(
        there_hidden, there_grads, contract_first, preferred_element_type=jnp.float32
    )
    first = 0.9 * old_first.astype(jnp.float32) + 0.1 * down_grad
    second = 0.999 * old_second.astype(jnp.float32) + 0.001 * down_grad * down_grad
    update = first / (jnp.sqrt(second) + 1e-08)
    shape = moment_first.shape
    return (
        layer_out.astype(jnp.bfloat16).reshape(tokens.shape),
        token_grad.astype(jnp.bfloat16).reshape(tokens.shape),
        update.astype(jnp.bfloat16).reshape(shape),
        first.astype(jnp.bfloat16).reshape(shape),
        second.astype(jnp.bfloat16).reshape(shape),
    )


def solution(mesh):
    placed = (
        P(None, "expert", "dp"),
        P(None, "expert", "dp"),
        P(None, "expert", None),
        P(None, "expert", None),
        P(),
        P("expert", None, None, "dp"),
        P("expert", "dp", None),
        P("expert", "dp", None),
        P("expert", "dp", None),
    )
    return jax.shard_map(
        per_device,
        mesh=mesh,
        in_specs=placed,
        out_specs=(
            P(None, "expert", "dp"),
            P(None, "expert", "dp"),
            P("expert", "dp", None),
            P("expert", "dp", None),
            P("expert", "dp", None),
        ),
        check_vma=False,
    )
```

```python
import functools

import jax
import jax.numpy as jnp
from jax import lax
from jax.experimental import pallas as pl
from jax.experimental.pallas import tpu as pltpu
from jax.sharding import PartitionSpec as P

contract_first = (((0,), (0,)), ((), ()))
contract_second = (((1,), (1,)), ((), ()))
VMEM_BYTES = 32 * 1024 * 1024


def exchange(blocks):
    return lax.all_to_all(blocks, "expert", split_axis=0, concat_axis=0, tiled=True)


def reorder_kernel(order_ref, blocks_ref, out_ref):
    for place in range(out_ref.shape[0]):
        out_ref[place] = blocks_ref[order_ref[place]]


def reorder(blocks, order):
    whole = pl.BlockSpec(memory_space=pltpu.VMEM)
    return pl.pallas_call(
        reorder_kernel,
        out_shape=jax.ShapeDtypeStruct(blocks.shape, blocks.dtype),
        in_specs=[pl.BlockSpec(memory_space=pltpu.SMEM), whole],
        out_specs=whole,
        compiler_params=pltpu.CompilerParams(vmem_limit_bytes=VMEM_BYTES),
        name="reorder",
    )(order, blocks)


def gather_features(rows):
    parts = lax.axis_size("dp")
    if parts == 2:
        other = lax.ppermute(rows, "dp", ((0, 1), (1, 0)))
        first = lax.axis_index("dp") == 0
        return [jnp.where(first, rows, other), jnp.where(first, other, rows)]
    whole = lax.all_gather(rows, "dp", axis=0, tiled=False)
    return [whole[part] for part in range(parts)]


def scatter_sum(partial):
    parts = lax.axis_size("dp")
    if parts == 2:
        half = partial.shape[1] // 2
        low, high = partial[:, :half], partial[:, half:]
        first = lax.axis_index("dp") == 0
        keep, send = jnp.where(first, low, high), jnp.where(first, high, low)
        other = lax.ppermute(send, "dp", ((0, 1), (1, 0)))
        return (keep.astype(jnp.float32) + other.astype(jnp.float32)).astype(jnp.bfloat16)
    return lax.psum_scatter(partial, "dp", scatter_dimension=1, tiled=True)


def relocate_spread(arrays, source, experts):
    outputs = []
    for array in arrays:
        blocks = array.reshape(experts, array.shape[1] // experts, array.shape[2])
        outputs.append(exchange(reorder(exchange(blocks), source)).reshape(array.shape[1:]))
    return outputs


PLANES = 4
GROUP = 4
KINDS = (((0, 1), (1, 2), (2, 3)), ((0, 2), (2, 3)), ((0, 1), (1, 3)), ((0, 3),))
KIND_ROW, UP_ROW, DOWN_ROW, FINAL_ROW = 0, 4, 8, 12


def plan_kernel(where_ref, source_ref, plan_ref, ends_ref):
    plane = where_ref[0]
    member = where_ref[1]
    for index in range(PLANES):
        plan_ref[KIND_ROW + index] = 0
        plan_ref[UP_ROW + index] = GROUP
        plan_ref[DOWN_ROW + index] = GROUP
        ends_ref[index] = 0
    for slot in range(PLANES * GROUP):
        low = slot // GROUP
        other = source_ref[slot]
        high = other // GROUP
        offset = (slot % GROUP) ^ member

        @pl.when(jnp.logical_and(high == low, plane == low))
        def _():
            plan_ref[FINAL_ROW + offset] = (other % GROUP) ^ member

        @pl.when(high > low)
        def _():
            turn = jnp.int32(PLANES - 1)
            for index in reversed(range(PLANES - 1)):
                turn = jnp.where(ends_ref[index] <= low, index, turn)
            ends_ref[turn] = high
            span = high - low
            kind = jnp.where(span == 3, 4, jnp.where(span == 2, 2 + low, 1))
            plan_ref[KIND_ROW + turn] = jnp.maximum(plan_ref[KIND_ROW + turn], kind)

            @pl.when(plane == low)
            def _():
                plan_ref[UP_ROW + turn] = offset
                plan_ref[FINAL_ROW + offset] = GROUP + 2 * turn + 1

            @pl.when(plane == high)
            def _():
                there = (other % GROUP) ^ member
                plan_ref[DOWN_ROW + turn] = there
                plan_ref[FINAL_ROW + there] = GROUP + 2 * turn


def make_plan(source, plane, member):
    smem = pl.BlockSpec(memory_space=pltpu.SMEM)
    return pl.pallas_call(
        plan_kernel,
        out_shape=jax.ShapeDtypeStruct((16,), jnp.int32),
        in_specs=[smem, smem],
        out_specs=smem,
        scratch_shapes=[pltpu.SMEM((PLANES,), jnp.int32)],
        name="plan",
    )(jnp.stack([plane, member]), source)


def cut_kernel(member_ref, first_ref, second_ref, *refs):
    outs, staged, in_sems, out_sems = refs[:GROUP], *refs[GROUP:]
    rows = outs[0].shape[1]
    loads, stores = [], []
    for offset in (1, 2, 3, 0):
        begin = pl.multiple_of((member_ref[0] ^ offset) * rows, rows)
        for which, array in enumerate((first_ref, second_ref)):
            loads.append(
                pltpu.make_async_copy(
                    array.at[pl.ds(begin, rows)],
                    staged.at[offset, which],
                    in_sems.at[offset, which],
                )
            )
            stores.append(
                pltpu.make_async_copy(
                    staged.at[offset, which],
                    outs[offset].at[which],
                    out_sems.at[offset, which],
                )
            )
    for load in loads:
        load.start()
    for load, store in zip(loads, stores):
        load.wait()
        store.start()
    for store in stores:
        store.wait()


def cut(first, second, member):
    rows, width = first.shape
    anywhere = pl.BlockSpec(memory_space=pl.ANY)
    piece = (2, rows // GROUP, width)
    return pl.pallas_call(
        cut_kernel,
        out_shape=[jax.ShapeDtypeStruct(piece, first.dtype)] * GROUP,
        in_specs=[pl.BlockSpec(memory_space=pltpu.SMEM), anywhere, anywhere],
        out_specs=[anywhere] * GROUP,
        scratch_shapes=[
            pltpu.VMEM((GROUP, *piece), first.dtype),
            pltpu.SemaphoreType.DMA((GROUP, 2)),
            pltpu.SemaphoreType.DMA((GROUP, 2)),
        ],
        compiler_params=pltpu.CompilerParams(vmem_limit_bytes=VMEM_BYTES),
        name="cut",
    )(member[None], first, second)


def choose_kernel(count, choice_ref, *refs):
    options, outs = refs[:count], refs[count:-3]
    staged, in_sems, out_sems = refs[-3:]
    for place in range(len(outs)):
        for index, option in enumerate(options):

            @pl.when(choice_ref[place] == index)
            def _():
                pltpu.make_async_copy(option, staged.at[place], in_sems.at[place]).start()

    for place, out in enumerate(outs):

        @pl.when(choice_ref[place] < count)
        def _():
            pltpu.make_async_copy(options[0], staged.at[place], in_sems.at[place]).wait()
            pltpu.make_async_copy(staged.at[place], out, out_sems.at[place]).start()

    for place, out in enumerate(outs):

        @pl.when(choice_ref[place] < count)
        def _():
            pltpu.make_async_copy(staged.at[place], out, out_sems.at[place]).wait()


def choose(choice, options):
    anywhere = pl.BlockSpec(memory_space=pl.ANY)
    shape, dtype = options[0].shape, options[0].dtype
    amount = choice.shape[0]
    return pl.pallas_call(
        functools.partial(choose_kernel, len(options)),
        out_shape=[jax.ShapeDtypeStruct(shape, dtype)] * amount,
        in_specs=[pl.BlockSpec(memory_space=pltpu.SMEM)] + [anywhere] * len(options),
        out_specs=[anywhere] * amount,
        scratch_shapes=[
            pltpu.VMEM((amount, *shape), dtype),
            pltpu.SemaphoreType.DMA((amount,)),
            pltpu.SemaphoreType.DMA((amount,)),
        ],
        compiler_params=pltpu.CompilerParams(vmem_limit_bytes=VMEM_BYTES),
        name="choose",
    )(choice, *options)


def within_plane(offset):
    return [(index, index ^ offset) for index in range(PLANES * GROUP)]


def between_planes(moves):
    return [(GROUP * a + index, GROUP * b + index) for a, b in moves for index in range(GROUP)]


def swap_round(moves):
    def run(up, down):
        return (
            lax.ppermute(up, "expert", between_planes(moves)),
            lax.ppermute(down, "expert", between_planes([(b, a) for a, b in moves])),
        )

    return run


def spread_quarters(first, second, source):
    index = lax.axis_index("expert")
    plane, member = index // GROUP, index % GROUP
    return make_plan(source, plane, member), cut(first, second, member)


def hand_out(pieces):
    return [pieces[0]] + [
        lax.ppermute(pieces[offset], "expert", within_plane(offset)) for offset in range(1, GROUP)
    ]


def swap_quarters(plan, held):
    ways = choose(plan[UP_ROW:FINAL_ROW], held)
    arrived = []
    for turn in range(PLANES):
        arrived += lax.switch(
            plan[KIND_ROW + turn],
            [lambda up, down: (up, down)] + [swap_round(moves) for moves in KINDS],
            ways[turn],
            ways[PLANES + turn],
        )
    return choose(plan[FINAL_ROW:], held + arrived)


def join_quarters(own):
    member = lax.axis_index("expert") % GROUP
    for bit in (1, 2):
        swap = (member & bit) != 0
        own = [jnp.where(swap, own[offset ^ bit], own[offset]) for offset in range(GROUP)]
    return [jnp.concatenate([piece[which] for piece in own], axis=0) for which in range(2)]


def per_device(
    tokens, cotangent, routes, gates, source, w_gate_up, w_down, moment_first, moment_second
):
    experts = lax.axis_size("expert")
    micro_count, token_count, part_width = tokens.shape
    model_width = w_gate_up.shape[1]
    hidden_part = w_gate_up.shape[3]
    top_count = routes.shape[2]
    capacity = max(2, 3 * token_count * top_count // (2 * experts))
    per_expert = micro_count * capacity
    slots = experts * per_expert
    all_tokens = micro_count * token_count

    swaps = experts == PLANES * GROUP
    if swaps:
        plan, pieces = spread_quarters(moment_first[0], moment_second[0], source)
        held = hand_out(pieces)

    pairs = token_count * top_count
    chosen = routes.reshape(micro_count, pairs)
    same = chosen[:, :, None] == chosen[:, None, :]
    order = jnp.arange(pairs, dtype=jnp.int32)
    earlier = order[None, :] < order[:, None]
    position = jnp.sum((same & earlier).astype(jnp.int32), axis=2)
    micro_ids = jnp.arange(micro_count, dtype=jnp.int32)[:, None]
    place = (chosen * per_expert + micro_ids * capacity + position).reshape(all_tokens, top_count)
    slot_ids = jnp.arange(slots, dtype=jnp.int32)
    flat_gates = gates.reshape(all_tokens, top_count)
    matches = [place[:, k][:, None] == slot_ids for k in range(top_count)]
    picks = [match.astype(jnp.bfloat16) for match in matches]
    plain = sum(picks[1:], picks[0])
    slot_gate = sum(
        jnp.sum(jnp.where(matches[k], flat_gates[:, k : k + 1], 0.0), axis=0)
        for k in range(top_count)
    )

    row_tokens = lax.dot_general(
        plain,
        tokens.reshape(all_tokens, part_width),
        contract_first,
        preferred_element_type=jnp.float32,
    ).astype(jnp.bfloat16)
    row_grads = (
        lax.dot_general(
            plain,
            cotangent.reshape(all_tokens, part_width),
            contract_first,
            preferred_element_type=jnp.float32,
        )
        * slot_gate[:, None]
    ).astype(jnp.bfloat16)
    if swaps:
        held[2], row_grads = lax.optimization_barrier((held[2], row_grads))
    grad_blocks = row_grads.reshape(experts, per_expert, part_width)
    here_tokens = exchange(row_tokens.reshape(experts, per_expert, part_width))
    here_grads = exchange(grad_blocks)
    token_parts = gather_features(here_tokens.reshape(slots, part_width))
    gate_up = w_gate_up.reshape(model_width, 2 * hidden_part)
    down = w_down.reshape(hidden_part, model_width)

    expert_in = jnp.concatenate(token_parts, axis=1)
    both = jnp.dot(expert_in, gate_up, preferred_element_type=jnp.float32).reshape(
        slots, 2, hidden_part
    )
    gate_pre = both[:, 0]
    up_pre = both[:, 1]
    gate_sig = jax.nn.sigmoid(gate_pre)
    hidden = (gate_pre * gate_sig * up_pre).astype(jnp.bfloat16)
    partial_out = jnp.dot(hidden, down, preferred_element_type=jnp.float32).astype(jnp.bfloat16)
    summed_out = scatter_sum(partial_out)
    if swaps:
        held, here_grads, summed_out = lax.optimization_barrier((held, here_grads, summed_out))
    back = exchange(
        jnp.concatenate([summed_out, hidden], axis=1).reshape(experts, per_expert, -1)
    )
    back_out = back[:, :, :part_width].reshape(slots, part_width)
    back_hidden = back[:, :, part_width:]
    layer_out = sum(
        flat_gates[:, k : k + 1] * jnp.dot(picks[k], back_out, preferred_element_type=jnp.float32)
        for k in range(top_count)
    )

    grad_parts = gather_features(here_grads.reshape(slots, part_width))
    grad_in = jnp.concatenate(grad_parts, axis=1)
    hidden_grad = lax.dot_general(
        grad_in, down, contract_second, preferred_element_type=jnp.float32
    )
    gate_grad = hidden_grad * up_pre * gate_sig * (1.0 + gate_pre * (1.0 - gate_sig))
    up_grad = hidden_grad * gate_pre * gate_sig
    both_grad = (
        jnp.stack([gate_grad, up_grad], axis=1)
        .astype(jnp.bfloat16)
        .reshape(slots, 2 * hidden_part)
    )
    partial_in = lax.dot_general(
        both_grad, gate_up, contract_second, preferred_element_type=jnp.float32
    ).astype(jnp.bfloat16)

    if swaps:
        held, back_hidden, partial_in = lax.optimization_barrier((held, back_hidden, partial_in))
        ready = swap_quarters(plan, held)
        ready, back_hidden = lax.optimization_barrier((ready, back_hidden))
        own = hand_out(ready)
    there = exchange(reorder(jnp.concatenate([back_hidden, grad_blocks], axis=2), source))
    there = there.reshape(slots, hidden_part + part_width)
    there_hidden = there[:, :hidden_part]
    there_grads = jnp.concatenate(gather_features(there[:, hidden_part:]), axis=1)

    summed_in = scatter_sum(partial_in)
    if swaps:
        there, own[2], summed_in = lax.optimization_barrier((there, own[2], summed_in))
    back_in = exchange(summed_in.reshape(experts, per_expert, part_width))
    if swaps:
        back_in, own = lax.optimization_barrier((back_in, own))
    token_grad = jnp.dot(
        plain, back_in.reshape(slots, part_width), preferred_element_type=jnp.float32
    )

    if swaps:
        old_first, old_second = join_quarters(own)
    else:
        old_first, old_second = relocate_spread((moment_first, moment_second), source, experts)
    down_grad = lax.dot_general(
        there_hidden, there_grads, contract_first, preferred_element_type=jnp.float32
    )
    first = 0.9 * old_first.astype(jnp.float32) + 0.1 * down_grad
    second = 0.999 * old_second.astype(jnp.float32) + 0.001 * down_grad * down_grad
    update = first / (jnp.sqrt(second) + 1e-08)
    shape = moment_first.shape
    return (
        layer_out.astype(jnp.bfloat16).reshape(tokens.shape),
        token_grad.astype(jnp.bfloat16).reshape(tokens.shape),
        update.astype(jnp.bfloat16).reshape(shape),
        first.astype(jnp.bfloat16).reshape(shape),
        second.astype(jnp.bfloat16).reshape(shape),
    )


def solution(mesh):
    placed = (
        P(None, "expert", "dp"),
        P(None, "expert", "dp"),
        P(None, "expert", None),
        P(None, "expert", None),
        P(),
        P("expert", None, None, "dp"),
        P("expert", "dp", None),
        P("expert", "dp", None),
        P("expert", "dp", None),
    )
    return jax.shard_map(
        per_device,
        mesh=mesh,
        in_specs=placed,
        out_specs=(
            P(None, "expert", "dp"),
            P(None, "expert", "dp"),
            P("expert", "dp", None),
            P("expert", "dp", None),
            P("expert", "dp", None),
        ),
        check_vma=False,
    )
```

```python
import functools

import jax
import jax.numpy as jnp
from jax import lax
from jax.experimental import pallas as pl
from jax.experimental.pallas import tpu as pltpu
from jax.sharding import PartitionSpec as P

contract_first = (((0,), (0,)), ((), ()))
contract_second = (((1,), (1,)), ((), ()))
VMEM_BYTES = 32 * 1024 * 1024


def fence(*values):
    return lax.optimization_barrier(values)


def exchange(blocks):
    return lax.all_to_all(blocks, "expert", split_axis=0, concat_axis=0, tiled=True)


def reorder_kernel(order_ref, blocks_ref, out_ref):
    for place in range(out_ref.shape[0]):
        out_ref[place] = blocks_ref[order_ref[place]]


def reorder(blocks, order):
    whole = pl.BlockSpec(memory_space=pltpu.VMEM)
    return pl.pallas_call(
        reorder_kernel,
        out_shape=jax.ShapeDtypeStruct(blocks.shape, blocks.dtype),
        in_specs=[pl.BlockSpec(memory_space=pltpu.SMEM), whole],
        out_specs=whole,
        compiler_params=pltpu.CompilerParams(vmem_limit_bytes=VMEM_BYTES),
        name="reorder",
    )(order, blocks)


def gather_features(rows):
    parts = lax.axis_size("dp")
    if parts == 2:
        other = lax.ppermute(rows, "dp", ((0, 1), (1, 0)))
        first = lax.axis_index("dp") == 0
        return [jnp.where(first, rows, other), jnp.where(first, other, rows)]
    whole = lax.all_gather(rows, "dp", axis=0, tiled=False)
    return [whole[part] for part in range(parts)]


def scatter_sum(partial):
    parts = lax.axis_size("dp")
    if parts == 2:
        half = partial.shape[1] // 2
        low, high = partial[:, :half], partial[:, half:]
        first = lax.axis_index("dp") == 0
        keep, send = jnp.where(first, low, high), jnp.where(first, high, low)
        other = lax.ppermute(send, "dp", ((0, 1), (1, 0)))
        return (keep.astype(jnp.float32) + other.astype(jnp.float32)).astype(jnp.bfloat16)
    return lax.psum_scatter(partial, "dp", scatter_dimension=1, tiled=True)


def relocate_spread(arrays, source, experts):
    outputs = []
    for array in arrays:
        blocks = array.reshape(experts, array.shape[1] // experts, array.shape[2])
        outputs.append(exchange(reorder(exchange(blocks), source)).reshape(array.shape[1:]))
    return outputs


PLANES = 4
GROUP = 4
KINDS = (((0, 1), (1, 2), (2, 3)), ((0, 2), (2, 3)), ((0, 1), (1, 3)), ((0, 3),))
KIND_ROW, UP_ROW, DOWN_ROW, FINAL_ROW = 0, 4, 8, 12


def plan_kernel(where_ref, source_ref, plan_ref, ends_ref):
    plane = where_ref[0]
    member = where_ref[1]
    for index in range(PLANES):
        plan_ref[KIND_ROW + index] = 0
        plan_ref[UP_ROW + index] = GROUP
        plan_ref[DOWN_ROW + index] = GROUP
        ends_ref[index] = 0
    for slot in range(PLANES * GROUP):
        low = slot // GROUP
        other = source_ref[slot]
        high = other // GROUP
        offset = (slot % GROUP) ^ member

        @pl.when(jnp.logical_and(high == low, plane == low))
        def _():
            plan_ref[FINAL_ROW + offset] = (other % GROUP) ^ member

        @pl.when(high > low)
        def _():
            turn = jnp.int32(PLANES - 1)
            for index in reversed(range(PLANES - 1)):
                turn = jnp.where(ends_ref[index] <= low, index, turn)
            ends_ref[turn] = high
            span = high - low
            kind = jnp.where(span == 3, 4, jnp.where(span == 2, 2 + low, 1))
            plan_ref[KIND_ROW + turn] = jnp.maximum(plan_ref[KIND_ROW + turn], kind)

            @pl.when(plane == low)
            def _():
                plan_ref[UP_ROW + turn] = offset
                plan_ref[FINAL_ROW + offset] = GROUP + 2 * turn + 1

            @pl.when(plane == high)
            def _():
                there = (other % GROUP) ^ member
                plan_ref[DOWN_ROW + turn] = there
                plan_ref[FINAL_ROW + there] = GROUP + 2 * turn


def make_plan(source, plane, member):
    smem = pl.BlockSpec(memory_space=pltpu.SMEM)
    return pl.pallas_call(
        plan_kernel,
        out_shape=jax.ShapeDtypeStruct((16,), jnp.int32),
        in_specs=[smem, smem],
        out_specs=smem,
        scratch_shapes=[pltpu.SMEM((PLANES,), jnp.int32)],
        name="plan",
    )(jnp.stack([plane, member]), source)


def cut_kernel(member_ref, first_ref, second_ref, *refs):
    outs, staged, in_sems, out_sems = refs[:GROUP], *refs[GROUP:]
    rows = outs[0].shape[1]
    loads, stores = [], []
    for offset in (1, 2, 3, 0):
        begin = pl.multiple_of((member_ref[0] ^ offset) * rows, rows)
        for which, array in enumerate((first_ref, second_ref)):
            loads.append(
                pltpu.make_async_copy(
                    array.at[pl.ds(begin, rows)],
                    staged.at[offset, which],
                    in_sems.at[offset, which],
                )
            )
            stores.append(
                pltpu.make_async_copy(
                    staged.at[offset, which],
                    outs[offset].at[which],
                    out_sems.at[offset, which],
                )
            )
    for load in loads:
        load.start()
    for load, store in zip(loads, stores):
        load.wait()
        store.start()
    for store in stores:
        store.wait()


def cut(first, second, member):
    rows, width = first.shape
    anywhere = pl.BlockSpec(memory_space=pl.ANY)
    piece = (2, rows // GROUP, width)
    return pl.pallas_call(
        cut_kernel,
        out_shape=[jax.ShapeDtypeStruct(piece, first.dtype)] * GROUP,
        in_specs=[pl.BlockSpec(memory_space=pltpu.SMEM), anywhere, anywhere],
        out_specs=[anywhere] * GROUP,
        scratch_shapes=[
            pltpu.VMEM((GROUP, *piece), first.dtype),
            pltpu.SemaphoreType.DMA((GROUP, 2)),
            pltpu.SemaphoreType.DMA((GROUP, 2)),
        ],
        compiler_params=pltpu.CompilerParams(vmem_limit_bytes=VMEM_BYTES),
        name="cut",
    )(member[None], first, second)


def choose_kernel(count, choice_ref, *refs):
    options, outs = refs[:count], refs[count:-3]
    staged, in_sems, out_sems = refs[-3:]
    for place in range(len(outs)):
        for index, option in enumerate(options):

            @pl.when(choice_ref[place] == index)
            def _():
                pltpu.make_async_copy(option, staged.at[place], in_sems.at[place]).start()

    for place, out in enumerate(outs):

        @pl.when(choice_ref[place] < count)
        def _():
            pltpu.make_async_copy(options[0], staged.at[place], in_sems.at[place]).wait()
            pltpu.make_async_copy(staged.at[place], out, out_sems.at[place]).start()

    for place, out in enumerate(outs):

        @pl.when(choice_ref[place] < count)
        def _():
            pltpu.make_async_copy(staged.at[place], out, out_sems.at[place]).wait()


def choose(choice, options):
    anywhere = pl.BlockSpec(memory_space=pl.ANY)
    shape, dtype = options[0].shape, options[0].dtype
    amount = choice.shape[0]
    return pl.pallas_call(
        functools.partial(choose_kernel, len(options)),
        out_shape=[jax.ShapeDtypeStruct(shape, dtype)] * amount,
        in_specs=[pl.BlockSpec(memory_space=pltpu.SMEM)] + [anywhere] * len(options),
        out_specs=[anywhere] * amount,
        scratch_shapes=[
            pltpu.VMEM((amount, *shape), dtype),
            pltpu.SemaphoreType.DMA((amount,)),
            pltpu.SemaphoreType.DMA((amount,)),
        ],
        compiler_params=pltpu.CompilerParams(vmem_limit_bytes=VMEM_BYTES),
        name="choose",
    )(choice, *options)


def within_plane(offset):
    return [(index, index ^ offset) for index in range(PLANES * GROUP)]


def between_planes(moves):
    return [(GROUP * a + index, GROUP * b + index) for a, b in moves for index in range(GROUP)]


def swap_round(moves):
    def run(up, down):
        return (
            lax.ppermute(up, "expert", between_planes(moves)),
            lax.ppermute(down, "expert", between_planes([(b, a) for a, b in moves])),
        )

    return run


def hand_over(pieces, offset):
    return lax.ppermute(pieces[offset], "expert", within_plane(offset))


def swap_pieces(turn, plan, ways):
    return list(
        lax.switch(
            plan[KIND_ROW + turn],
            [lambda up, down: (up, down)] + [swap_round(moves) for moves in KINDS],
            ways[turn],
            ways[PLANES + turn],
        )
    )


def join_quarters(own):
    member = lax.axis_index("expert") % GROUP
    for bit in (1, 2):
        swap = (member & bit) != 0
        own = [jnp.where(swap, own[offset ^ bit], own[offset]) for offset in range(GROUP)]
    return [jnp.concatenate([piece[which] for piece in own], axis=0) for which in range(2)]


def per_device(
    tokens, cotangent, routes, gates, source, w_gate_up, w_down, moment_first, moment_second
):
    experts = lax.axis_size("expert")
    micro_count, token_count, part_width = tokens.shape
    model_width = w_gate_up.shape[1]
    hidden_part = w_gate_up.shape[3]
    top_count = routes.shape[2]
    capacity = max(2, 3 * token_count * top_count // (2 * experts))
    per_expert = micro_count * capacity
    slots = experts * per_expert
    all_tokens = micro_count * token_count
    swaps = experts == PLANES * GROUP

    pairs = token_count * top_count
    chosen = routes.reshape(micro_count, pairs)
    same = chosen[:, :, None] == chosen[:, None, :]
    order = jnp.arange(pairs, dtype=jnp.int32)
    earlier = order[None, :] < order[:, None]
    position = jnp.sum((same & earlier).astype(jnp.int32), axis=2)
    micro_ids = jnp.arange(micro_count, dtype=jnp.int32)[:, None]
    place = (chosen * per_expert + micro_ids * capacity + position).reshape(all_tokens, top_count)
    slot_ids = jnp.arange(slots, dtype=jnp.int32)
    flat_gates = gates.reshape(all_tokens, top_count)
    matches = [place[:, k][:, None] == slot_ids for k in range(top_count)]
    picks = [match.astype(jnp.bfloat16) for match in matches]
    plain = sum(picks[1:], picks[0])
    slot_gate = sum(
        jnp.sum(jnp.where(matches[k], flat_gates[:, k : k + 1], 0.0), axis=0)
        for k in range(top_count)
    )

    row_tokens = lax.dot_general(
        plain,
        tokens.reshape(all_tokens, part_width),
        contract_first,
        preferred_element_type=jnp.float32,
    ).astype(jnp.bfloat16)
    if swaps:
        index = lax.axis_index("expert")
        plane, member = index // GROUP, index % GROUP
        plan = make_plan(source, plane, member)
        pieces = cut(moment_first[0], moment_second[0], member)
        row_tokens, pieces = fence(row_tokens, pieces)
        held = [pieces[0], None, hand_over(pieces, 2), None]
    here_tokens = exchange(row_tokens.reshape(experts, per_expert, part_width))
    row_grads = (
        lax.dot_general(
            plain,
            cotangent.reshape(all_tokens, part_width),
            contract_first,
            preferred_element_type=jnp.float32,
        )
        * slot_gate[:, None]
    ).astype(jnp.bfloat16)
    gate_up = w_gate_up.reshape(model_width, 2 * hidden_part)
    down = w_down.reshape(hidden_part, model_width)

    if swaps:
        here_tokens, row_grads, gate_up, held[2], pieces, plan = fence(
            here_tokens, row_grads, gate_up, held[2], pieces, plan
        )
        held[1], held[3] = hand_over(pieces, 1), hand_over(pieces, 3)
    grad_blocks = row_grads.reshape(experts, per_expert, part_width)
    here_grads = exchange(grad_blocks)
    expert_in = jnp.concatenate(gather_features(here_tokens.reshape(slots, part_width)), axis=1)
    both = jnp.dot(expert_in, gate_up, preferred_element_type=jnp.float32).reshape(
        slots, 2, hidden_part
    )
    gate_pre = both[:, 0]
    up_pre = both[:, 1]
    gate_sig = jax.nn.sigmoid(gate_pre)
    hidden = (gate_pre * gate_sig * up_pre).astype(jnp.bfloat16)
    partial_out = jnp.dot(hidden, down, preferred_element_type=jnp.float32).astype(jnp.bfloat16)

    if swaps:
        held, here_grads, hidden, partial_out = fence(held, here_grads, hidden, partial_out)
        ways = choose(plan[UP_ROW:FINAL_ROW], held)
        ways, partial_out = fence(ways, partial_out)
        arrived = swap_pieces(0, plan, ways)
    summed_out = scatter_sum(partial_out)

    if swaps:
        summed_out, here_grads, arrived = fence(summed_out, here_grads, arrived)
    back = exchange(
        jnp.concatenate([summed_out, hidden], axis=1).reshape(experts, per_expert, -1)
    )
    grad_in = jnp.concatenate(gather_features(here_grads.reshape(slots, part_width)), axis=1)
    hidden_grad = lax.dot_general(
        grad_in, down, contract_second, preferred_element_type=jnp.float32
    )
    gate_grad = hidden_grad * up_pre * gate_sig * (1.0 + gate_pre * (1.0 - gate_sig))
    up_grad = hidden_grad * gate_pre * gate_sig
    both_grad = (
        jnp.stack([gate_grad, up_grad], axis=1)
        .astype(jnp.bfloat16)
        .reshape(slots, 2 * hidden_part)
    )
    partial_in = lax.dot_general(
        both_grad, gate_up, contract_second, preferred_element_type=jnp.float32
    ).astype(jnp.bfloat16)

    if swaps:
        back, partial_in, arrived, ways = fence(back, partial_in, arrived, ways)
        arrived += swap_pieces(1, plan, ways)
    summed_in = scatter_sum(partial_in)
    to_move = reorder(jnp.concatenate([back[:, :, part_width:], grad_blocks], axis=2), source)
    if swaps:
        summed_in, to_move, arrived, ways = fence(summed_in, to_move, arrived, ways)
        arrived += swap_pieces(2, plan, ways)
        arrived += swap_pieces(3, plan, ways)
        ready = choose(plan[FINAL_ROW:], held + arrived)

    if swaps:
        to_move, ready = fence(to_move, ready)
        own = [ready[0], hand_over(ready, 1), hand_over(ready, 2), None]
    there = exchange(to_move).reshape(slots, hidden_part + part_width)
    back_out = back[:, :, :part_width].reshape(slots, part_width)
    layer_out = sum(
        flat_gates[:, k : k + 1] * jnp.dot(picks[k], back_out, preferred_element_type=jnp.float32)
        for k in range(top_count)
    ).astype(jnp.bfloat16)

    if swaps:
        there, summed_in, own[1], own[2], ready, layer_out = fence(
            there, summed_in, own[1], own[2], ready, layer_out
        )
        own[3] = hand_over(ready, 3)
    back_in = exchange(summed_in.reshape(experts, per_expert, part_width))
    token_grad = jnp.dot(
        plain, back_in.reshape(slots, part_width), preferred_element_type=jnp.float32
    )

    there_hidden = there[:, :hidden_part]
    there_grads = jnp.concatenate(gather_features(there[:, hidden_part:]), axis=1)
    if swaps:
        old_first, old_second = join_quarters(own)
    else:
        old_first, old_second = relocate_spread((moment_first, moment_second), source, experts)
    down_grad = lax.dot_general(
        there_hidden, there_grads, contract_first, preferred_element_type=jnp.float32
    )
    first = 0.9 * old_first.astype(jnp.float32) + 0.1 * down_grad
    second = 0.999 * old_second.astype(jnp.float32) + 0.001 * down_grad * down_grad
    update = first / (jnp.sqrt(second) + 1e-08)
    shape = moment_first.shape
    return (
        layer_out.reshape(tokens.shape),
        token_grad.astype(jnp.bfloat16).reshape(tokens.shape),
        update.astype(jnp.bfloat16).reshape(shape),
        first.astype(jnp.bfloat16).reshape(shape),
        second.astype(jnp.bfloat16).reshape(shape),
    )


def solution(mesh):
    placed = (
        P(None, "expert", "dp"),
        P(None, "expert", "dp"),
        P(None, "expert", None),
        P(None, "expert", None),
        P(),
        P("expert", None, None, "dp"),
        P("expert", "dp", None),
        P("expert", "dp", None),
        P("expert", "dp", None),
    )
    return jax.shard_map(
        per_device,
        mesh=mesh,
        in_specs=placed,
        out_specs=(
            P(None, "expert", "dp"),
            P(None, "expert", "dp"),
            P("expert", "dp", None),
            P("expert", "dp", None),
            P("expert", "dp", None),
        ),
        check_vma=False,
    )
```

```python
import functools

import jax
import jax.numpy as jnp
from jax import lax
from jax.experimental import pallas as pl
from jax.experimental.pallas import tpu as pltpu
from jax.sharding import PartitionSpec as P

contract_first = (((0,), (0,)), ((), ()))
contract_second = (((1,), (1,)), ((), ()))
VMEM_BYTES = 32 * 1024 * 1024


def fence(*values):
    return lax.optimization_barrier(values)


def exchange(blocks):
    return lax.all_to_all(blocks, "expert", split_axis=0, concat_axis=0, tiled=True)


def reorder_kernel(order_ref, blocks_ref, out_ref):
    for place in range(out_ref.shape[0]):
        out_ref[place] = blocks_ref[order_ref[place]]


def reorder(blocks, order):
    whole = pl.BlockSpec(memory_space=pltpu.VMEM)
    return pl.pallas_call(
        reorder_kernel,
        out_shape=jax.ShapeDtypeStruct(blocks.shape, blocks.dtype),
        in_specs=[pl.BlockSpec(memory_space=pltpu.SMEM), whole],
        out_specs=whole,
        compiler_params=pltpu.CompilerParams(vmem_limit_bytes=VMEM_BYTES),
        name="reorder",
    )(order, blocks)


def gather_features(rows):
    parts = lax.axis_size("dp")
    if parts == 2:
        other = lax.ppermute(rows, "dp", ((0, 1), (1, 0)))
        first = lax.axis_index("dp") == 0
        return [jnp.where(first, rows, other), jnp.where(first, other, rows)]
    whole = lax.all_gather(rows, "dp", axis=0, tiled=False)
    return [whole[part] for part in range(parts)]


def scatter_sum(partial):
    parts = lax.axis_size("dp")
    if parts == 2:
        half = partial.shape[1] // 2
        low, high = partial[:, :half], partial[:, half:]
        first = lax.axis_index("dp") == 0
        keep, send = jnp.where(first, low, high), jnp.where(first, high, low)
        other = lax.ppermute(send, "dp", ((0, 1), (1, 0)))
        return (keep.astype(jnp.float32) + other.astype(jnp.float32)).astype(jnp.bfloat16)
    return lax.psum_scatter(partial, "dp", scatter_dimension=1, tiled=True)


def relocate_spread(arrays, source, experts):
    outputs = []
    for array in arrays:
        blocks = array.reshape(experts, array.shape[1] // experts, array.shape[2])
        outputs.append(exchange(reorder(exchange(blocks), source)).reshape(array.shape[1:]))
    return outputs


PLANES = 4
GROUP = 4
KINDS = (((0, 1), (1, 2), (2, 3)), ((0, 2), (2, 3)), ((0, 1), (1, 3)), ((0, 3),))
KIND_ROW, UP_ROW, DOWN_ROW, FINAL_ROW = 0, 4, 8, 12


def plan_kernel(where_ref, source_ref, plan_ref, ends_ref):
    plane = where_ref[0]
    member = where_ref[1]
    for index in range(PLANES):
        plan_ref[KIND_ROW + index] = 0
        plan_ref[UP_ROW + index] = GROUP
        plan_ref[DOWN_ROW + index] = GROUP
        ends_ref[index] = 0
    for slot in range(PLANES * GROUP):
        low = slot // GROUP
        other = source_ref[slot]
        high = other // GROUP
        offset = (slot % GROUP) ^ member

        @pl.when(jnp.logical_and(high == low, plane == low))
        def _():
            plan_ref[FINAL_ROW + offset] = (other % GROUP) ^ member

        @pl.when(high > low)
        def _():
            turn = jnp.int32(PLANES - 1)
            for index in reversed(range(PLANES - 1)):
                turn = jnp.where(ends_ref[index] <= low, index, turn)
            ends_ref[turn] = high
            span = high - low
            kind = jnp.where(span == 3, 4, jnp.where(span == 2, 2 + low, 1))
            plan_ref[KIND_ROW + turn] = jnp.maximum(plan_ref[KIND_ROW + turn], kind)

            @pl.when(plane == low)
            def _():
                plan_ref[UP_ROW + turn] = offset
                plan_ref[FINAL_ROW + offset] = GROUP + 2 * turn + 1

            @pl.when(plane == high)
            def _():
                there = (other % GROUP) ^ member
                plan_ref[DOWN_ROW + turn] = there
                plan_ref[FINAL_ROW + there] = GROUP + 2 * turn


def make_plan(source, plane, member):
    smem = pl.BlockSpec(memory_space=pltpu.SMEM)
    return pl.pallas_call(
        plan_kernel,
        out_shape=jax.ShapeDtypeStruct((16,), jnp.int32),
        in_specs=[smem, smem],
        out_specs=smem,
        scratch_shapes=[pltpu.SMEM((PLANES,), jnp.int32)],
        name="plan",
    )(jnp.stack([plane, member]), source)


def cut_kernel(member_ref, *refs):
    count = (len(refs) - 3) // (1 + GROUP)
    arrays, outs = refs[:count], refs[count:-3]
    staged, in_sems, out_sems = refs[-3:]
    rows = outs[0].shape[0]
    loads, stores = [], []
    for which, array in enumerate(arrays):
        for offset in (2, 3, 1, 0):
            begin = pl.multiple_of((member_ref[0] ^ offset) * rows, rows)
            place = which * GROUP + offset
            loads.append(
                pltpu.make_async_copy(
                    array.at[pl.ds(begin, rows)], staged.at[place], in_sems.at[place]
                )
            )
            stores.append(
                pltpu.make_async_copy(staged.at[place], outs[place], out_sems.at[place])
            )
    for load in loads:
        load.start()
    for load, store in zip(loads, stores):
        load.wait()
        store.start()
    for store in stores:
        store.wait()


def cut(arrays, member):
    rows, width = arrays[0].shape
    anywhere = pl.BlockSpec(memory_space=pl.ANY)
    piece = (rows // GROUP, width)
    amount = GROUP * len(arrays)
    pieces = pl.pallas_call(
        cut_kernel,
        out_shape=[jax.ShapeDtypeStruct(piece, arrays[0].dtype)] * amount,
        in_specs=[pl.BlockSpec(memory_space=pltpu.SMEM)] + [anywhere] * len(arrays),
        out_specs=[anywhere] * amount,
        scratch_shapes=[
            pltpu.VMEM((amount, *piece), arrays[0].dtype),
            pltpu.SemaphoreType.DMA((amount,)),
            pltpu.SemaphoreType.DMA((amount,)),
        ],
        compiler_params=pltpu.CompilerParams(vmem_limit_bytes=VMEM_BYTES),
        name="cut",
    )(member[None], *arrays)
    return [list(pieces[at : at + GROUP]) for at in range(0, amount, GROUP)]


def choose_kernel(count, choice_ref, *refs):
    options, outs = refs[:count], refs[count:-3]
    staged, in_sems, out_sems = refs[-3:]
    for place in range(len(outs)):
        for index, option in enumerate(options):

            @pl.when(choice_ref[place] == index)
            def _():
                pltpu.make_async_copy(option, staged.at[place], in_sems.at[place]).start()

    for place, out in enumerate(outs):

        @pl.when(choice_ref[place] < count)
        def _():
            pltpu.make_async_copy(options[0], staged.at[place], in_sems.at[place]).wait()
            pltpu.make_async_copy(staged.at[place], out, out_sems.at[place]).start()

    for place, out in enumerate(outs):

        @pl.when(choice_ref[place] < count)
        def _():
            pltpu.make_async_copy(staged.at[place], out, out_sems.at[place]).wait()


def choose(choice, options):
    anywhere = pl.BlockSpec(memory_space=pl.ANY)
    shape, dtype = options[0].shape, options[0].dtype
    amount = choice.shape[0]
    return pl.pallas_call(
        functools.partial(choose_kernel, len(options)),
        out_shape=[jax.ShapeDtypeStruct(shape, dtype)] * amount,
        in_specs=[pl.BlockSpec(memory_space=pltpu.SMEM)] + [anywhere] * len(options),
        out_specs=[anywhere] * amount,
        scratch_shapes=[
            pltpu.VMEM((amount, *shape), dtype),
            pltpu.SemaphoreType.DMA((amount,)),
            pltpu.SemaphoreType.DMA((amount,)),
        ],
        compiler_params=pltpu.CompilerParams(vmem_limit_bytes=VMEM_BYTES),
        name="choose",
    )(choice, *options)


def within_plane(offset):
    return [(index, index ^ offset) for index in range(PLANES * GROUP)]


def between_planes(moves):
    return [(GROUP * a + index, GROUP * b + index) for a, b in moves for index in range(GROUP)]


def swap_round(moves):
    def run(up, down):
        return (
            lax.ppermute(up, "expert", between_planes(moves)),
            lax.ppermute(down, "expert", between_planes([(b, a) for a, b in moves])),
        )

    return run


def hand_over(pieces):
    return list(pieces[:1]) + [
        lax.ppermute(pieces[offset], "expert", within_plane(offset)) for offset in range(1, GROUP)
    ]


def swap_pieces(turn, plan, ways):
    return list(
        lax.switch(
            plan[KIND_ROW + turn],
            [lambda up, down: (up, down)] + [swap_round(moves) for moves in KINDS],
            ways[turn],
            ways[PLANES + turn],
        )
    )


def join_quarters(own):
    member = lax.axis_index("expert") % GROUP
    for bit in (1, 2):
        swap = (member & bit) != 0
        own = [jnp.where(swap, own[offset ^ bit], own[offset]) for offset in range(GROUP)]
    return jnp.concatenate(own, axis=0)


def per_device(
    tokens, cotangent, routes, gates, source, w_gate_up, w_down, moment_first, moment_second
):
    experts = lax.axis_size("expert")
    micro_count, token_count, part_width = tokens.shape
    model_width = w_gate_up.shape[1]
    hidden_part = w_gate_up.shape[3]
    top_count = routes.shape[2]
    capacity = max(2, 3 * token_count * top_count // (2 * experts))
    per_expert = micro_count * capacity
    slots = experts * per_expert
    all_tokens = micro_count * token_count
    swaps = experts == PLANES * GROUP

    pairs = token_count * top_count
    chosen = routes.reshape(micro_count, pairs)
    same = chosen[:, :, None] == chosen[:, None, :]
    order = jnp.arange(pairs, dtype=jnp.int32)
    earlier = order[None, :] < order[:, None]
    position = jnp.sum((same & earlier).astype(jnp.int32), axis=2)
    micro_ids = jnp.arange(micro_count, dtype=jnp.int32)[:, None]
    place = (chosen * per_expert + micro_ids * capacity + position).reshape(all_tokens, top_count)
    slot_ids = jnp.arange(slots, dtype=jnp.int32)
    flat_gates = gates.reshape(all_tokens, top_count)
    matches = [place[:, k][:, None] == slot_ids for k in range(top_count)]
    picks = [match.astype(jnp.bfloat16) for match in matches]
    plain = sum(picks[1:], picks[0])
    slot_gate = sum(
        jnp.sum(jnp.where(matches[k], flat_gates[:, k : k + 1], 0.0), axis=0)
        for k in range(top_count)
    )

    row_tokens = lax.dot_general(
        plain,
        tokens.reshape(all_tokens, part_width),
        contract_first,
        preferred_element_type=jnp.float32,
    ).astype(jnp.bfloat16)
    if swaps:
        index = lax.axis_index("expert")
        plane, member = index // GROUP, index % GROUP
        plan = make_plan(source, plane, member)
        row_tokens, (pieces_a, pieces_b) = fence(
            row_tokens, cut((moment_first[0], moment_second[0]), member)
        )
        held_a = hand_over(pieces_a)
    here_tokens = exchange(row_tokens.reshape(experts, per_expert, part_width))
    row_grads = (
        lax.dot_general(
            plain,
            cotangent.reshape(all_tokens, part_width),
            contract_first,
            preferred_element_type=jnp.float32,
        )
        * slot_gate[:, None]
    ).astype(jnp.bfloat16)
    gate_up = w_gate_up.reshape(model_width, 2 * hidden_part)
    down = w_down.reshape(hidden_part, model_width)

    if swaps:
        here_tokens, row_grads, gate_up, held_a, pieces_b, plan = fence(
            here_tokens, row_grads, gate_up, held_a, pieces_b, plan
        )
        held_b = hand_over(pieces_b)
        ways_a = choose(plan[UP_ROW:FINAL_ROW], held_a)
        arrived_a = swap_pieces(0, plan, ways_a) + swap_pieces(1, plan, ways_a)
    grad_blocks = row_grads.reshape(experts, per_expert, part_width)
    here_grads = exchange(grad_blocks)
    expert_in = jnp.concatenate(gather_features(here_tokens.reshape(slots, part_width)), axis=1)
    if swaps:
        expert_in, here_grads, arrived_a, held_b = fence(
            expert_in, here_grads, arrived_a, held_b
        )
    both = jnp.dot(expert_in, gate_up, preferred_element_type=jnp.float32)
    gate_pre = both[:, :hidden_part]
    up_pre = both[:, hidden_part:]
    gate_sig = jax.nn.sigmoid(gate_pre)
    hidden = (gate_pre * gate_sig * up_pre).astype(jnp.bfloat16)
    partial_out = jnp.dot(hidden, down, preferred_element_type=jnp.float32).astype(jnp.bfloat16)

    if swaps:
        hidden, partial_out, ways_a, held_b = fence(hidden, partial_out, ways_a, held_b)
        arrived_a += swap_pieces(2, plan, ways_a) + swap_pieces(3, plan, ways_a)
        ways_b = choose(plan[UP_ROW:FINAL_ROW], held_b)
        arrived_b = swap_pieces(0, plan, ways_b)
    summed_out = scatter_sum(partial_out)

    if swaps:
        summed_out, here_grads, arrived_a, arrived_b, ways_b = fence(
            summed_out, here_grads, arrived_a, arrived_b, ways_b
        )
        own_a = hand_over(choose(plan[FINAL_ROW:], [*held_a, *arrived_a]))
        arrived_b += swap_pieces(1, plan, ways_b)
    back = exchange(
        jnp.concatenate([summed_out, hidden], axis=1).reshape(experts, per_expert, -1)
    )
    grad_in = jnp.concatenate(gather_features(here_grads.reshape(slots, part_width)), axis=1)
    hidden_grad = lax.dot_general(
        grad_in, down, contract_second, preferred_element_type=jnp.float32
    )
    gate_grad = hidden_grad * up_pre * gate_sig * (1.0 + gate_pre * (1.0 - gate_sig))
    up_grad = hidden_grad * gate_pre * gate_sig
    both_grad = jnp.concatenate([gate_grad, up_grad], axis=1).astype(jnp.bfloat16)
    partial_in = lax.dot_general(
        both_grad, gate_up, contract_second, preferred_element_type=jnp.float32
    ).astype(jnp.bfloat16)
    to_move = reorder(jnp.concatenate([back[:, :, part_width:], grad_blocks], axis=2), source)

    if swaps:
        to_move, partial_in, own_a, arrived_b, ways_b = fence(
            to_move, partial_in, own_a, arrived_b, ways_b
        )
        arrived_b += swap_pieces(2, plan, ways_b) + swap_pieces(3, plan, ways_b)
        ready_b = choose(plan[FINAL_ROW:], [*held_b, *arrived_b])
    there = exchange(to_move).reshape(slots, hidden_part + part_width)
    summed_in = scatter_sum(partial_in)
    back_out = back[:, :, :part_width].reshape(slots, part_width)
    layer_out = sum(
        flat_gates[:, k : k + 1] * jnp.dot(picks[k], back_out, preferred_element_type=jnp.float32)
        for k in range(top_count)
    ).astype(jnp.bfloat16)

    if swaps:
        there, summed_in, ready_b, layer_out = fence(there, summed_in, ready_b, layer_out)
        own_b = hand_over(ready_b)
    back_in = exchange(summed_in.reshape(experts, per_expert, part_width))
    token_grad = jnp.dot(
        plain, back_in.reshape(slots, part_width), preferred_element_type=jnp.float32
    )

    there_hidden = there[:, :hidden_part]
    there_grads = jnp.concatenate(gather_features(there[:, hidden_part:]), axis=1)
    if swaps:
        old_first, old_second = join_quarters(own_a), join_quarters(own_b)
    else:
        old_first, old_second = relocate_spread((moment_first, moment_second), source, experts)
    down_grad = lax.dot_general(
        there_hidden, there_grads, contract_first, preferred_element_type=jnp.float32
    )
    first = 0.9 * old_first.astype(jnp.float32) + 0.1 * down_grad
    second = 0.999 * old_second.astype(jnp.float32) + 0.001 * down_grad * down_grad
    update = first / (jnp.sqrt(second) + 1e-08)
    shape = moment_first.shape
    return (
        layer_out.reshape(tokens.shape),
        token_grad.astype(jnp.bfloat16).reshape(tokens.shape),
        update.astype(jnp.bfloat16).reshape(shape),
        first.astype(jnp.bfloat16).reshape(shape),
        second.astype(jnp.bfloat16).reshape(shape),
    )


def solution(mesh):
    placed = (
        P(None, "expert", "dp"),
        P(None, "expert", "dp"),
        P(None, "expert", None),
        P(None, "expert", None),
        P(),
        P("expert", None, None, "dp"),
        P("expert", "dp", None),
        P("expert", "dp", None),
        P("expert", "dp", None),
    )
    return jax.shard_map(
        per_device,
        mesh=mesh,
        in_specs=placed,
        out_specs=(
            P(None, "expert", "dp"),
            P(None, "expert", "dp"),
            P("expert", "dp", None),
            P("expert", "dp", None),
            P("expert", "dp", None),
        ),
        check_vma=False,
    )
```

```python
import functools

import jax
import jax.numpy as jnp
from jax import lax
from jax.experimental import pallas as pl
from jax.experimental.pallas import tpu as pltpu
from jax.sharding import PartitionSpec as P

contract_first = (((0,), (0,)), ((), ()))
contract_second = (((1,), (1,)), ((), ()))
VMEM_BYTES = 32 * 1024 * 1024


def fence(*values):
    return lax.optimization_barrier(values)


def exchange(blocks):
    return lax.all_to_all(blocks, "expert", split_axis=0, concat_axis=0, tiled=True)


def reorder_kernel(order_ref, blocks_ref, out_ref):
    for place in range(out_ref.shape[0]):
        out_ref[place] = blocks_ref[order_ref[place]]


def reorder(blocks, order):
    whole = pl.BlockSpec(memory_space=pltpu.VMEM)
    return pl.pallas_call(
        reorder_kernel,
        out_shape=jax.ShapeDtypeStruct(blocks.shape, blocks.dtype),
        in_specs=[pl.BlockSpec(memory_space=pltpu.SMEM), whole],
        out_specs=whole,
        compiler_params=pltpu.CompilerParams(vmem_limit_bytes=VMEM_BYTES),
        name="reorder",
    )(order, blocks)


def gather_features(rows):
    parts = lax.axis_size("dp")
    if parts == 2:
        other = lax.ppermute(rows, "dp", ((0, 1), (1, 0)))
        first = lax.axis_index("dp") == 0
        return [jnp.where(first, rows, other), jnp.where(first, other, rows)]
    whole = lax.all_gather(rows, "dp", axis=0, tiled=False)
    return [whole[part] for part in range(parts)]


def scatter_sum(partial):
    parts = lax.axis_size("dp")
    if parts == 2:
        half = partial.shape[1] // 2
        low, high = partial[:, :half], partial[:, half:]
        first = lax.axis_index("dp") == 0
        keep, send = jnp.where(first, low, high), jnp.where(first, high, low)
        other = lax.ppermute(send, "dp", ((0, 1), (1, 0)))
        return (keep.astype(jnp.float32) + other.astype(jnp.float32)).astype(jnp.bfloat16)
    return lax.psum_scatter(partial, "dp", scatter_dimension=1, tiled=True)


def relocate_spread(arrays, source, experts):
    outputs = []
    for array in arrays:
        blocks = array.reshape(experts, array.shape[1] // experts, array.shape[2])
        outputs.append(exchange(reorder(exchange(blocks), source)).reshape(array.shape[1:]))
    return outputs


PLANES = 4
GROUP = 4
KINDS = (((0, 1), (1, 2), (2, 3)), ((0, 2), (2, 3)), ((0, 1), (1, 3)), ((0, 3),))
KIND_ROW, UP_ROW, DOWN_ROW, FINAL_ROW = 0, 4, 8, 12


def plan_kernel(where_ref, source_ref, plan_ref, ends_ref):
    plane = where_ref[0]
    member = where_ref[1]
    for index in range(PLANES):
        plan_ref[KIND_ROW + index] = 0
        plan_ref[UP_ROW + index] = GROUP
        plan_ref[DOWN_ROW + index] = GROUP
        ends_ref[index] = 0
    for slot in range(PLANES * GROUP):
        low = slot // GROUP
        other = source_ref[slot]
        high = other // GROUP
        offset = (slot % GROUP) ^ member

        @pl.when(jnp.logical_and(high == low, plane == low))
        def _():
            plan_ref[FINAL_ROW + offset] = (other % GROUP) ^ member

        @pl.when(high > low)
        def _():
            turn = jnp.int32(PLANES - 1)
            for index in reversed(range(PLANES - 1)):
                turn = jnp.where(ends_ref[index] <= low, index, turn)
            ends_ref[turn] = high
            span = high - low
            kind = jnp.where(span == 3, 4, jnp.where(span == 2, 2 + low, 1))
            plan_ref[KIND_ROW + turn] = jnp.maximum(plan_ref[KIND_ROW + turn], kind)

            @pl.when(plane == low)
            def _():
                plan_ref[UP_ROW + turn] = offset
                plan_ref[FINAL_ROW + offset] = GROUP + 2 * turn + 1

            @pl.when(plane == high)
            def _():
                there = (other % GROUP) ^ member
                plan_ref[DOWN_ROW + turn] = there
                plan_ref[FINAL_ROW + there] = GROUP + 2 * turn


def make_plan(source, plane, member):
    smem = pl.BlockSpec(memory_space=pltpu.SMEM)
    return pl.pallas_call(
        plan_kernel,
        out_shape=jax.ShapeDtypeStruct((16,), jnp.int32),
        in_specs=[smem, smem],
        out_specs=smem,
        scratch_shapes=[pltpu.SMEM((PLANES,), jnp.int32)],
        name="plan",
    )(jnp.stack([plane, member]), source)


def cut_kernel(member_ref, *refs):
    count = (len(refs) - 3) // (1 + GROUP)
    arrays, outs = refs[:count], refs[count:-3]
    staged, in_sems, out_sems = refs[-3:]
    rows = outs[0].shape[0]
    loads, stores = [], []
    for which, array in enumerate(arrays):
        for offset in (2, 3, 1, 0):
            begin = pl.multiple_of((member_ref[0] ^ offset) * rows, rows)
            place = which * GROUP + offset
            loads.append(
                pltpu.make_async_copy(
                    array.at[pl.ds(begin, rows)], staged.at[place], in_sems.at[place]
                )
            )
            stores.append(
                pltpu.make_async_copy(staged.at[place], outs[place], out_sems.at[place])
            )
    for load in loads:
        load.start()
    for load, store in zip(loads, stores):
        load.wait()
        store.start()
    for store in stores:
        store.wait()


def cut(arrays, member):
    rows, width = arrays[0].shape
    anywhere = pl.BlockSpec(memory_space=pltpu.HBM)
    piece = (rows // GROUP, width)
    amount = GROUP * len(arrays)
    pieces = pl.pallas_call(
        cut_kernel,
        out_shape=[jax.ShapeDtypeStruct(piece, arrays[0].dtype)] * amount,
        in_specs=[pl.BlockSpec(memory_space=pltpu.SMEM)] + [anywhere] * len(arrays),
        out_specs=[anywhere] * amount,
        scratch_shapes=[
            pltpu.VMEM((amount, *piece), arrays[0].dtype),
            pltpu.SemaphoreType.DMA((amount,)),
            pltpu.SemaphoreType.DMA((amount,)),
        ],
        compiler_params=pltpu.CompilerParams(vmem_limit_bytes=VMEM_BYTES),
        name="cut",
    )(member[None], *arrays)
    return [list(pieces[at : at + GROUP]) for at in range(0, amount, GROUP)]


def choose_kernel(count, choice_ref, *refs):
    options, outs = refs[:count], refs[count:-3]
    staged, in_sems, out_sems = refs[-3:]
    for place in range(len(outs)):
        for index, option in enumerate(options):

            @pl.when(choice_ref[place] == index)
            def _():
                pltpu.make_async_copy(option, staged.at[place], in_sems.at[place]).start()

    for place, out in enumerate(outs):

        @pl.when(choice_ref[place] < count)
        def _():
            pltpu.make_async_copy(options[0], staged.at[place], in_sems.at[place]).wait()
            pltpu.make_async_copy(staged.at[place], out, out_sems.at[place]).start()

    for place, out in enumerate(outs):

        @pl.when(choice_ref[place] < count)
        def _():
            pltpu.make_async_copy(staged.at[place], out, out_sems.at[place]).wait()


def choose(choice, options):
    anywhere = pl.BlockSpec(memory_space=pltpu.HBM)
    shape, dtype = options[0].shape, options[0].dtype
    amount = choice.shape[0]
    return pl.pallas_call(
        functools.partial(choose_kernel, len(options)),
        out_shape=[jax.ShapeDtypeStruct(shape, dtype)] * amount,
        in_specs=[pl.BlockSpec(memory_space=pltpu.SMEM)] + [anywhere] * len(options),
        out_specs=[anywhere] * amount,
        scratch_shapes=[
            pltpu.VMEM((amount, *shape), dtype),
            pltpu.SemaphoreType.DMA((amount,)),
            pltpu.SemaphoreType.DMA((amount,)),
        ],
        compiler_params=pltpu.CompilerParams(vmem_limit_bytes=VMEM_BYTES),
        name="choose",
    )(choice, *options)


def within_plane(offset):
    return [(index, index ^ offset) for index in range(PLANES * GROUP)]


def between_planes(moves):
    return [(GROUP * a + index, GROUP * b + index) for a, b in moves for index in range(GROUP)]


def swap_round(kind, up, down):
    if kind == 0:
        return up, down
    moves = KINDS[kind - 1]
    return (
        lax.ppermute(up, "expert", between_planes(moves)),
        lax.ppermute(down, "expert", between_planes([(b, a) for a, b in moves])),
    )


def swap_rounds(first_kind, second_kind):
    def run(first_up, first_down, second_up, second_down):
        return (
            *swap_round(first_kind, first_up, first_down),
            *swap_round(second_kind, second_up, second_down),
        )

    return run


def hand_over(pieces):
    moved = {
        offset: lax.ppermute(pieces[offset], "expert", within_plane(offset))
        for offset in reversed(range(1, GROUP))
    }
    return [pieces[0]] + [moved[offset] for offset in range(1, GROUP)]


def swap_one(turn, plan, ways):
    return list(
        lax.switch(
            plan[KIND_ROW + turn],
            [functools.partial(swap_round, kind) for kind in range(len(KINDS) + 1)],
            ways[turn],
            ways[PLANES + turn],
        )
    )


def swap_two(plan, ways):
    first, second = plan[KIND_ROW], plan[KIND_ROW + 1]
    amount = len(KINDS) + 1
    branches = [swap_rounds(0, 0)] + [
        swap_rounds(a, b) for a in range(1, amount) for b in range(amount)
    ]
    return list(
        lax.switch(
            jnp.where(first == 0, 0, 1 + (first - 1) * amount + second),
            branches,
            ways[0],
            ways[PLANES],
            ways[1],
            ways[PLANES + 1],
        )
    )


def join_quarters(own):
    member = lax.axis_index("expert") % GROUP
    for bit in (1, 2):
        swap = (member & bit) != 0
        own = [jnp.where(swap, own[offset ^ bit], own[offset]) for offset in range(GROUP)]
    return jnp.concatenate(own, axis=0)


def per_device(
    tokens, cotangent, routes, gates, source, w_gate_up, w_down, moment_first, moment_second
):
    experts = lax.axis_size("expert")
    micro_count, token_count, part_width = tokens.shape
    model_width = w_gate_up.shape[1]
    hidden_part = w_gate_up.shape[3]
    top_count = routes.shape[2]
    capacity = max(2, 3 * token_count * top_count // (2 * experts))
    per_expert = micro_count * capacity
    slots = experts * per_expert
    all_tokens = micro_count * token_count
    swaps = experts == PLANES * GROUP

    pairs = token_count * top_count
    chosen = routes.reshape(micro_count, pairs)
    same = chosen[:, :, None] == chosen[:, None, :]
    order = jnp.arange(pairs, dtype=jnp.int32)
    earlier = order[None, :] < order[:, None]
    position = jnp.sum((same & earlier).astype(jnp.int32), axis=2)
    micro_ids = jnp.arange(micro_count, dtype=jnp.int32)[:, None]
    place = (chosen * per_expert + micro_ids * capacity + position).reshape(all_tokens, top_count)
    slot_ids = jnp.arange(slots, dtype=jnp.int32)
    flat_gates = gates.reshape(all_tokens, top_count)
    matches = [place[:, k][:, None] == slot_ids for k in range(top_count)]
    picks = [match.astype(jnp.bfloat16) for match in matches]
    plain = sum(picks[1:], picks[0])
    slot_gate = sum(
        jnp.sum(jnp.where(matches[k], flat_gates[:, k : k + 1], 0.0), axis=0)
        for k in range(top_count)
    )

    row_tokens = lax.dot_general(
        plain,
        tokens.reshape(all_tokens, part_width),
        contract_first,
        preferred_element_type=jnp.float32,
    ).astype(jnp.bfloat16)
    if swaps:
        index = lax.axis_index("expert")
        plane, member = index // GROUP, index % GROUP
        plan = make_plan(source, plane, member)
        row_tokens, (pieces_a, pieces_b) = fence(
            row_tokens, cut((moment_first[0], moment_second[0]), member)
        )
        held_a = hand_over(pieces_a)
    here_tokens = exchange(row_tokens.reshape(experts, per_expert, part_width))
    row_grads = (
        lax.dot_general(
            plain,
            cotangent.reshape(all_tokens, part_width),
            contract_first,
            preferred_element_type=jnp.float32,
        )
        * slot_gate[:, None]
    ).astype(jnp.bfloat16)
    gate_up = w_gate_up.reshape(model_width, 2 * hidden_part)
    down = w_down.reshape(hidden_part, model_width)

    if swaps:
        here_tokens, row_grads, gate_up, held_a, pieces_b, plan = fence(
            here_tokens, row_grads, gate_up, held_a, pieces_b, plan
        )
        held_b = hand_over(pieces_b)
        ways_a = choose(plan[UP_ROW:FINAL_ROW], held_a)
        arrived_a = swap_two(plan, ways_a)
    grad_blocks = row_grads.reshape(experts, per_expert, part_width)
    here_grads = exchange(grad_blocks)
    expert_in = jnp.concatenate(gather_features(here_tokens.reshape(slots, part_width)), axis=1)
    if swaps:
        expert_in, here_grads, arrived_a, held_b = fence(
            expert_in, here_grads, arrived_a, held_b
        )
    both = jnp.dot(expert_in, gate_up, preferred_element_type=jnp.float32)
    gate_pre = both[:, :hidden_part]
    up_pre = both[:, hidden_part:]
    gate_sig = jax.nn.sigmoid(gate_pre)
    hidden = (gate_pre * gate_sig * up_pre).astype(jnp.bfloat16)
    partial_out = jnp.dot(hidden, down, preferred_element_type=jnp.float32).astype(jnp.bfloat16)

    if swaps:
        hidden, partial_out, ways_a, held_b = fence(hidden, partial_out, ways_a, held_b)
        arrived_a += swap_one(2, plan, ways_a) + swap_one(3, plan, ways_a)
        ways_b = choose(plan[UP_ROW:FINAL_ROW], held_b)
        arrived_b = swap_two(plan, ways_b)
    summed_out = scatter_sum(partial_out)

    if swaps:
        summed_out, here_grads, arrived_a, arrived_b, ways_b = fence(
            summed_out, here_grads, arrived_a, arrived_b, ways_b
        )
        own_a = hand_over(choose(plan[FINAL_ROW:], [*held_a, *arrived_a]))
        arrived_b += swap_one(2, plan, ways_b) + swap_one(3, plan, ways_b)
        ready_b = choose(plan[FINAL_ROW:], [*held_b, *arrived_b])
    back = exchange(
        jnp.concatenate([summed_out, hidden], axis=1).reshape(experts, per_expert, -1)
    )
    grad_in = jnp.concatenate(gather_features(here_grads.reshape(slots, part_width)), axis=1)
    hidden_grad = lax.dot_general(
        grad_in, down, contract_second, preferred_element_type=jnp.float32
    )
    gate_grad = hidden_grad * up_pre * gate_sig * (1.0 + gate_pre * (1.0 - gate_sig))
    up_grad = hidden_grad * gate_pre * gate_sig
    both_grad = jnp.concatenate([gate_grad, up_grad], axis=1).astype(jnp.bfloat16)
    partial_in = lax.dot_general(
        both_grad, gate_up, contract_second, preferred_element_type=jnp.float32
    ).astype(jnp.bfloat16)
    to_move = reorder(jnp.concatenate([back[:, :, part_width:], grad_blocks], axis=2), source)

    if swaps:
        to_move, partial_in, own_a, ready_b = fence(to_move, partial_in, own_a, ready_b)
        own_b = hand_over(ready_b)
    there = exchange(to_move).reshape(slots, hidden_part + part_width)
    summed_in = scatter_sum(partial_in)
    back_out = back[:, :, :part_width].reshape(slots, part_width)
    layer_out = sum(
        flat_gates[:, k : k + 1] * jnp.dot(picks[k], back_out, preferred_element_type=jnp.float32)
        for k in range(top_count)
    ).astype(jnp.bfloat16)

    if swaps:
        there, summed_in, own_b, layer_out = fence(there, summed_in, own_b, layer_out)
    back_in = exchange(summed_in.reshape(experts, per_expert, part_width))
    token_grad = jnp.dot(
        plain, back_in.reshape(slots, part_width), preferred_element_type=jnp.float32
    )

    there_hidden = there[:, :hidden_part]
    there_grads = jnp.concatenate(gather_features(there[:, hidden_part:]), axis=1)
    if swaps:
        old_first, old_second = join_quarters(own_a), join_quarters(own_b)
    else:
        old_first, old_second = relocate_spread((moment_first, moment_second), source, experts)
    down_grad = lax.dot_general(
        there_hidden, there_grads, contract_first, preferred_element_type=jnp.float32
    )
    first = 0.9 * old_first.astype(jnp.float32) + 0.1 * down_grad
    second = 0.999 * old_second.astype(jnp.float32) + 0.001 * down_grad * down_grad
    update = first / (jnp.sqrt(second) + 1e-08)
    shape = moment_first.shape
    return (
        layer_out.reshape(tokens.shape),
        token_grad.astype(jnp.bfloat16).reshape(tokens.shape),
        update.astype(jnp.bfloat16).reshape(shape),
        first.astype(jnp.bfloat16).reshape(shape),
        second.astype(jnp.bfloat16).reshape(shape),
    )


def solution(mesh):
    placed = (
        P(None, "expert", "dp"),
        P(None, "expert", "dp"),
        P(None, "expert", None),
        P(None, "expert", None),
        P(),
        P("expert", None, None, "dp"),
        P("expert", "dp", None),
        P("expert", "dp", None),
        P("expert", "dp", None),
    )
    return jax.shard_map(
        per_device,
        mesh=mesh,
        in_specs=placed,
        out_specs=(
            P(None, "expert", "dp"),
            P(None, "expert", "dp"),
            P("expert", "dp", None),
            P("expert", "dp", None),
            P("expert", "dp", None),
        ),
        check_vma=False,
    )
```

```python
import functools

import jax
import jax.numpy as jnp
from jax import lax
from jax.experimental import pallas as pl
from jax.experimental.pallas import tpu as pltpu
from jax.sharding import PartitionSpec as P

contract_first = (((0,), (0,)), ((), ()))
contract_second = (((1,), (1,)), ((), ()))
VMEM_BYTES = 32 * 1024 * 1024


def fence(*values):
    return lax.optimization_barrier(values)


def exchange(blocks):
    return lax.all_to_all(blocks, "expert", split_axis=0, concat_axis=0, tiled=True)


def reorder_kernel(order_ref, blocks_ref, out_ref):
    for place in range(out_ref.shape[0]):
        out_ref[place] = blocks_ref[order_ref[place]]


def reorder(blocks, order):
    whole = pl.BlockSpec(memory_space=pltpu.VMEM)
    return pl.pallas_call(
        reorder_kernel,
        out_shape=jax.ShapeDtypeStruct(blocks.shape, blocks.dtype),
        in_specs=[pl.BlockSpec(memory_space=pltpu.SMEM), whole],
        out_specs=whole,
        compiler_params=pltpu.CompilerParams(vmem_limit_bytes=VMEM_BYTES),
        name="reorder",
    )(order, blocks)


def gather_features(rows):
    parts = lax.axis_size("dp")
    if parts == 2:
        other = lax.ppermute(rows, "dp", ((0, 1), (1, 0)))
        first = lax.axis_index("dp") == 0
        return [jnp.where(first, rows, other), jnp.where(first, other, rows)]
    whole = lax.all_gather(rows, "dp", axis=0, tiled=False)
    return [whole[part] for part in range(parts)]


def scatter_sum(partial):
    parts = lax.axis_size("dp")
    if parts == 2:
        half = partial.shape[1] // 2
        low, high = partial[:, :half], partial[:, half:]
        first = lax.axis_index("dp") == 0
        keep, send = jnp.where(first, low, high), jnp.where(first, high, low)
        other = lax.ppermute(send, "dp", ((0, 1), (1, 0)))
        return (keep.astype(jnp.float32) + other.astype(jnp.float32)).astype(jnp.bfloat16)
    return lax.psum_scatter(partial, "dp", scatter_dimension=1, tiled=True)


def relocate_spread(arrays, source, experts):
    outputs = []
    for array in arrays:
        blocks = array.reshape(experts, array.shape[1] // experts, array.shape[2])
        outputs.append(exchange(reorder(exchange(blocks), source)).reshape(array.shape[1:]))
    return outputs


PLANES = 4
GROUP = 4
KINDS = (((0, 1), (1, 2), (2, 3)), ((0, 2), (2, 3)), ((0, 1), (1, 3)), ((0, 3),))
KIND_ROW, UP_ROW, DOWN_ROW, FINAL_ROW = 0, 4, 8, 12


def plan_kernel(where_ref, source_ref, plan_ref, ends_ref):
    plane = where_ref[0]
    member = where_ref[1]
    for index in range(PLANES):
        plan_ref[KIND_ROW + index] = 0
        plan_ref[UP_ROW + index] = GROUP
        plan_ref[DOWN_ROW + index] = GROUP
        ends_ref[index] = 0
    for slot in range(PLANES * GROUP):
        low = slot // GROUP
        other = source_ref[slot]
        high = other // GROUP
        offset = (slot % GROUP) ^ member

        @pl.when(jnp.logical_and(high == low, plane == low))
        def _():
            plan_ref[FINAL_ROW + offset] = (other % GROUP) ^ member

        @pl.when(high > low)
        def _():
            turn = jnp.int32(PLANES - 1)
            for index in reversed(range(PLANES - 1)):
                turn = jnp.where(ends_ref[index] <= low, index, turn)
            ends_ref[turn] = high
            span = high - low
            kind = jnp.where(span == 3, 4, jnp.where(span == 2, 2 + low, 1))
            plan_ref[KIND_ROW + turn] = jnp.maximum(plan_ref[KIND_ROW + turn], kind)

            @pl.when(plane == low)
            def _():
                plan_ref[UP_ROW + turn] = offset
                plan_ref[FINAL_ROW + offset] = GROUP + 2 * turn + 1

            @pl.when(plane == high)
            def _():
                there = (other % GROUP) ^ member
                plan_ref[DOWN_ROW + turn] = there
                plan_ref[FINAL_ROW + there] = GROUP + 2 * turn


def make_plan(source, plane, member):
    smem = pl.BlockSpec(memory_space=pltpu.SMEM)
    return pl.pallas_call(
        plan_kernel,
        out_shape=jax.ShapeDtypeStruct((16,), jnp.int32),
        in_specs=[smem, smem],
        out_specs=smem,
        scratch_shapes=[pltpu.SMEM((PLANES,), jnp.int32)],
        name="plan",
    )(jnp.stack([plane, member]), source)


def cut_kernel(member_ref, *refs):
    count = (len(refs) - 3) // (1 + GROUP)
    arrays, outs = refs[:count], refs[count:-3]
    staged, in_sems, out_sems = refs[-3:]
    rows = outs[0].shape[0]
    loads, stores = [], []
    for which, array in enumerate(arrays):
        for offset in (2, 3, 1, 0):
            begin = pl.multiple_of((member_ref[0] ^ offset) * rows, rows)
            place = which * GROUP + offset
            loads.append(
                pltpu.make_async_copy(
                    array.at[pl.ds(begin, rows)], staged.at[place], in_sems.at[place]
                )
            )
            stores.append(
                pltpu.make_async_copy(staged.at[place], outs[place], out_sems.at[place])
            )
    for load in loads:
        load.start()
    for load, store in zip(loads, stores):
        load.wait()
        store.start()
    for store in stores:
        store.wait()


def cut(arrays, member):
    rows, width = arrays[0].shape
    anywhere = pl.BlockSpec(memory_space=pltpu.HBM)
    piece = (rows // GROUP, width)
    amount = GROUP * len(arrays)
    pieces = pl.pallas_call(
        cut_kernel,
        out_shape=[jax.ShapeDtypeStruct(piece, arrays[0].dtype)] * amount,
        in_specs=[pl.BlockSpec(memory_space=pltpu.SMEM)] + [anywhere] * len(arrays),
        out_specs=[anywhere] * amount,
        scratch_shapes=[
            pltpu.VMEM((amount, *piece), arrays[0].dtype),
            pltpu.SemaphoreType.DMA((amount,)),
            pltpu.SemaphoreType.DMA((amount,)),
        ],
        compiler_params=pltpu.CompilerParams(vmem_limit_bytes=VMEM_BYTES),
        name="cut",
    )(member[None], *arrays)
    return [list(pieces[at : at + GROUP]) for at in range(0, amount, GROUP)]


def choose_kernel(count, choice_ref, *refs):
    options, outs = refs[:count], refs[count:-3]
    staged, in_sems, out_sems = refs[-3:]
    for place in range(len(outs)):
        for index, option in enumerate(options):

            @pl.when(choice_ref[place] == index)
            def _():
                pltpu.make_async_copy(option, staged.at[place], in_sems.at[place]).start()

    for place, out in enumerate(outs):

        @pl.when(choice_ref[place] < count)
        def _():
            pltpu.make_async_copy(options[0], staged.at[place], in_sems.at[place]).wait()
            pltpu.make_async_copy(staged.at[place], out, out_sems.at[place]).start()

    for place, out in enumerate(outs):

        @pl.when(choice_ref[place] < count)
        def _():
            pltpu.make_async_copy(staged.at[place], out, out_sems.at[place]).wait()


def choose(choice, options):
    anywhere = pl.BlockSpec(memory_space=pltpu.HBM)
    shape, dtype = options[0].shape, options[0].dtype
    amount = choice.shape[0]
    return pl.pallas_call(
        functools.partial(choose_kernel, len(options)),
        out_shape=[jax.ShapeDtypeStruct(shape, dtype)] * amount,
        in_specs=[pl.BlockSpec(memory_space=pltpu.SMEM)] + [anywhere] * len(options),
        out_specs=[anywhere] * amount,
        scratch_shapes=[
            pltpu.VMEM((amount, *shape), dtype),
            pltpu.SemaphoreType.DMA((amount,)),
            pltpu.SemaphoreType.DMA((amount,)),
        ],
        compiler_params=pltpu.CompilerParams(vmem_limit_bytes=VMEM_BYTES),
        name="choose",
    )(choice, *options)


def within_plane(offset):
    return [(index, index ^ offset) for index in range(PLANES * GROUP)]


def between_planes(moves):
    return [(GROUP * a + index, GROUP * b + index) for a, b in moves for index in range(GROUP)]


def swap_round(kind, up, down):
    if kind == 0:
        return up, down
    moves = KINDS[kind - 1]
    return (
        lax.ppermute(up, "expert", between_planes(moves)),
        lax.ppermute(down, "expert", between_planes([(b, a) for a, b in moves])),
    )


def hand_over(pieces, offsets):
    return [lax.ppermute(pieces[offset], "expert", within_plane(offset)) for offset in offsets]


OFFSETS = (3, 2, 1)


def in_order(own, moved):
    third, second, first = moved
    return [own, first, second, third]


def swap_one(turn, plan, ways):
    return list(
        lax.switch(
            plan[KIND_ROW + turn],
            [functools.partial(swap_round, kind) for kind in range(len(KINDS) + 1)],
            ways[turn],
            ways[PLANES + turn],
        )
    )


def swap_two(plan, ways, pieces):
    first, second = plan[KIND_ROW], plan[KIND_ROW + 1]
    amount = len(KINDS) + 1

    def branch(first_kind, second_kind):
        def run(ways, pieces):
            return (
                hand_over(pieces, OFFSETS),
                swap_round(first_kind, ways[0], ways[PLANES]),
                swap_round(second_kind, ways[1], ways[PLANES + 1]),
            )

        return run

    moved, arrived, more = lax.switch(
        jnp.where(first == 0, 0, 1 + (first - 1) * amount + second),
        [branch(0, 0)] + [branch(a, b) for a in range(1, amount) for b in range(amount)],
        tuple(ways),
        tuple(pieces),
    )
    return [*arrived, *more], in_order(pieces[0], moved)


def join_quarters(own):
    member = lax.axis_index("expert") % GROUP
    for bit in (1, 2):
        swap = (member & bit) != 0
        own = [jnp.where(swap, own[offset ^ bit], own[offset]) for offset in range(GROUP)]
    return jnp.concatenate(own, axis=0)


def per_device(
    tokens, cotangent, routes, gates, source, w_gate_up, w_down, moment_first, moment_second
):
    experts = lax.axis_size("expert")
    micro_count, token_count, part_width = tokens.shape
    model_width = w_gate_up.shape[1]
    hidden_part = w_gate_up.shape[3]
    top_count = routes.shape[2]
    capacity = max(2, 3 * token_count * top_count // (2 * experts))
    per_expert = micro_count * capacity
    slots = experts * per_expert
    all_tokens = micro_count * token_count
    swaps = experts == PLANES * GROUP

    pairs = token_count * top_count
    chosen = routes.reshape(micro_count, pairs)
    same = chosen[:, :, None] == chosen[:, None, :]
    order = jnp.arange(pairs, dtype=jnp.int32)
    earlier = order[None, :] < order[:, None]
    position = jnp.sum((same & earlier).astype(jnp.int32), axis=2)
    micro_ids = jnp.arange(micro_count, dtype=jnp.int32)[:, None]
    place = (chosen * per_expert + micro_ids * capacity + position).reshape(all_tokens, top_count)
    slot_ids = jnp.arange(slots, dtype=jnp.int32)
    flat_gates = gates.reshape(all_tokens, top_count)
    matches = [place[:, k][:, None] == slot_ids for k in range(top_count)]
    picks = [match.astype(jnp.bfloat16) for match in matches]
    plain = sum(picks[1:], picks[0])
    slot_gate = sum(
        jnp.sum(jnp.where(matches[k], flat_gates[:, k : k + 1], 0.0), axis=0)
        for k in range(top_count)
    )

    row_tokens = lax.dot_general(
        plain,
        tokens.reshape(all_tokens, part_width),
        contract_first,
        preferred_element_type=jnp.float32,
    ).astype(jnp.bfloat16)
    if swaps:
        index = lax.axis_index("expert")
        plane, member = index // GROUP, index % GROUP
        plan = make_plan(source, plane, member)
        row_tokens, (pieces_a, pieces_b) = fence(
            row_tokens, cut((moment_first[0], moment_second[0]), member)
        )
        held_a = in_order(pieces_a[0], hand_over(pieces_a, OFFSETS))
    here_tokens = exchange(row_tokens.reshape(experts, per_expert, part_width))
    row_grads = (
        lax.dot_general(
            plain,
            cotangent.reshape(all_tokens, part_width),
            contract_first,
            preferred_element_type=jnp.float32,
        )
        * slot_gate[:, None]
    ).astype(jnp.bfloat16)
    gate_up = w_gate_up.reshape(model_width, 2 * hidden_part)
    down = w_down.reshape(hidden_part, model_width)

    if swaps:
        here_tokens, row_grads, gate_up, held_a, pieces_b, plan = fence(
            here_tokens, row_grads, gate_up, held_a, pieces_b, plan
        )
        ways_a = choose(plan[UP_ROW:FINAL_ROW], held_a)
        arrived_a, held_b = swap_two(plan, ways_a, pieces_b)
    grad_blocks = row_grads.reshape(experts, per_expert, part_width)
    here_grads = exchange(grad_blocks)
    expert_in = jnp.concatenate(gather_features(here_tokens.reshape(slots, part_width)), axis=1)
    if swaps:
        expert_in, here_grads, arrived_a, held_b = fence(
            expert_in, here_grads, arrived_a, held_b
        )
    both = jnp.dot(expert_in, gate_up, preferred_element_type=jnp.float32)
    gate_pre = both[:, :hidden_part]
    up_pre = both[:, hidden_part:]
    gate_sig = jax.nn.sigmoid(gate_pre)
    hidden = (gate_pre * gate_sig * up_pre).astype(jnp.bfloat16)
    partial_out = jnp.dot(hidden, down, preferred_element_type=jnp.float32).astype(jnp.bfloat16)

    if swaps:
        hidden, partial_out, ways_a, held_b = fence(hidden, partial_out, ways_a, held_b)
        arrived_a += swap_one(2, plan, ways_a) + swap_one(3, plan, ways_a)
        ready_a = choose(plan[FINAL_ROW:], [*held_a, *arrived_a])
        ways_b = choose(plan[UP_ROW:FINAL_ROW], held_b)
        arrived_b, own_a = swap_two(plan, ways_b, ready_a)
    summed_out = scatter_sum(partial_out)

    if swaps:
        summed_out, here_grads, arrived_b, own_a, ways_b = fence(
            summed_out, here_grads, arrived_b, own_a, ways_b
        )
        arrived_b += swap_one(2, plan, ways_b) + swap_one(3, plan, ways_b)
        ready_b = choose(plan[FINAL_ROW:], [*held_b, *arrived_b])
    back = exchange(
        jnp.concatenate([summed_out, hidden], axis=1).reshape(experts, per_expert, -1)
    )
    grad_in = jnp.concatenate(gather_features(here_grads.reshape(slots, part_width)), axis=1)
    hidden_grad = lax.dot_general(
        grad_in, down, contract_second, preferred_element_type=jnp.float32
    )
    gate_grad = hidden_grad * up_pre * gate_sig * (1.0 + gate_pre * (1.0 - gate_sig))
    up_grad = hidden_grad * gate_pre * gate_sig
    both_grad = jnp.concatenate([gate_grad, up_grad], axis=1).astype(jnp.bfloat16)
    partial_in = lax.dot_general(
        both_grad, gate_up, contract_second, preferred_element_type=jnp.float32
    ).astype(jnp.bfloat16)
    to_move = reorder(jnp.concatenate([back[:, :, part_width:], grad_blocks], axis=2), source)

    if swaps:
        to_move, partial_in, own_a, ready_b = fence(to_move, partial_in, own_a, ready_b)
        moved = hand_over(ready_b, OFFSETS[:1])
    there = exchange(to_move).reshape(slots, hidden_part + part_width)
    summed_in = scatter_sum(partial_in)
    back_out = back[:, :, :part_width].reshape(slots, part_width)
    layer_out = sum(
        flat_gates[:, k : k + 1] * jnp.dot(picks[k], back_out, preferred_element_type=jnp.float32)
        for k in range(top_count)
    ).astype(jnp.bfloat16)

    if swaps:
        there, summed_in, moved, layer_out, ready_b = fence(
            there, summed_in, moved, layer_out, ready_b
        )
        own_b = in_order(ready_b[0], moved + hand_over(ready_b, OFFSETS[1:]))
    back_in = exchange(summed_in.reshape(experts, per_expert, part_width))
    token_grad = jnp.dot(
        plain, back_in.reshape(slots, part_width), preferred_element_type=jnp.float32
    )

    there_hidden = there[:, :hidden_part]
    there_grads = jnp.concatenate(gather_features(there[:, hidden_part:]), axis=1)
    if swaps:
        old_first, old_second = join_quarters(own_a), join_quarters(own_b)
    else:
        old_first, old_second = relocate_spread((moment_first, moment_second), source, experts)
    down_grad = lax.dot_general(
        there_hidden, there_grads, contract_first, preferred_element_type=jnp.float32
    )
    first = 0.9 * old_first.astype(jnp.float32) + 0.1 * down_grad
    second = 0.999 * old_second.astype(jnp.float32) + 0.001 * down_grad * down_grad
    update = first / (jnp.sqrt(second) + 1e-08)
    shape = moment_first.shape
    return (
        layer_out.reshape(tokens.shape),
        token_grad.astype(jnp.bfloat16).reshape(tokens.shape),
        update.astype(jnp.bfloat16).reshape(shape),
        first.astype(jnp.bfloat16).reshape(shape),
        second.astype(jnp.bfloat16).reshape(shape),
    )


def solution(mesh):
    placed = (
        P(None, "expert", "dp"),
        P(None, "expert", "dp"),
        P(None, "expert", None),
        P(None, "expert", None),
        P(),
        P("expert", None, None, "dp"),
        P("expert", "dp", None),
        P("expert", "dp", None),
        P("expert", "dp", None),
    )
    return jax.shard_map(
        per_device,
        mesh=mesh,
        in_specs=placed,
        out_specs=(
            P(None, "expert", "dp"),
            P(None, "expert", "dp"),
            P("expert", "dp", None),
            P("expert", "dp", None),
            P("expert", "dp", None),
        ),
        check_vma=False,
    )
```

```python
import functools

import jax
import jax.numpy as jnp
from jax import lax
from jax.experimental import pallas as pl
from jax.experimental.pallas import tpu as pltpu
from jax.sharding import PartitionSpec as P

contract_first = (((0,), (0,)), ((), ()))
contract_second = (((1,), (1,)), ((), ()))
VMEM_BYTES = 32 * 1024 * 1024
MOST_VMEM_BYTES = 60 * 1024 * 1024


def fence(*values):
    return lax.optimization_barrier(values)


def exchange(blocks):
    return lax.all_to_all(blocks, "expert", split_axis=0, concat_axis=0, tiled=True)


def reorder_kernel(order_ref, blocks_ref, out_ref):
    for place in range(out_ref.shape[0]):
        out_ref[place] = blocks_ref[order_ref[place]]


def reorder(blocks, order):
    whole = pl.BlockSpec(memory_space=pltpu.VMEM)
    return pl.pallas_call(
        reorder_kernel,
        out_shape=jax.ShapeDtypeStruct(blocks.shape, blocks.dtype),
        in_specs=[pl.BlockSpec(memory_space=pltpu.SMEM), whole],
        out_specs=whole,
        compiler_params=pltpu.CompilerParams(vmem_limit_bytes=VMEM_BYTES),
        name="reorder",
    )(order, blocks)


def gather_features(rows):
    parts = lax.axis_size("dp")
    if parts == 2:
        other = lax.ppermute(rows, "dp", ((0, 1), (1, 0)))
        first = lax.axis_index("dp") == 0
        return [jnp.where(first, rows, other), jnp.where(first, other, rows)]
    whole = lax.all_gather(rows, "dp", axis=0, tiled=False)
    return [whole[part] for part in range(parts)]


def scatter_sum(partial):
    parts = lax.axis_size("dp")
    if parts == 2:
        half = partial.shape[1] // 2
        low, high = partial[:, :half], partial[:, half:]
        first = lax.axis_index("dp") == 0
        keep, send = jnp.where(first, low, high), jnp.where(first, high, low)
        other = lax.ppermute(send, "dp", ((0, 1), (1, 0)))
        return (keep.astype(jnp.float32) + other.astype(jnp.float32)).astype(jnp.bfloat16)
    return lax.psum_scatter(partial, "dp", scatter_dimension=1, tiled=True)


def relocate_spread(arrays, source, experts):
    outputs = []
    for array in arrays:
        blocks = array.reshape(experts, array.shape[1] // experts, array.shape[2])
        outputs.append(exchange(reorder(exchange(blocks), source)).reshape(array.shape[1:]))
    return outputs


PLANES = 4
GROUP = 4
KINDS = (((0, 1), (1, 2), (2, 3)), ((0, 2), (2, 3)), ((0, 1), (1, 3)), ((0, 3),))
KIND_ROW, UP_ROW, DOWN_ROW, FINAL_ROW = 0, 4, 8, 12


def plan_kernel(where_ref, source_ref, plan_ref, ends_ref):
    plane = where_ref[0]
    member = where_ref[1]
    for index in range(PLANES):
        plan_ref[KIND_ROW + index] = 0
        plan_ref[UP_ROW + index] = GROUP
        plan_ref[DOWN_ROW + index] = GROUP
        ends_ref[index] = 0
    for slot in range(PLANES * GROUP):
        low = slot // GROUP
        other = source_ref[slot]
        high = other // GROUP
        offset = (slot % GROUP) ^ member

        @pl.when(jnp.logical_and(high == low, plane == low))
        def _():
            plan_ref[FINAL_ROW + offset] = (other % GROUP) ^ member

        @pl.when(high > low)
        def _():
            turn = jnp.int32(PLANES - 1)
            for index in reversed(range(PLANES - 1)):
                turn = jnp.where(ends_ref[index] <= low, index, turn)
            ends_ref[turn] = high
            span = high - low
            kind = jnp.where(span == 3, 4, jnp.where(span == 2, 2 + low, 1))
            plan_ref[KIND_ROW + turn] = jnp.maximum(plan_ref[KIND_ROW + turn], kind)

            @pl.when(plane == low)
            def _():
                plan_ref[UP_ROW + turn] = offset
                plan_ref[FINAL_ROW + offset] = GROUP + 2 * turn + 1

            @pl.when(plane == high)
            def _():
                there = (other % GROUP) ^ member
                plan_ref[DOWN_ROW + turn] = there
                plan_ref[FINAL_ROW + there] = GROUP + 2 * turn


def make_plan(source, plane, member):
    smem = pl.BlockSpec(memory_space=pltpu.SMEM)
    return pl.pallas_call(
        plan_kernel,
        out_shape=jax.ShapeDtypeStruct((16,), jnp.int32),
        in_specs=[smem, smem],
        out_specs=smem,
        scratch_shapes=[pltpu.SMEM((PLANES,), jnp.int32)],
        name="plan",
    )(jnp.stack([plane, member]), source)


def cut_kernel(member_ref, *refs):
    count = (len(refs) - 3) // (1 + GROUP)
    arrays, outs = refs[:count], refs[count:-3]
    staged, in_sems, out_sems = refs[-3:]
    rows = outs[0].shape[0]
    loads, stores = [], []
    for which, array in enumerate(arrays):
        for offset in (2, 3, 1, 0):
            begin = pl.multiple_of((member_ref[0] ^ offset) * rows, rows)
            place = which * GROUP + offset
            loads.append(
                pltpu.make_async_copy(
                    array.at[pl.ds(begin, rows)], staged.at[place], in_sems.at[place]
                )
            )
            stores.append(
                pltpu.make_async_copy(staged.at[place], outs[place], out_sems.at[place])
            )
    for load in loads:
        load.start()
    for load, store in zip(loads, stores):
        load.wait()
        store.start()
    for store in stores:
        store.wait()


def cut(arrays, member):
    rows, width = arrays[0].shape
    anywhere = pl.BlockSpec(memory_space=pltpu.HBM)
    piece = (rows // GROUP, width)
    amount = GROUP * len(arrays)
    pieces = pl.pallas_call(
        cut_kernel,
        out_shape=[jax.ShapeDtypeStruct(piece, arrays[0].dtype)] * amount,
        in_specs=[pl.BlockSpec(memory_space=pltpu.SMEM)] + [anywhere] * len(arrays),
        out_specs=[anywhere] * amount,
        scratch_shapes=[
            pltpu.VMEM((amount, *piece), arrays[0].dtype),
            pltpu.SemaphoreType.DMA((amount,)),
            pltpu.SemaphoreType.DMA((amount,)),
        ],
        compiler_params=pltpu.CompilerParams(vmem_limit_bytes=MOST_VMEM_BYTES),
        name="cut",
    )(member[None], *arrays)
    return [list(pieces[at : at + GROUP]) for at in range(0, amount, GROUP)]


def choose_kernel(count, choice_ref, *refs):
    options, outs = refs[:count], refs[count:-3]
    staged, in_sems, out_sems = refs[-3:]
    for place in range(len(outs)):
        for index, option in enumerate(options):

            @pl.when(choice_ref[place] == index)
            def _():
                pltpu.make_async_copy(option, staged.at[place], in_sems.at[place]).start()

    for place, out in enumerate(outs):

        @pl.when(choice_ref[place] < count)
        def _():
            pltpu.make_async_copy(options[0], staged.at[place], in_sems.at[place]).wait()
            pltpu.make_async_copy(staged.at[place], out, out_sems.at[place]).start()

    for place, out in enumerate(outs):

        @pl.when(choice_ref[place] < count)
        def _():
            pltpu.make_async_copy(staged.at[place], out, out_sems.at[place]).wait()


def choose(choice, options):
    anywhere = pl.BlockSpec(memory_space=pltpu.HBM)
    shape, dtype = options[0].shape, options[0].dtype
    amount = choice.shape[0]
    return pl.pallas_call(
        functools.partial(choose_kernel, len(options)),
        out_shape=[jax.ShapeDtypeStruct(shape, dtype)] * amount,
        in_specs=[pl.BlockSpec(memory_space=pltpu.SMEM)] + [anywhere] * len(options),
        out_specs=[anywhere] * amount,
        scratch_shapes=[
            pltpu.VMEM((amount, *shape), dtype),
            pltpu.SemaphoreType.DMA((amount,)),
            pltpu.SemaphoreType.DMA((amount,)),
        ],
        compiler_params=pltpu.CompilerParams(vmem_limit_bytes=MOST_VMEM_BYTES),
        name="choose",
    )(choice, *options)


def within_plane(offset):
    return [(index, index ^ offset) for index in range(PLANES * GROUP)]


def between_planes(moves):
    return [(GROUP * a + index, GROUP * b + index) for a, b in moves for index in range(GROUP)]


def swap_round(kind, up, down):
    if kind == 0:
        return up, down
    moves = KINDS[kind - 1]
    return (
        lax.ppermute(up, "expert", between_planes(moves)),
        lax.ppermute(down, "expert", between_planes([(b, a) for a, b in moves])),
    )


def step(first, second, offset):
    moved = lax.ppermute(jnp.stack([first, second]), "expert", within_plane(offset))
    return moved[0], moved[1]


def hand_over(pieces):
    moved = [
        lax.ppermute(pieces[offset], "expert", within_plane(offset))
        for offset in reversed(range(1, GROUP))
    ]
    return [pieces[0], *reversed(moved)]


def swap(turn, plan, ways):
    return list(
        lax.switch(
            plan[KIND_ROW + turn],
            [functools.partial(swap_round, kind) for kind in range(len(KINDS) + 1)],
            ways[turn],
            ways[PLANES + turn],
        )
    )


def join_quarters(own):
    member = lax.axis_index("expert") % GROUP
    for bit in (1, 2):
        swap = (member & bit) != 0
        own = [jnp.where(swap, own[offset ^ bit], own[offset]) for offset in range(GROUP)]
    return jnp.concatenate(own, axis=0)


def per_device(
    tokens, cotangent, routes, gates, source, w_gate_up, w_down, moment_first, moment_second
):
    experts = lax.axis_size("expert")
    micro_count, token_count, part_width = tokens.shape
    model_width = w_gate_up.shape[1]
    hidden_part = w_gate_up.shape[3]
    top_count = routes.shape[2]
    capacity = max(2, 3 * token_count * top_count // (2 * experts))
    per_expert = micro_count * capacity
    slots = experts * per_expert
    all_tokens = micro_count * token_count
    swaps = experts == PLANES * GROUP

    pairs = token_count * top_count
    chosen = routes.reshape(micro_count, pairs)
    same = chosen[:, :, None] == chosen[:, None, :]
    order = jnp.arange(pairs, dtype=jnp.int32)
    earlier = order[None, :] < order[:, None]
    position = jnp.sum((same & earlier).astype(jnp.int32), axis=2)
    micro_ids = jnp.arange(micro_count, dtype=jnp.int32)[:, None]
    place = (chosen * per_expert + micro_ids * capacity + position).reshape(all_tokens, top_count)
    slot_ids = jnp.arange(slots, dtype=jnp.int32)
    flat_gates = gates.reshape(all_tokens, top_count)
    matches = [place[:, k][:, None] == slot_ids for k in range(top_count)]
    picks = [match.astype(jnp.bfloat16) for match in matches]
    plain = sum(picks[1:], picks[0])
    slot_gate = sum(
        jnp.sum(jnp.where(matches[k], flat_gates[:, k : k + 1], 0.0), axis=0)
        for k in range(top_count)
    )

    row_tokens = lax.dot_general(
        plain,
        tokens.reshape(all_tokens, part_width),
        contract_first,
        preferred_element_type=jnp.float32,
    ).astype(jnp.bfloat16)
    if swaps:
        index = lax.axis_index("expert")
        plane, member = index // GROUP, index % GROUP
        plan = make_plan(source, plane, member)
        row_tokens, (pieces_a, pieces_b) = fence(
            row_tokens, cut((moment_first[0], moment_second[0]), member)
        )
        held_a = hand_over(pieces_a)
        chip_b = step(pieces_b[1], pieces_b[3], 1)
    here_tokens = exchange(row_tokens.reshape(experts, per_expert, part_width))
    row_grads = (
        lax.dot_general(
            plain,
            cotangent.reshape(all_tokens, part_width),
            contract_first,
            preferred_element_type=jnp.float32,
        )
        * slot_gate[:, None]
    ).astype(jnp.bfloat16)
    gate_up = w_gate_up.reshape(model_width, 2 * hidden_part)
    down = w_down.reshape(hidden_part, model_width)

    if swaps:
        here_tokens, row_grads, gate_up, held_a, pieces_b, chip_b, plan = fence(
            here_tokens, row_grads, gate_up, held_a, pieces_b, chip_b, plan
        )
        held_b = [pieces_b[0], chip_b[0], *step(pieces_b[2], chip_b[1], 2)]
        ways_a = choose(plan[UP_ROW:FINAL_ROW], held_a)
        arrived_a = swap(0, plan, ways_a) + swap(1, plan, ways_a)
    grad_blocks = row_grads.reshape(experts, per_expert, part_width)
    here_grads = exchange(grad_blocks)
    expert_in = jnp.concatenate(gather_features(here_tokens.reshape(slots, part_width)), axis=1)
    if swaps:
        expert_in, here_grads, arrived_a, held_b = fence(
            expert_in, here_grads, arrived_a, held_b
        )
    both = jnp.dot(expert_in, gate_up, preferred_element_type=jnp.float32)
    gate_pre = both[:, :hidden_part]
    up_pre = both[:, hidden_part:]
    gate_sig = jax.nn.sigmoid(gate_pre)
    hidden = (gate_pre * gate_sig * up_pre).astype(jnp.bfloat16)
    partial_out = jnp.dot(hidden, down, preferred_element_type=jnp.float32).astype(jnp.bfloat16)

    if swaps:
        hidden, partial_out, ways_a, held_b = fence(hidden, partial_out, ways_a, held_b)
        arrived_a += swap(2, plan, ways_a) + swap(3, plan, ways_a)
        ready_a = choose(plan[FINAL_ROW:], [*held_a, *arrived_a])
        ways_b = choose(plan[UP_ROW:FINAL_ROW], held_b)
        cross_a = step(ready_a[2], ready_a[3], 2)
        arrived_b = swap(0, plan, ways_b) + swap(1, plan, ways_b)
    summed_out = scatter_sum(partial_out)

    if swaps:
        summed_out, here_grads, arrived_b, ready_a, cross_a, ways_b = fence(
            summed_out, here_grads, arrived_b, ready_a, cross_a, ways_b
        )
        chip_a = step(ready_a[1], cross_a[1], 1)
        own_a = [ready_a[0], chip_a[0], cross_a[0], chip_a[1]]
        arrived_b += swap(2, plan, ways_b) + swap(3, plan, ways_b)
        ready_b = choose(plan[FINAL_ROW:], [*held_b, *arrived_b])
    back = exchange(
        jnp.concatenate([summed_out, hidden], axis=1).reshape(experts, per_expert, -1)
    )
    grad_in = jnp.concatenate(gather_features(here_grads.reshape(slots, part_width)), axis=1)
    hidden_grad = lax.dot_general(
        grad_in, down, contract_second, preferred_element_type=jnp.float32
    )
    gate_grad = hidden_grad * up_pre * gate_sig * (1.0 + gate_pre * (1.0 - gate_sig))
    up_grad = hidden_grad * gate_pre * gate_sig
    both_grad = jnp.concatenate([gate_grad, up_grad], axis=1).astype(jnp.bfloat16)
    partial_in = lax.dot_general(
        both_grad, gate_up, contract_second, preferred_element_type=jnp.float32
    ).astype(jnp.bfloat16)
    to_move = reorder(jnp.concatenate([back[:, :, part_width:], grad_blocks], axis=2), source)

    if swaps:
        to_move, partial_in, own_a, ready_b = fence(to_move, partial_in, own_a, ready_b)
        cross_b = step(ready_b[2], ready_b[3], 2)
    there = exchange(to_move).reshape(slots, hidden_part + part_width)
    summed_in = scatter_sum(partial_in)
    back_out = back[:, :, :part_width].reshape(slots, part_width)
    layer_out = sum(
        flat_gates[:, k : k + 1] * jnp.dot(picks[k], back_out, preferred_element_type=jnp.float32)
        for k in range(top_count)
    ).astype(jnp.bfloat16)

    if swaps:
        there, summed_in, cross_b, layer_out, ready_b = fence(
            there, summed_in, cross_b, layer_out, ready_b
        )
        chip_b = step(ready_b[1], cross_b[1], 1)
        own_b = [ready_b[0], chip_b[0], cross_b[0], chip_b[1]]
    back_in = exchange(summed_in.reshape(experts, per_expert, part_width))
    token_grad = jnp.dot(
        plain, back_in.reshape(slots, part_width), preferred_element_type=jnp.float32
    )

    there_hidden = there[:, :hidden_part]
    there_grads = jnp.concatenate(gather_features(there[:, hidden_part:]), axis=1)
    if swaps:
        old_first, old_second = join_quarters(own_a), join_quarters(own_b)
    else:
        old_first, old_second = relocate_spread((moment_first, moment_second), source, experts)
    down_grad = lax.dot_general(
        there_hidden, there_grads, contract_first, preferred_element_type=jnp.float32
    )
    first = 0.9 * old_first.astype(jnp.float32) + 0.1 * down_grad
    second = 0.999 * old_second.astype(jnp.float32) + 0.001 * down_grad * down_grad
    update = first / (jnp.sqrt(second) + 1e-08)
    shape = moment_first.shape
    return (
        layer_out.reshape(tokens.shape),
        token_grad.astype(jnp.bfloat16).reshape(tokens.shape),
        update.astype(jnp.bfloat16).reshape(shape),
        first.astype(jnp.bfloat16).reshape(shape),
        second.astype(jnp.bfloat16).reshape(shape),
    )


def solution(mesh):
    placed = (
        P(None, "expert", "dp"),
        P(None, "expert", "dp"),
        P(None, "expert", None),
        P(None, "expert", None),
        P(),
        P("expert", None, None, "dp"),
        P("expert", "dp", None),
        P("expert", "dp", None),
        P("expert", "dp", None),
    )
    return jax.shard_map(
        per_device,
        mesh=mesh,
        in_specs=placed,
        out_specs=(
            P(None, "expert", "dp"),
            P(None, "expert", "dp"),
            P("expert", "dp", None),
            P("expert", "dp", None),
            P("expert", "dp", None),
        ),
        check_vma=False,
    )
```

```python
import functools

import jax
import jax.numpy as jnp
from jax import lax
from jax.experimental import pallas as pl
from jax.experimental.pallas import tpu as pltpu
from jax.sharding import PartitionSpec as P

contract_first = (((0,), (0,)), ((), ()))
contract_second = (((1,), (1,)), ((), ()))
VMEM_BYTES = 32 * 1024 * 1024
MOST_VMEM_BYTES = 60 * 1024 * 1024


def fence(*values):
    return lax.optimization_barrier(values)


def exchange(blocks):
    return lax.all_to_all(blocks, "expert", split_axis=0, concat_axis=0, tiled=True)


def reorder_kernel(order_ref, blocks_ref, out_ref):
    for place in range(out_ref.shape[0]):
        out_ref[place] = blocks_ref[order_ref[place]]


def reorder(blocks, order):
    whole = pl.BlockSpec(memory_space=pltpu.VMEM)
    return pl.pallas_call(
        reorder_kernel,
        out_shape=jax.ShapeDtypeStruct(blocks.shape, blocks.dtype),
        in_specs=[pl.BlockSpec(memory_space=pltpu.SMEM), whole],
        out_specs=whole,
        compiler_params=pltpu.CompilerParams(vmem_limit_bytes=VMEM_BYTES),
        name="reorder",
    )(order, blocks)


def gather_features(rows):
    parts = lax.axis_size("dp")
    if parts == 2:
        other = lax.ppermute(rows, "dp", ((0, 1), (1, 0)))
        first = lax.axis_index("dp") == 0
        return [jnp.where(first, rows, other), jnp.where(first, other, rows)]
    whole = lax.all_gather(rows, "dp", axis=0, tiled=False)
    return [whole[part] for part in range(parts)]


def scatter_sum(partial):
    parts = lax.axis_size("dp")
    if parts == 2:
        half = partial.shape[1] // 2
        low, high = partial[:, :half], partial[:, half:]
        first = lax.axis_index("dp") == 0
        keep, send = jnp.where(first, low, high), jnp.where(first, high, low)
        other = lax.ppermute(send, "dp", ((0, 1), (1, 0)))
        return (keep.astype(jnp.float32) + other.astype(jnp.float32)).astype(jnp.bfloat16)
    return lax.psum_scatter(partial, "dp", scatter_dimension=1, tiled=True)


def relocate_spread(arrays, source, experts):
    outputs = []
    for array in arrays:
        blocks = array.reshape(experts, array.shape[1] // experts, array.shape[2])
        outputs.append(exchange(reorder(exchange(blocks), source)).reshape(array.shape[1:]))
    return outputs


PLANES = 4
GROUP = 4
KINDS = (((0, 1), (1, 2), (2, 3)), ((0, 2), (2, 3)), ((0, 1), (1, 3)), ((0, 3),))
KIND_ROW, UP_ROW, DOWN_ROW, FINAL_ROW = 0, 4, 8, 12
HELD = GROUP + 1
EACH = (1,) * (2 * PLANES)


def held_place(offset):
    return jnp.where(offset == GROUP - 1, GROUP, offset)


def plan_kernel(where_ref, source_ref, plan_ref, ends_ref):
    plane = where_ref[0]
    member = where_ref[1]
    for index in range(PLANES):
        plan_ref[KIND_ROW + index] = 0
        plan_ref[UP_ROW + index] = HELD
        plan_ref[DOWN_ROW + index] = HELD
        ends_ref[index] = 0
    for slot in range(PLANES * GROUP):
        low = slot // GROUP
        other = source_ref[slot]
        high = other // GROUP
        offset = (slot % GROUP) ^ member

        @pl.when(jnp.logical_and(high == low, plane == low))
        def _():
            plan_ref[FINAL_ROW + offset] = held_place((other % GROUP) ^ member)

        @pl.when(high > low)
        def _():
            turn = jnp.int32(PLANES - 1)
            for index in reversed(range(PLANES - 1)):
                turn = jnp.where(ends_ref[index] <= low, index, turn)
            ends_ref[turn] = high
            span = high - low
            kind = jnp.where(span == 3, 4, jnp.where(span == 2, 2 + low, 1))
            plan_ref[KIND_ROW + turn] = jnp.maximum(plan_ref[KIND_ROW + turn], kind)

            @pl.when(plane == low)
            def _():
                plan_ref[UP_ROW + turn] = held_place(offset)
                plan_ref[FINAL_ROW + offset] = HELD + 2 * turn + 1

            @pl.when(plane == high)
            def _():
                there = (other % GROUP) ^ member
                plan_ref[DOWN_ROW + turn] = held_place(there)
                plan_ref[FINAL_ROW + there] = HELD + 2 * turn


def make_plan(source, plane, member):
    smem = pl.BlockSpec(memory_space=pltpu.SMEM)
    return pl.pallas_call(
        plan_kernel,
        out_shape=jax.ShapeDtypeStruct((16,), jnp.int32),
        in_specs=[smem, smem],
        out_specs=smem,
        scratch_shapes=[pltpu.SMEM((PLANES,), jnp.int32)],
        name="plan",
    )(jnp.stack([plane, member]), source)


def copy_all(loads, stores):
    for load in loads:
        load.start()
    for load, store in zip(loads, stores):
        load.wait()
        store.start()
    for store in stores:
        store.wait()


def cut_kernel(member_ref, *refs):
    count = (len(refs) - 3) // 4
    arrays, outs = refs[:count], refs[count:-3]
    staged, in_sems, out_sems = refs[-3:]
    rows = outs[0].shape[0]
    loads, stores = [], []
    for which, array in enumerate(arrays):
        own, near, across = outs[3 * which : 3 * which + 3]
        for offset, out in ((2, across.at[0]), (3, across.at[1]), (1, near), (0, own)):
            begin = pl.multiple_of((member_ref[0] ^ offset) * rows, rows)
            place = which * GROUP + offset
            loads.append(
                pltpu.make_async_copy(
                    array.at[pl.ds(begin, rows)], staged.at[place], in_sems.at[place]
                )
            )
            stores.append(pltpu.make_async_copy(staged.at[place], out, out_sems.at[place]))
    copy_all(loads, stores)


def cut(arrays, member):
    rows, width = arrays[0].shape
    anywhere = pl.BlockSpec(memory_space=pltpu.HBM)
    piece = (rows // GROUP, width)
    dtype = arrays[0].dtype
    amount = GROUP * len(arrays)
    shapes = [
        jax.ShapeDtypeStruct(piece, dtype),
        jax.ShapeDtypeStruct(piece, dtype),
        jax.ShapeDtypeStruct((2, *piece), dtype),
    ]
    pieces = pl.pallas_call(
        cut_kernel,
        out_shape=shapes * len(arrays),
        in_specs=[pl.BlockSpec(memory_space=pltpu.SMEM)] + [anywhere] * len(arrays),
        out_specs=[anywhere] * (3 * len(arrays)),
        scratch_shapes=[
            pltpu.VMEM((amount, *piece), dtype),
            pltpu.SemaphoreType.DMA((amount,)),
            pltpu.SemaphoreType.DMA((amount,)),
        ],
        compiler_params=pltpu.CompilerParams(vmem_limit_bytes=MOST_VMEM_BYTES),
        name="cut",
    )(member[None], *arrays)
    return [list(pieces[at : at + 3]) for at in range(0, 3 * len(arrays), 3)]


def choose_kernel(count, groups, choice_ref, *refs):
    arrays, outs = refs[:count], refs[count:-3]
    staged, in_sems, out_sems = refs[-3:]
    options = []
    for array in arrays:
        options += [array] if len(array.shape) == 2 else [array.at[i] for i in range(2)]
    places = []
    for out, group in zip(outs, groups):
        places += [out] if group == 1 else [out.at[i] for i in range(group)]
    for place in range(len(places)):
        for index, option in enumerate(options):

            @pl.when(choice_ref[place] == index)
            def _():
                pltpu.make_async_copy(option, staged.at[place], in_sems.at[place]).start()

    for place, out in enumerate(places):

        @pl.when(choice_ref[place] < len(options))
        def _():
            pltpu.make_async_copy(options[0], staged.at[place], in_sems.at[place]).wait()
            pltpu.make_async_copy(staged.at[place], out, out_sems.at[place]).start()

    for place, out in enumerate(places):

        @pl.when(choice_ref[place] < len(options))
        def _():
            pltpu.make_async_copy(staged.at[place], out, out_sems.at[place]).wait()


def choose(choice, arrays, groups):
    anywhere = pl.BlockSpec(memory_space=pltpu.HBM)
    piece, dtype = arrays[0].shape, arrays[0].dtype
    amount = choice.shape[0]
    return pl.pallas_call(
        functools.partial(choose_kernel, len(arrays), groups),
        out_shape=[
            jax.ShapeDtypeStruct(piece if group == 1 else (group, *piece), dtype)
            for group in groups
        ],
        in_specs=[pl.BlockSpec(memory_space=pltpu.SMEM)] + [anywhere] * len(arrays),
        out_specs=[anywhere] * len(groups),
        scratch_shapes=[
            pltpu.VMEM((amount, *piece), dtype),
            pltpu.SemaphoreType.DMA((amount,)),
            pltpu.SemaphoreType.DMA((amount,)),
        ],
        compiler_params=pltpu.CompilerParams(vmem_limit_bytes=MOST_VMEM_BYTES),
        name="choose",
    )(choice, *arrays)


def blank_kernel(*refs):
    pass


def blank(up, down):
    anywhere = pl.BlockSpec(memory_space=pltpu.HBM)
    return pl.pallas_call(
        blank_kernel,
        out_shape=[jax.ShapeDtypeStruct(like.shape, like.dtype) for like in (up, down)],
        out_specs=[anywhere] * 2,
        name="blank",
    )()


def within_plane(offset):
    return [(index, index ^ offset) for index in range(PLANES * GROUP)]


def between_planes(moves):
    return [(GROUP * a + index, GROUP * b + index) for a, b in moves for index in range(GROUP)]


def swap_round(kind, up, down):
    if kind == 0:
        return tuple(blank(up, down))
    moves = KINDS[kind - 1]
    return (
        lax.ppermute(up, "expert", between_planes(moves)),
        lax.ppermute(down, "expert", between_planes([(b, a) for a, b in moves])),
    )


def hand(piece, offset):
    return lax.ppermute(piece, "expert", within_plane(offset))


def swap(turn, plan, ways):
    return list(
        lax.switch(
            plan[KIND_ROW + turn],
            [functools.partial(swap_round, kind) for kind in range(len(KINDS) + 1)],
            ways[turn],
            ways[PLANES + turn],
        )
    )


def join_quarters(own):
    member = lax.axis_index("expert") % GROUP
    for bit in (1, 2):
        swap = (member & bit) != 0
        own = [jnp.where(swap, own[offset ^ bit], own[offset]) for offset in range(GROUP)]
    return jnp.concatenate(own, axis=0)


def per_device(
    tokens, cotangent, routes, gates, source, w_gate_up, w_down, moment_first, moment_second
):
    experts = lax.axis_size("expert")
    micro_count, token_count, part_width = tokens.shape
    model_width = w_gate_up.shape[1]
    hidden_part = w_gate_up.shape[3]
    top_count = routes.shape[2]
    capacity = max(2, 3 * token_count * top_count // (2 * experts))
    per_expert = micro_count * capacity
    slots = experts * per_expert
    all_tokens = micro_count * token_count
    swaps = experts == PLANES * GROUP

    pairs = token_count * top_count
    chosen = routes.reshape(micro_count, pairs)
    same = chosen[:, :, None] == chosen[:, None, :]
    order = jnp.arange(pairs, dtype=jnp.int32)
    earlier = order[None, :] < order[:, None]
    position = jnp.sum((same & earlier).astype(jnp.int32), axis=2)
    micro_ids = jnp.arange(micro_count, dtype=jnp.int32)[:, None]
    place = (chosen * per_expert + micro_ids * capacity + position).reshape(all_tokens, top_count)
    slot_ids = jnp.arange(slots, dtype=jnp.int32)
    flat_gates = gates.reshape(all_tokens, top_count)
    matches = [place[:, k][:, None] == slot_ids for k in range(top_count)]
    picks = [match.astype(jnp.bfloat16) for match in matches]
    plain = sum(picks[1:], picks[0])
    slot_gate = sum(
        jnp.sum(jnp.where(matches[k], flat_gates[:, k : k + 1], 0.0), axis=0)
        for k in range(top_count)
    )

    row_tokens = lax.dot_general(
        plain,
        tokens.reshape(all_tokens, part_width),
        contract_first,
        preferred_element_type=jnp.float32,
    ).astype(jnp.bfloat16)
    if swaps:
        index = lax.axis_index("expert")
        plane, member = index // GROUP, index % GROUP
        plan = make_plan(source, plane, member)
        row_tokens, ((own_a, near_a, across_a), (own_b, near_b, across_b)) = fence(
            row_tokens, cut((moment_first[0], moment_second[0]), member)
        )
        across_a, near_a, near_b = hand(across_a, 2), hand(near_a, 1), hand(near_b, 1)
    here_tokens = exchange(row_tokens.reshape(experts, per_expert, part_width))
    row_grads = (
        lax.dot_general(
            plain,
            cotangent.reshape(all_tokens, part_width),
            contract_first,
            preferred_element_type=jnp.float32,
        )
        * slot_gate[:, None]
    ).astype(jnp.bfloat16)
    gate_up = w_gate_up.reshape(model_width, 2 * hidden_part)
    down = w_down.reshape(hidden_part, model_width)

    if swaps:
        (here_tokens, row_grads, gate_up, own_a, near_a, across_a, near_b, across_b, plan) = fence(
            here_tokens, row_grads, gate_up, own_a, near_a, across_a, near_b, across_b, plan
        )
        held_a = [own_a, near_a, across_a, hand(across_a[1], 1)]
        across_b = hand(across_b, 2)
        ways_a = choose(plan[UP_ROW:FINAL_ROW], held_a, EACH)
        arrived_a = swap(0, plan, ways_a) + swap(1, plan, ways_a)
    grad_blocks = row_grads.reshape(experts, per_expert, part_width)
    here_grads = exchange(grad_blocks)
    expert_in = jnp.concatenate(gather_features(here_tokens.reshape(slots, part_width)), axis=1)
    if swaps:
        expert_in, here_grads, arrived_a, across_b = fence(
            expert_in, here_grads, arrived_a, across_b
        )
    both = jnp.dot(expert_in, gate_up, preferred_element_type=jnp.float32)
    gate_pre = both[:, :hidden_part]
    up_pre = both[:, hidden_part:]
    gate_sig = jax.nn.sigmoid(gate_pre)
    hidden = (gate_pre * gate_sig * up_pre).astype(jnp.bfloat16)
    partial_out = jnp.dot(hidden, down, preferred_element_type=jnp.float32).astype(jnp.bfloat16)

    if swaps:
        hidden, partial_out, ways_a, across_b = fence(hidden, partial_out, ways_a, across_b)
        held_b = [own_b, near_b, across_b, hand(across_b[1], 1)]
        arrived_a += swap(2, plan, ways_a) + swap(3, plan, ways_a)
        ready_a = choose(plan[FINAL_ROW:], [*held_a, *arrived_a], (1, 1, 2))
        ways_b = choose(plan[UP_ROW:FINAL_ROW], held_b, EACH)
        home_a = hand(ready_a[2], 2)
        arrived_b = swap(0, plan, ways_b) + swap(1, plan, ways_b)
    summed_out = scatter_sum(partial_out)

    if swaps:
        summed_out, here_grads, arrived_b, ready_a, home_a, ways_b = fence(
            summed_out, here_grads, arrived_b, ready_a, home_a, ways_b
        )
        old_first = join_quarters(
            [ready_a[0], hand(ready_a[1], 1), home_a[0], hand(home_a[1], 1)]
        )
        arrived_b += swap(2, plan, ways_b) + swap(3, plan, ways_b)
        ready_b = choose(plan[FINAL_ROW:], [*held_b, *arrived_b], (1, 1, 1, 1))
    back = exchange(
        jnp.concatenate([summed_out, hidden], axis=1).reshape(experts, per_expert, -1)
    )
    grad_in = jnp.concatenate(gather_features(here_grads.reshape(slots, part_width)), axis=1)
    hidden_grad = lax.dot_general(
        grad_in, down, contract_second, preferred_element_type=jnp.float32
    )
    gate_grad = hidden_grad * up_pre * gate_sig * (1.0 + gate_pre * (1.0 - gate_sig))
    up_grad = hidden_grad * gate_pre * gate_sig
    both_grad = jnp.concatenate([gate_grad, up_grad], axis=1).astype(jnp.bfloat16)
    partial_in = lax.dot_general(
        both_grad, gate_up, contract_second, preferred_element_type=jnp.float32
    ).astype(jnp.bfloat16)
    to_move = reorder(jnp.concatenate([back[:, :, part_width:], grad_blocks], axis=2), source)

    if swaps:
        to_move, partial_in, old_first, ready_b = fence(to_move, partial_in, old_first, ready_b)
        home_b = hand(ready_b[3], 3)
    there = exchange(to_move).reshape(slots, hidden_part + part_width)
    summed_in = scatter_sum(partial_in)
    back_out = back[:, :, :part_width].reshape(slots, part_width)
    layer_out = sum(
        flat_gates[:, k : k + 1] * jnp.dot(picks[k], back_out, preferred_element_type=jnp.float32)
        for k in range(top_count)
    ).astype(jnp.bfloat16)

    if swaps:
        there, summed_in, home_b, layer_out, ready_b = fence(
            there, summed_in, home_b, layer_out, ready_b
        )
        home_b = [ready_b[0], hand(ready_b[1], 1), hand(ready_b[2], 2), home_b]
    back_in = exchange(summed_in.reshape(experts, per_expert, part_width))
    token_grad = jnp.dot(
        plain, back_in.reshape(slots, part_width), preferred_element_type=jnp.float32
    )

    there_hidden = there[:, :hidden_part]
    there_grads = jnp.concatenate(gather_features(there[:, hidden_part:]), axis=1)
    if swaps:
        old_second = join_quarters(home_b)
    else:
        old_first, old_second = relocate_spread((moment_first, moment_second), source, experts)
    down_grad = lax.dot_general(
        there_hidden, there_grads, contract_first, preferred_element_type=jnp.float32
    )
    first = 0.9 * old_first.astype(jnp.float32) + 0.1 * down_grad
    second = 0.999 * old_second.astype(jnp.float32) + 0.001 * down_grad * down_grad
    update = first / (jnp.sqrt(second) + 1e-08)
    shape = moment_first.shape
    return (
        layer_out.reshape(tokens.shape),
        token_grad.astype(jnp.bfloat16).reshape(tokens.shape),
        update.astype(jnp.bfloat16).reshape(shape),
        first.astype(jnp.bfloat16).reshape(shape),
        second.astype(jnp.bfloat16).reshape(shape),
    )


def solution(mesh):
    placed = (
        P(None, "expert", "dp"),
        P(None, "expert", "dp"),
        P(None, "expert", None),
        P(None, "expert", None),
        P(),
        P("expert", None, None, "dp"),
        P("expert", "dp", None),
        P("expert", "dp", None),
        P("expert", "dp", None),
    )
    return jax.shard_map(
        per_device,
        mesh=mesh,
        in_specs=placed,
        out_specs=(
            P(None, "expert", "dp"),
            P(None, "expert", "dp"),
            P("expert", "dp", None),
            P("expert", "dp", None),
            P("expert", "dp", None),
        ),
        check_vma=False,
    )
```

```python
import functools

import jax
import jax.numpy as jnp
from jax import lax
from jax.experimental import pallas as pl
from jax.experimental.pallas import tpu as pltpu
from jax.sharding import PartitionSpec as P

contract_first = (((0,), (0,)), ((), ()))
contract_second = (((1,), (1,)), ((), ()))
VMEM_BYTES = 32 * 1024 * 1024
MOST_VMEM_BYTES = 60 * 1024 * 1024


def fence(*values):
    return lax.optimization_barrier(values)


def exchange(blocks):
    return lax.all_to_all(blocks, "expert", split_axis=0, concat_axis=0, tiled=True)


def reorder_kernel(order_ref, blocks_ref, out_ref):
    for place in range(out_ref.shape[0]):
        out_ref[place] = blocks_ref[order_ref[place]]


def reorder(blocks, order):
    whole = pl.BlockSpec(memory_space=pltpu.VMEM)
    return pl.pallas_call(
        reorder_kernel,
        out_shape=jax.ShapeDtypeStruct(blocks.shape, blocks.dtype),
        in_specs=[pl.BlockSpec(memory_space=pltpu.SMEM), whole],
        out_specs=whole,
        compiler_params=pltpu.CompilerParams(vmem_limit_bytes=VMEM_BYTES),
        name="reorder",
    )(order, blocks)


def gather_features(rows):
    parts = lax.axis_size("dp")
    if parts == 2:
        other = lax.ppermute(rows, "dp", ((0, 1), (1, 0)))
        first = lax.axis_index("dp") == 0
        return [jnp.where(first, rows, other), jnp.where(first, other, rows)]
    whole = lax.all_gather(rows, "dp", axis=0, tiled=False)
    return [whole[part] for part in range(parts)]


def scatter_sum(partial):
    parts = lax.axis_size("dp")
    if parts == 2:
        half = partial.shape[1] // 2
        low, high = partial[:, :half], partial[:, half:]
        first = lax.axis_index("dp") == 0
        keep, send = jnp.where(first, low, high), jnp.where(first, high, low)
        other = lax.ppermute(send, "dp", ((0, 1), (1, 0)))
        return (keep.astype(jnp.float32) + other.astype(jnp.float32)).astype(jnp.bfloat16)
    return lax.psum_scatter(partial, "dp", scatter_dimension=1, tiled=True)


def relocate_spread(arrays, source, experts):
    outputs = []
    for array in arrays:
        blocks = array.reshape(experts, array.shape[1] // experts, array.shape[2])
        outputs.append(exchange(reorder(exchange(blocks), source)).reshape(array.shape[1:]))
    return outputs


PLANES = 4
GROUP = 4
KINDS = (((0, 1), (1, 2), (2, 3)), ((0, 2), (2, 3)), ((0, 1), (1, 3)), ((0, 3),))
KIND_ROW, UP_ROW, DOWN_ROW, FINAL_ROW = 0, 4, 8, 12


def plan_kernel(where_ref, source_ref, plan_ref, ends_ref):
    plane = where_ref[0]
    member = where_ref[1]
    for index in range(PLANES):
        plan_ref[KIND_ROW + index] = 0
        plan_ref[UP_ROW + index] = GROUP
        plan_ref[DOWN_ROW + index] = GROUP
        ends_ref[index] = 0
    for slot in range(PLANES * GROUP):
        low = slot // GROUP
        other = source_ref[slot]
        high = other // GROUP
        offset = (slot % GROUP) ^ member

        @pl.when(jnp.logical_and(high == low, plane == low))
        def _():
            plan_ref[FINAL_ROW + offset] = (other % GROUP) ^ member

        @pl.when(high > low)
        def _():
            turn = jnp.int32(PLANES - 1)
            for index in reversed(range(PLANES - 1)):
                turn = jnp.where(ends_ref[index] <= low, index, turn)
            ends_ref[turn] = high
            span = high - low
            kind = jnp.where(span == 3, 4, jnp.where(span == 2, 2 + low, 1))
            plan_ref[KIND_ROW + turn] = jnp.maximum(plan_ref[KIND_ROW + turn], kind)

            @pl.when(plane == low)
            def _():
                plan_ref[UP_ROW + turn] = offset
                plan_ref[FINAL_ROW + offset] = GROUP + 2 * turn + 1

            @pl.when(plane == high)
            def _():
                there = (other % GROUP) ^ member
                plan_ref[DOWN_ROW + turn] = there
                plan_ref[FINAL_ROW + there] = GROUP + 2 * turn


def make_plan(source, plane, member):
    smem = pl.BlockSpec(memory_space=pltpu.SMEM)
    return pl.pallas_call(
        plan_kernel,
        out_shape=jax.ShapeDtypeStruct((16,), jnp.int32),
        in_specs=[smem, smem],
        out_specs=smem,
        scratch_shapes=[pltpu.SMEM((PLANES,), jnp.int32)],
        name="plan",
    )(jnp.stack([plane, member]), source)


def copy_all(loads, stores):
    for load in loads:
        load.start()
    for load, store in zip(loads, stores):
        load.wait()
        store.start()
    for store in stores:
        store.wait()


def cut_kernel(batches, member_ref, *refs):
    count = len(batches)
    first_ref, second_ref, outs = refs[0], refs[1], refs[2 : 2 + GROUP * count]
    staged, in_sems, out_sems = refs[2 + GROUP * count : -2], refs[-2], refs[-1]
    quarter = first_ref.shape[0] // GROUP
    loads, stores = [], []
    for which, parts in enumerate(batches):
        for offset in reversed(range(GROUP)):
            at = 0
            for part, (array, low, high) in enumerate(parts):
                begin = pl.multiple_of((member_ref[0] ^ offset) * quarter + low, 16)
                here = staged[which].at[offset, pl.ds(at, high - low)]
                out = outs[GROUP * which + offset].at[pl.ds(at, high - low)]
                source = (first_ref, second_ref)[array].at[pl.ds(begin, high - low)]
                place = (which * GROUP + offset) * 2 + part
                loads.append(pltpu.make_async_copy(source, here, in_sems.at[place]))
                stores.append(pltpu.make_async_copy(here, out, out_sems.at[place]))
                at += high - low
    copy_all(loads, stores)


def cut(first, second, batches, member):
    width = first.shape[1]
    anywhere = pl.BlockSpec(memory_space=pltpu.HBM)
    shapes = [(sum(high - low for _, low, high in parts), width) for parts in batches]
    amount = 2 * GROUP * len(batches)
    pieces = pl.pallas_call(
        functools.partial(cut_kernel, batches),
        out_shape=[jax.ShapeDtypeStruct(shape, first.dtype) for shape in shapes for _ in range(GROUP)],
        in_specs=[pl.BlockSpec(memory_space=pltpu.SMEM), anywhere, anywhere],
        out_specs=[anywhere] * (GROUP * len(batches)),
        scratch_shapes=[
            *[pltpu.VMEM((GROUP, *shape), first.dtype) for shape in shapes],
            pltpu.SemaphoreType.DMA((amount,)),
            pltpu.SemaphoreType.DMA((amount,)),
        ],
        compiler_params=pltpu.CompilerParams(vmem_limit_bytes=MOST_VMEM_BYTES),
        name="cut",
    )(member[None], first, second)
    return [list(pieces[at : at + GROUP]) for at in range(0, len(pieces), GROUP)]


def choose_kernel(count, choice_ref, *refs):
    options, outs = refs[:count], refs[count:-3]
    staged, in_sems, out_sems = refs[-3:]
    for place in range(len(outs)):
        for index, option in enumerate(options):

            @pl.when(choice_ref[place] == index)
            def _():
                pltpu.make_async_copy(option, staged.at[place], in_sems.at[place]).start()

    for place, out in enumerate(outs):

        @pl.when(choice_ref[place] < count)
        def _():
            pltpu.make_async_copy(options[0], staged.at[place], in_sems.at[place]).wait()
            pltpu.make_async_copy(staged.at[place], out, out_sems.at[place]).start()

    for place, out in enumerate(outs):

        @pl.when(choice_ref[place] < count)
        def _():
            pltpu.make_async_copy(staged.at[place], out, out_sems.at[place]).wait()


def choose(choice, options):
    anywhere = pl.BlockSpec(memory_space=pltpu.HBM)
    piece, dtype = options[0].shape, options[0].dtype
    amount = choice.shape[0]
    return pl.pallas_call(
        functools.partial(choose_kernel, len(options)),
        out_shape=[jax.ShapeDtypeStruct(piece, dtype)] * amount,
        in_specs=[pl.BlockSpec(memory_space=pltpu.SMEM)] + [anywhere] * len(options),
        out_specs=[anywhere] * amount,
        scratch_shapes=[
            pltpu.VMEM((amount, *piece), dtype),
            pltpu.SemaphoreType.DMA((amount,)),
            pltpu.SemaphoreType.DMA((amount,)),
        ],
        compiler_params=pltpu.CompilerParams(vmem_limit_bytes=MOST_VMEM_BYTES),
        name="choose",
    )(choice, *options)


def blank_kernel(*refs):
    pass


def blank(up, down):
    anywhere = pl.BlockSpec(memory_space=pltpu.HBM)
    return pl.pallas_call(
        blank_kernel,
        out_shape=[jax.ShapeDtypeStruct(like.shape, like.dtype) for like in (up, down)],
        out_specs=[anywhere] * 2,
        name="blank",
    )()


def within_plane(offset):
    return [(index, index ^ offset) for index in range(PLANES * GROUP)]


def between_planes(moves):
    return [(GROUP * a + index, GROUP * b + index) for a, b in moves for index in range(GROUP)]


def swap_round(kind, up, down):
    if kind == 0:
        return tuple(blank(up, down))
    moves = KINDS[kind - 1]
    return (
        lax.ppermute(up, "expert", between_planes(moves)),
        lax.ppermute(down, "expert", between_planes([(b, a) for a, b in moves])),
    )


def hand(piece, offset):
    return lax.ppermute(piece, "expert", within_plane(offset))


def swap(turn, plan, ways):
    return list(
        lax.switch(
            plan[KIND_ROW + turn],
            [functools.partial(swap_round, kind) for kind in range(len(KINDS) + 1)],
            ways[turn],
            ways[PLANES + turn],
        )
    )


def join_quarters(own):
    member = lax.axis_index("expert") % GROUP
    for bit in (1, 2):
        swap = (member & bit) != 0
        own = [jnp.where(swap, own[offset ^ bit], own[offset]) for offset in range(GROUP)]
    return own


def per_device(
    tokens, cotangent, routes, gates, source, w_gate_up, w_down, moment_first, moment_second
):
    experts = lax.axis_size("expert")
    micro_count, token_count, part_width = tokens.shape
    model_width = w_gate_up.shape[1]
    hidden_part = w_gate_up.shape[3]
    top_count = routes.shape[2]
    capacity = max(2, 3 * token_count * top_count // (2 * experts))
    per_expert = micro_count * capacity
    slots = experts * per_expert
    all_tokens = micro_count * token_count
    swaps = experts == PLANES * GROUP

    pairs = token_count * top_count
    chosen = routes.reshape(micro_count, pairs)
    same = chosen[:, :, None] == chosen[:, None, :]
    order = jnp.arange(pairs, dtype=jnp.int32)
    earlier = order[None, :] < order[:, None]
    position = jnp.sum((same & earlier).astype(jnp.int32), axis=2)
    micro_ids = jnp.arange(micro_count, dtype=jnp.int32)[:, None]
    place = (chosen * per_expert + micro_ids * capacity + position).reshape(all_tokens, top_count)
    slot_ids = jnp.arange(slots, dtype=jnp.int32)
    flat_gates = gates.reshape(all_tokens, top_count)
    matches = [place[:, k][:, None] == slot_ids for k in range(top_count)]
    picks = [match.astype(jnp.bfloat16) for match in matches]
    plain = sum(picks[1:], picks[0])
    slot_gate = sum(
        jnp.sum(jnp.where(matches[k], flat_gates[:, k : k + 1], 0.0), axis=0)
        for k in range(top_count)
    )

    row_tokens = lax.dot_general(
        plain,
        tokens.reshape(all_tokens, part_width),
        contract_first,
        preferred_element_type=jnp.float32,
    ).astype(jnp.bfloat16)
    if swaps:
        index = lax.axis_index("expert")
        plane, member = index // GROUP, index % GROUP
        plan = make_plan(source, plane, member)
        quarter = moment_first.shape[1] // GROUP
        half = quarter // 2
        row_tokens, (piece_a, piece_b) = fence(
            row_tokens,
            cut(
                moment_first[0],
                moment_second[0],
                (((0, 0, half),), ((0, half, quarter), (1, 0, quarter))),
                member,
            ),
        )
        held_a = [piece_a[0]] + [hand(piece_a[offset], offset) for offset in range(1, GROUP)]
        near_b = hand(piece_b[1], 1)
    here_tokens = exchange(row_tokens.reshape(experts, per_expert, part_width))
    row_grads = (
        lax.dot_general(
            plain,
            cotangent.reshape(all_tokens, part_width),
            contract_first,
            preferred_element_type=jnp.float32,
        )
        * slot_gate[:, None]
    ).astype(jnp.bfloat16)
    gate_up = w_gate_up.reshape(model_width, 2 * hidden_part)
    down = w_down.reshape(hidden_part, model_width)

    if swaps:
        here_tokens, row_grads, gate_up, held_a, piece_b, near_b, plan = fence(
            here_tokens, row_grads, gate_up, held_a, piece_b, near_b, plan
        )
        held_b = [piece_b[0], near_b, hand(piece_b[2], 2), hand(piece_b[3], 3)]
        ways_a = choose(plan[UP_ROW:FINAL_ROW], held_a)
        arrived_a = swap(0, plan, ways_a) + swap(1, plan, ways_a)
    grad_blocks = row_grads.reshape(experts, per_expert, part_width)
    here_grads = exchange(grad_blocks)
    expert_in = jnp.concatenate(gather_features(here_tokens.reshape(slots, part_width)), axis=1)
    if swaps:
        expert_in, here_grads, arrived_a, held_b = fence(
            expert_in, here_grads, arrived_a, held_b
        )
    both = jnp.dot(expert_in, gate_up, preferred_element_type=jnp.float32)
    gate_pre = both[:, :hidden_part]
    up_pre = both[:, hidden_part:]
    gate_sig = jax.nn.sigmoid(gate_pre)
    hidden = (gate_pre * gate_sig * up_pre).astype(jnp.bfloat16)
    partial_out = jnp.dot(hidden, down, preferred_element_type=jnp.float32).astype(jnp.bfloat16)

    if swaps:
        hidden, partial_out, ways_a, held_b = fence(hidden, partial_out, ways_a, held_b)
        arrived_a += swap(2, plan, ways_a) + swap(3, plan, ways_a)
        ready_a = choose(plan[FINAL_ROW:], [*held_a, *arrived_a])
        ways_b = choose(plan[UP_ROW:FINAL_ROW], held_b)
        home_a = [hand(ready_a[2], 2), hand(ready_a[3], 3)]
        arrived_b = swap(0, plan, ways_b) + swap(1, plan, ways_b)
    summed_out = scatter_sum(partial_out)

    if swaps:
        summed_out, here_grads, arrived_b, ready_a, home_a, ways_b = fence(
            summed_out, here_grads, arrived_b, ready_a, home_a, ways_b
        )
        rows_a = join_quarters([ready_a[0], hand(ready_a[1], 1), *home_a])
        arrived_b += swap(2, plan, ways_b) + swap(3, plan, ways_b)
        ready_b = choose(plan[FINAL_ROW:], [*held_b, *arrived_b])
    back = exchange(
        jnp.concatenate([summed_out, hidden], axis=1).reshape(experts, per_expert, -1)
    )
    grad_in = jnp.concatenate(gather_features(here_grads.reshape(slots, part_width)), axis=1)
    hidden_grad = lax.dot_general(
        grad_in, down, contract_second, preferred_element_type=jnp.float32
    )
    gate_grad = hidden_grad * up_pre * gate_sig * (1.0 + gate_pre * (1.0 - gate_sig))
    up_grad = hidden_grad * gate_pre * gate_sig
    both_grad = jnp.concatenate([gate_grad, up_grad], axis=1).astype(jnp.bfloat16)
    partial_in = lax.dot_general(
        both_grad, gate_up, contract_second, preferred_element_type=jnp.float32
    ).astype(jnp.bfloat16)
    to_move = reorder(jnp.concatenate([back[:, :, part_width:], grad_blocks], axis=2), source)

    if swaps:
        to_move, partial_in, rows_a, ready_b = fence(to_move, partial_in, rows_a, ready_b)
        home_b = hand(ready_b[3], 3)
    there = exchange(to_move).reshape(slots, hidden_part + part_width)
    summed_in = scatter_sum(partial_in)
    back_out = back[:, :, :part_width].reshape(slots, part_width)
    layer_out = sum(
        flat_gates[:, k : k + 1] * jnp.dot(picks[k], back_out, preferred_element_type=jnp.float32)
        for k in range(top_count)
    ).astype(jnp.bfloat16)

    if swaps:
        there, summed_in, home_b, layer_out, ready_b = fence(
            there, summed_in, home_b, layer_out, ready_b
        )
        home_b = [ready_b[0], hand(ready_b[1], 1), hand(ready_b[2], 2), home_b]
    back_in = exchange(summed_in.reshape(experts, per_expert, part_width))
    token_grad = jnp.dot(
        plain, back_in.reshape(slots, part_width), preferred_element_type=jnp.float32
    )

    there_hidden = there[:, :hidden_part]
    there_grads = jnp.concatenate(gather_features(there[:, hidden_part:]), axis=1)
    if swaps:
        rows_b = join_quarters(home_b)
        old_first = jnp.concatenate(
            [part for a, b in zip(rows_a, rows_b) for part in (a, b[: quarter - half])]
        )
        old_second = jnp.concatenate([b[quarter - half :] for b in rows_b])
    else:
        old_first, old_second = relocate_spread((moment_first, moment_second), source, experts)
    down_grad = lax.dot_general(
        there_hidden, there_grads, contract_first, preferred_element_type=jnp.float32
    )
    first = 0.9 * old_first.astype(jnp.float32) + 0.1 * down_grad
    second = 0.999 * old_second.astype(jnp.float32) + 0.001 * down_grad * down_grad
    update = first / (jnp.sqrt(second) + 1e-08)
    shape = moment_first.shape
    return (
        layer_out.reshape(tokens.shape),
        token_grad.astype(jnp.bfloat16).reshape(tokens.shape),
        update.astype(jnp.bfloat16).reshape(shape),
        first.astype(jnp.bfloat16).reshape(shape),
        second.astype(jnp.bfloat16).reshape(shape),
    )


def solution(mesh):
    placed = (
        P(None, "expert", "dp"),
        P(None, "expert", "dp"),
        P(None, "expert", None),
        P(None, "expert", None),
        P(),
        P("expert", None, None, "dp"),
        P("expert", "dp", None),
        P("expert", "dp", None),
        P("expert", "dp", None),
    )
    return jax.shard_map(
        per_device,
        mesh=mesh,
        in_specs=placed,
        out_specs=(
            P(None, "expert", "dp"),
            P(None, "expert", "dp"),
            P("expert", "dp", None),
            P("expert", "dp", None),
            P("expert", "dp", None),
        ),
        check_vma=False,
    )
```

```python
import functools

import jax
import jax.numpy as jnp
from jax import lax
from jax.experimental import pallas as pl
from jax.experimental.pallas import tpu as pltpu
from jax.sharding import PartitionSpec as P

contract_first = (((0,), (0,)), ((), ()))
contract_second = (((1,), (1,)), ((), ()))
VMEM_BYTES = 32 * 1024 * 1024
MOST_VMEM_BYTES = 60 * 1024 * 1024


def fence(*values):
    return lax.optimization_barrier(values)


def exchange(blocks):
    return lax.all_to_all(blocks, "expert", split_axis=0, concat_axis=0, tiled=True)


def reorder_kernel(order_ref, blocks_ref, out_ref):
    for place in range(out_ref.shape[0]):
        out_ref[place] = blocks_ref[order_ref[place]]


def reorder(blocks, order):
    whole = pl.BlockSpec(memory_space=pltpu.VMEM)
    return pl.pallas_call(
        reorder_kernel,
        out_shape=jax.ShapeDtypeStruct(blocks.shape, blocks.dtype),
        in_specs=[pl.BlockSpec(memory_space=pltpu.SMEM), whole],
        out_specs=whole,
        compiler_params=pltpu.CompilerParams(vmem_limit_bytes=VMEM_BYTES),
        name="reorder",
    )(order, blocks)


def gather_features(rows):
    parts = lax.axis_size("dp")
    if parts == 2:
        other = lax.ppermute(rows, "dp", ((0, 1), (1, 0)))
        first = lax.axis_index("dp") == 0
        return [jnp.where(first, rows, other), jnp.where(first, other, rows)]
    whole = lax.all_gather(rows, "dp", axis=0, tiled=False)
    return [whole[part] for part in range(parts)]


def scatter_sum(partial):
    parts = lax.axis_size("dp")
    if parts == 2:
        half = partial.shape[1] // 2
        low, high = partial[:, :half], partial[:, half:]
        first = lax.axis_index("dp") == 0
        keep, send = jnp.where(first, low, high), jnp.where(first, high, low)
        other = lax.ppermute(send, "dp", ((0, 1), (1, 0)))
        return (keep.astype(jnp.float32) + other.astype(jnp.float32)).astype(jnp.bfloat16)
    return lax.psum_scatter(partial, "dp", scatter_dimension=1, tiled=True)


def relocate_spread(arrays, source, experts):
    outputs = []
    for array in arrays:
        blocks = array.reshape(experts, array.shape[1] // experts, array.shape[2])
        outputs.append(exchange(reorder(exchange(blocks), source)).reshape(array.shape[1:]))
    return outputs


PLANES = 4
GROUP = 4
SWAPS = (((0, 1), (2, 3)), ((1, 2),), ((0, 2),), ((1, 3),), ((0, 3),))
CHAINS = (((0, 1), (1, 2), (2, 3)), ((0, 2), (2, 3)), ((0, 1), (1, 3)))
KIND_ROW, UP_ROW, DOWN_ROW, FINAL_ROW = 0, 4, 8, 12
END_ROW, PAIR_ROW, TURN_ROW = 0, 4, 8


def kind_of(pairs):
    def has(bit):
        return (pairs & (1 << bit)) != 0

    near = jnp.where(has(1), jnp.where(jnp.logical_or(has(0), has(2)), 6, 2), 1)
    kind = jnp.where(has(4), jnp.where(has(0), 8, 4), near)
    kind = jnp.where(has(3), jnp.where(has(2), 7, 3), kind)
    kind = jnp.where(has(5), 5, kind)
    return jnp.where(pairs == 0, 0, kind)


def plan_kernel(where_ref, source_ref, plan_ref, notes_ref):
    plane = where_ref[0]
    member = where_ref[1]
    for index in range(PLANES):
        plan_ref[UP_ROW + index] = GROUP
        plan_ref[DOWN_ROW + index] = GROUP
        notes_ref[END_ROW + index] = 0
        notes_ref[PAIR_ROW + index] = 0
    for slot in range(PLANES * GROUP):
        low = slot // GROUP
        high = source_ref[slot] // GROUP

        @pl.when(high > low)
        def _():
            turn = jnp.int32(PLANES - 1)
            for index in reversed(range(PLANES - 1)):
                turn = jnp.where(notes_ref[END_ROW + index] <= low, index, turn)
            notes_ref[END_ROW + turn] = high
            span = high - low
            bit = jnp.where(span == 3, 5, jnp.where(span == 2, 3 + low, low))
            notes_ref[PAIR_ROW + turn] = notes_ref[PAIR_ROW + turn] | (1 << bit)
            notes_ref[TURN_ROW + slot] = turn

    for index in range(PLANES):
        plan_ref[KIND_ROW + index] = kind_of(notes_ref[PAIR_ROW + index])
    for slot in range(PLANES * GROUP):
        low = slot // GROUP
        other = source_ref[slot]
        high = other // GROUP
        offset = (slot % GROUP) ^ member
        there = (other % GROUP) ^ member

        @pl.when(jnp.logical_and(high == low, plane == low))
        def _():
            plan_ref[FINAL_ROW + offset] = there

        @pl.when(high > low)
        def _():
            turn = notes_ref[TURN_ROW + slot]
            apart = (plan_ref[KIND_ROW + turn] > len(SWAPS)).astype(jnp.int32)

            @pl.when(plane == low)
            def _():
                plan_ref[UP_ROW + turn] = offset
                plan_ref[FINAL_ROW + offset] = GROUP + 2 * turn + apart

            @pl.when(plane == high)
            def _():
                plan_ref[UP_ROW + turn + (DOWN_ROW - UP_ROW) * apart] = there
                plan_ref[FINAL_ROW + there] = GROUP + 2 * turn


def make_plan(source, plane, member):
    smem = pl.BlockSpec(memory_space=pltpu.SMEM)
    return pl.pallas_call(
        plan_kernel,
        out_shape=jax.ShapeDtypeStruct((16,), jnp.int32),
        in_specs=[smem, smem],
        out_specs=smem,
        scratch_shapes=[pltpu.SMEM((TURN_ROW + PLANES * GROUP,), jnp.int32)],
        name="plan",
    )(jnp.stack([plane, member]), source)


def copy_all(loads, stores):
    for load in loads:
        load.start()
    for load, store in zip(loads, stores):
        load.wait()
        store.start()
    for store in stores:
        store.wait()


def cut_kernel(batches, member_ref, *refs):
    count = len(batches)
    first_ref, second_ref, outs = refs[0], refs[1], refs[2 : 2 + GROUP * count]
    staged, in_sems, out_sems = refs[2 + GROUP * count : -2], refs[-2], refs[-1]
    quarter = first_ref.shape[0] // GROUP
    loads, stores = [], []
    for which, parts in enumerate(batches):
        for offset in reversed(range(GROUP)):
            at = 0
            for part, (array, low, high) in enumerate(parts):
                begin = pl.multiple_of((member_ref[0] ^ offset) * quarter + low, 16)
                here = staged[which].at[offset, pl.ds(at, high - low)]
                out = outs[GROUP * which + offset].at[pl.ds(at, high - low)]
                source = (first_ref, second_ref)[array].at[pl.ds(begin, high - low)]
                place = (which * GROUP + offset) * 2 + part
                loads.append(pltpu.make_async_copy(source, here, in_sems.at[place]))
                stores.append(pltpu.make_async_copy(here, out, out_sems.at[place]))
                at += high - low
    copy_all(loads, stores)


def cut(first, second, batches, member):
    width = first.shape[1]
    anywhere = pl.BlockSpec(memory_space=pltpu.HBM)
    shapes = [(sum(high - low for _, low, high in parts), width) for parts in batches]
    amount = 2 * GROUP * len(batches)
    pieces = pl.pallas_call(
        functools.partial(cut_kernel, batches),
        out_shape=[jax.ShapeDtypeStruct(shape, first.dtype) for shape in shapes for _ in range(GROUP)],
        in_specs=[pl.BlockSpec(memory_space=pltpu.SMEM), anywhere, anywhere],
        out_specs=[anywhere] * (GROUP * len(batches)),
        scratch_shapes=[
            *[pltpu.VMEM((GROUP, *shape), first.dtype) for shape in shapes],
            pltpu.SemaphoreType.DMA((amount,)),
            pltpu.SemaphoreType.DMA((amount,)),
        ],
        compiler_params=pltpu.CompilerParams(vmem_limit_bytes=MOST_VMEM_BYTES),
        name="cut",
    )(member[None], first, second)
    return [list(pieces[at : at + GROUP]) for at in range(0, len(pieces), GROUP)]


def choose_kernel(count, choice_ref, *refs):
    options, outs = refs[:count], refs[count:-3]
    staged, in_sems, out_sems = refs[-3:]
    for place in range(len(outs)):
        for index, option in enumerate(options):

            @pl.when(choice_ref[place] == index)
            def _():
                pltpu.make_async_copy(option, staged.at[place], in_sems.at[place]).start()

    for place, out in enumerate(outs):

        @pl.when(choice_ref[place] < count)
        def _():
            pltpu.make_async_copy(options[0], staged.at[place], in_sems.at[place]).wait()
            pltpu.make_async_copy(staged.at[place], out, out_sems.at[place]).start()

    for place, out in enumerate(outs):

        @pl.when(choice_ref[place] < count)
        def _():
            pltpu.make_async_copy(staged.at[place], out, out_sems.at[place]).wait()


def choose(choice, options):
    anywhere = pl.BlockSpec(memory_space=pltpu.HBM)
    piece, dtype = options[0].shape, options[0].dtype
    amount = choice.shape[0]
    return pl.pallas_call(
        functools.partial(choose_kernel, len(options)),
        out_shape=[jax.ShapeDtypeStruct(piece, dtype)] * amount,
        in_specs=[pl.BlockSpec(memory_space=pltpu.SMEM)] + [anywhere] * len(options),
        out_specs=[anywhere] * amount,
        scratch_shapes=[
            pltpu.VMEM((amount, *piece), dtype),
            pltpu.SemaphoreType.DMA((amount,)),
            pltpu.SemaphoreType.DMA((amount,)),
        ],
        compiler_params=pltpu.CompilerParams(vmem_limit_bytes=MOST_VMEM_BYTES),
        name="choose",
    )(choice, *options)


def blank_kernel(*refs):
    pass


def blank(like):
    return pl.pallas_call(
        blank_kernel,
        out_shape=jax.ShapeDtypeStruct(like.shape, like.dtype),
        out_specs=pl.BlockSpec(memory_space=pltpu.HBM),
        name="blank",
    )()


def within_plane(offset):
    return [(index, index ^ offset) for index in range(PLANES * GROUP)]


def between_planes(moves):
    return [(GROUP * a + index, GROUP * b + index) for a, b in moves for index in range(GROUP)]


def turned(moves):
    return tuple((b, a) for a, b in moves)


def swap_nothing(up, down):
    return blank(up), blank(down)


def swap_together(moves, up, down):
    pairs = between_planes(moves + turned(moves))
    return lax.ppermute(up, "expert", pairs), blank(down)


def swap_apart(moves, up, down):
    return (
        lax.ppermute(up, "expert", between_planes(moves)),
        lax.ppermute(down, "expert", between_planes(turned(moves))),
    )


def hand(piece, offset):
    return lax.ppermute(piece, "expert", within_plane(offset))


def swap(turn, plan, ways):
    return list(
        lax.switch(
            plan[KIND_ROW + turn],
            [swap_nothing]
            + [functools.partial(swap_together, moves) for moves in SWAPS]
            + [functools.partial(swap_apart, moves) for moves in CHAINS],
            ways[turn],
            ways[PLANES + turn],
        )
    )


def join_quarters(own):
    member = lax.axis_index("expert") % GROUP
    for bit in (1, 2):
        swap = (member & bit) != 0
        own = [jnp.where(swap, own[offset ^ bit], own[offset]) for offset in range(GROUP)]
    return own


def per_device(
    tokens, cotangent, routes, gates, source, w_gate_up, w_down, moment_first, moment_second
):
    experts = lax.axis_size("expert")
    micro_count, token_count, part_width = tokens.shape
    model_width = w_gate_up.shape[1]
    hidden_part = w_gate_up.shape[3]
    top_count = routes.shape[2]
    capacity = max(2, 3 * token_count * top_count // (2 * experts))
    per_expert = micro_count * capacity
    slots = experts * per_expert
    all_tokens = micro_count * token_count
    swaps = experts == PLANES * GROUP

    pairs = token_count * top_count
    chosen = routes.reshape(micro_count, pairs)
    same = chosen[:, :, None] == chosen[:, None, :]
    order = jnp.arange(pairs, dtype=jnp.int32)
    earlier = order[None, :] < order[:, None]
    position = jnp.sum((same & earlier).astype(jnp.int32), axis=2)
    micro_ids = jnp.arange(micro_count, dtype=jnp.int32)[:, None]
    place = (chosen * per_expert + micro_ids * capacity + position).reshape(all_tokens, top_count)
    slot_ids = jnp.arange(slots, dtype=jnp.int32)
    flat_gates = gates.reshape(all_tokens, top_count)
    matches = [place[:, k][:, None] == slot_ids for k in range(top_count)]
    picks = [match.astype(jnp.bfloat16) for match in matches]
    plain = sum(picks[1:], picks[0])
    slot_gate = sum(
        jnp.sum(jnp.where(matches[k], flat_gates[:, k : k + 1], 0.0), axis=0)
        for k in range(top_count)
    )

    row_tokens = lax.dot_general(
        plain,
        tokens.reshape(all_tokens, part_width),
        contract_first,
        preferred_element_type=jnp.float32,
    ).astype(jnp.bfloat16)
    if swaps:
        index = lax.axis_index("expert")
        plane, member = index // GROUP, index % GROUP
        plan = make_plan(source, plane, member)
        quarter = moment_first.shape[1] // GROUP
        part = 3 * quarter // 4
        row_tokens, (piece_a, piece_b) = fence(
            row_tokens,
            cut(
                moment_first[0],
                moment_second[0],
                (((0, 0, part),), ((0, part, quarter), (1, 0, quarter))),
                member,
            ),
        )
        held_a = [piece_a[0]] + [hand(piece_a[offset], offset) for offset in range(1, GROUP)]
        near_b = hand(piece_b[1], 1)
    here_tokens = exchange(row_tokens.reshape(experts, per_expert, part_width))
    row_grads = (
        lax.dot_general(
            plain,
            cotangent.reshape(all_tokens, part_width),
            contract_first,
            preferred_element_type=jnp.float32,
        )
        * slot_gate[:, None]
    ).astype(jnp.bfloat16)
    gate_up = w_gate_up.reshape(model_width, 2 * hidden_part)
    down = w_down.reshape(hidden_part, model_width)

    if swaps:
        here_tokens, row_grads, gate_up, held_a, piece_b, near_b, plan = fence(
            here_tokens, row_grads, gate_up, held_a, piece_b, near_b, plan
        )
        held_b = [piece_b[0], near_b, hand(piece_b[2], 2), hand(piece_b[3], 3)]
        ways_a = choose(plan[UP_ROW:FINAL_ROW], held_a)
        arrived_a = swap(0, plan, ways_a) + swap(1, plan, ways_a)
    grad_blocks = row_grads.reshape(experts, per_expert, part_width)
    here_grads = exchange(grad_blocks)
    expert_in = jnp.concatenate(gather_features(here_tokens.reshape(slots, part_width)), axis=1)
    if swaps:
        expert_in, here_grads, arrived_a, held_b = fence(
            expert_in, here_grads, arrived_a, held_b
        )
    both = jnp.dot(expert_in, gate_up, preferred_element_type=jnp.float32)
    gate_pre = both[:, :hidden_part]
    up_pre = both[:, hidden_part:]
    gate_sig = jax.nn.sigmoid(gate_pre)
    hidden = (gate_pre * gate_sig * up_pre).astype(jnp.bfloat16)
    partial_out = jnp.dot(hidden, down, preferred_element_type=jnp.float32).astype(jnp.bfloat16)

    if swaps:
        hidden, partial_out, ways_a, held_b = fence(hidden, partial_out, ways_a, held_b)
        arrived_a += swap(2, plan, ways_a) + swap(3, plan, ways_a)
        ready_a = choose(plan[FINAL_ROW:], [*held_a, *arrived_a])
        ways_b = choose(plan[UP_ROW:FINAL_ROW], held_b)
        home_a = [hand(ready_a[2], 2), hand(ready_a[3], 3)]
        arrived_b = swap(0, plan, ways_b) + swap(1, plan, ways_b)
    summed_out = scatter_sum(partial_out)

    if swaps:
        summed_out, here_grads, arrived_b, ready_a, home_a, ways_b = fence(
            summed_out, here_grads, arrived_b, ready_a, home_a, ways_b
        )
        rows_a = join_quarters([ready_a[0], hand(ready_a[1], 1), *home_a])
        arrived_b += swap(2, plan, ways_b) + swap(3, plan, ways_b)
        ready_b = choose(plan[FINAL_ROW:], [*held_b, *arrived_b])
    back = exchange(
        jnp.concatenate([summed_out, hidden], axis=1).reshape(experts, per_expert, -1)
    )
    grad_in = jnp.concatenate(gather_features(here_grads.reshape(slots, part_width)), axis=1)
    hidden_grad = lax.dot_general(
        grad_in, down, contract_second, preferred_element_type=jnp.float32
    )
    gate_grad = hidden_grad * up_pre * gate_sig * (1.0 + gate_pre * (1.0 - gate_sig))
    up_grad = hidden_grad * gate_pre * gate_sig
    both_grad = jnp.concatenate([gate_grad, up_grad], axis=1).astype(jnp.bfloat16)
    partial_in = lax.dot_general(
        both_grad, gate_up, contract_second, preferred_element_type=jnp.float32
    ).astype(jnp.bfloat16)
    to_move = reorder(jnp.concatenate([back[:, :, part_width:], grad_blocks], axis=2), source)

    if swaps:
        to_move, partial_in, rows_a, ready_b = fence(to_move, partial_in, rows_a, ready_b)
        home_b = hand(ready_b[3], 3)
    there = exchange(to_move).reshape(slots, hidden_part + part_width)
    summed_in = scatter_sum(partial_in)
    back_out = back[:, :, :part_width].reshape(slots, part_width)
    layer_out = sum(
        flat_gates[:, k : k + 1] * jnp.dot(picks[k], back_out, preferred_element_type=jnp.float32)
        for k in range(top_count)
    ).astype(jnp.bfloat16)

    if swaps:
        there, summed_in, home_b, layer_out, ready_b = fence(
            there, summed_in, home_b, layer_out, ready_b
        )
        home_b = [ready_b[0], hand(ready_b[1], 1), hand(ready_b[2], 2), home_b]
    back_in = exchange(summed_in.reshape(experts, per_expert, part_width))
    token_grad = jnp.dot(
        plain, back_in.reshape(slots, part_width), preferred_element_type=jnp.float32
    )

    there_hidden = there[:, :hidden_part]
    there_grads = jnp.concatenate(gather_features(there[:, hidden_part:]), axis=1)
    if swaps:
        rows_b = join_quarters(home_b)
        old_first = jnp.concatenate(
            [rows for a, b in zip(rows_a, rows_b) for rows in (a, b[: quarter - part])]
        )
        old_second = jnp.concatenate([b[quarter - part :] for b in rows_b])
    else:
        old_first, old_second = relocate_spread((moment_first, moment_second), source, experts)
    down_grad = lax.dot_general(
        there_hidden, there_grads, contract_first, preferred_element_type=jnp.float32
    )
    first = 0.9 * old_first.astype(jnp.float32) + 0.1 * down_grad
    second = 0.999 * old_second.astype(jnp.float32) + 0.001 * down_grad * down_grad
    update = first / (jnp.sqrt(second) + 1e-08)
    shape = moment_first.shape
    return (
        layer_out.reshape(tokens.shape),
        token_grad.astype(jnp.bfloat16).reshape(tokens.shape),
        update.astype(jnp.bfloat16).reshape(shape),
        first.astype(jnp.bfloat16).reshape(shape),
        second.astype(jnp.bfloat16).reshape(shape),
    )


def solution(mesh):
    placed = (
        P(None, "expert", "dp"),
        P(None, "expert", "dp"),
        P(None, "expert", None),
        P(None, "expert", None),
        P(),
        P("expert", None, None, "dp"),
        P("expert", "dp", None),
        P("expert", "dp", None),
        P("expert", "dp", None),
    )
    return jax.shard_map(
        per_device,
        mesh=mesh,
        in_specs=placed,
        out_specs=(
            P(None, "expert", "dp"),
            P(None, "expert", "dp"),
            P("expert", "dp", None),
            P("expert", "dp", None),
            P("expert", "dp", None),
        ),
        check_vma=False,
    )
```

```python
import functools

import jax
import jax.numpy as jnp
from jax import lax
from jax.experimental import pallas as pl
from jax.experimental.pallas import tpu as pltpu
from jax.sharding import PartitionSpec as P

contract_first = (((0,), (0,)), ((), ()))
contract_second = (((1,), (1,)), ((), ()))
VMEM_BYTES = 32 * 1024 * 1024
MOST_VMEM_BYTES = 60 * 1024 * 1024


def fence(*values):
    return lax.optimization_barrier(values)


def exchange(blocks):
    return lax.all_to_all(blocks, "expert", split_axis=0, concat_axis=0, tiled=True)


def reorder_kernel(starts, order_ref, *refs):
    out_ref = refs[-1]
    for place in range(out_ref.shape[0]):
        at = 0
        for start, ref in zip(starts, refs[:-1]):
            width = ref.shape[2] - start
            out_ref[place, :, pl.ds(at, width)] = ref[order_ref[place], :, pl.ds(start, width)]
            at += width


def reorder(sources, order):
    whole = pl.BlockSpec(memory_space=pltpu.VMEM)
    blocks = [blocks for blocks, _ in sources]
    starts = [start for _, start in sources]
    width = sum(each.shape[2] - start for each, start in sources)
    return pl.pallas_call(
        functools.partial(reorder_kernel, starts),
        out_shape=jax.ShapeDtypeStruct((*blocks[0].shape[:2], width), blocks[0].dtype),
        in_specs=[pl.BlockSpec(memory_space=pltpu.SMEM)] + [whole] * len(blocks),
        out_specs=whole,
        compiler_params=pltpu.CompilerParams(vmem_limit_bytes=VMEM_BYTES),
        name="reorder",
    )(order, *blocks)


def gather_features(rows):
    parts = lax.axis_size("dp")
    if parts == 2:
        other = lax.ppermute(rows, "dp", ((0, 1), (1, 0)))
        first = lax.axis_index("dp") == 0
        return [jnp.where(first, rows, other), jnp.where(first, other, rows)]
    whole = lax.all_gather(rows, "dp", axis=0, tiled=False)
    return [whole[part] for part in range(parts)]


def split_parts(partial):
    half = partial.shape[1] // 2
    low, high = partial[:, :half], partial[:, half:]
    first = lax.axis_index("dp") == 0
    return jnp.where(first, low, high), jnp.where(first, high, low)


def add_parts(keep, other):
    return (keep.astype(jnp.float32) + other.astype(jnp.float32)).astype(jnp.bfloat16)


def scatter_sum(partial):
    if lax.axis_size("dp") == 2:
        keep, send = split_parts(partial)
        return add_parts(keep, lax.ppermute(send, "dp", ((0, 1), (1, 0))))
    return lax.psum_scatter(partial, "dp", scatter_dimension=1, tiled=True)


def relocate_spread(arrays, source, experts):
    outputs = []
    for array in arrays:
        blocks = array.reshape(experts, array.shape[1] // experts, array.shape[2])
        outputs.append(exchange(reorder([(exchange(blocks), 0)], source)).reshape(array.shape[1:]))
    return outputs


PLANES = 4
GROUP = 4
SWAPS = (((0, 1), (2, 3)), ((1, 2),), ((0, 2),), ((1, 3),), ((0, 3),))
CHAINS = (((0, 1), (1, 2), (2, 3)), ((0, 2), (2, 3)), ((0, 1), (1, 3)))
KIND_ROW, UP_ROW, DOWN_ROW, FINAL_ROW = 0, 4, 8, 12
END_ROW, PAIR_ROW, TURN_ROW = 0, 4, 8


def kind_of(pairs):
    def has(bit):
        return (pairs & (1 << bit)) != 0

    near = jnp.where(has(1), jnp.where(jnp.logical_or(has(0), has(2)), 6, 2), 1)
    kind = jnp.where(has(4), jnp.where(has(0), 8, 4), near)
    kind = jnp.where(has(3), jnp.where(has(2), 7, 3), kind)
    kind = jnp.where(has(5), 5, kind)
    return jnp.where(pairs == 0, 0, kind)


def plan_kernel(where_ref, source_ref, plan_ref, notes_ref):
    plane = where_ref[0]
    member = where_ref[1]
    for index in range(PLANES):
        plan_ref[UP_ROW + index] = GROUP
        plan_ref[DOWN_ROW + index] = GROUP
        notes_ref[END_ROW + index] = 0
        notes_ref[PAIR_ROW + index] = 0
    for slot in range(PLANES * GROUP):
        low = slot // GROUP
        high = source_ref[slot] // GROUP

        @pl.when(high > low)
        def _():
            turn = jnp.int32(PLANES - 1)
            for index in reversed(range(PLANES - 1)):
                turn = jnp.where(notes_ref[END_ROW + index] <= low, index, turn)
            notes_ref[END_ROW + turn] = high
            span = high - low
            bit = jnp.where(span == 3, 5, jnp.where(span == 2, 3 + low, low))
            notes_ref[PAIR_ROW + turn] = notes_ref[PAIR_ROW + turn] | (1 << bit)
            notes_ref[TURN_ROW + slot] = turn

    for index in range(PLANES):
        plan_ref[KIND_ROW + index] = kind_of(notes_ref[PAIR_ROW + index])
    for slot in range(PLANES * GROUP):
        low = slot // GROUP
        other = source_ref[slot]
        high = other // GROUP
        offset = (slot % GROUP) ^ member
        there = (other % GROUP) ^ member

        @pl.when(jnp.logical_and(high == low, plane == low))
        def _():
            plan_ref[FINAL_ROW + offset] = there

        @pl.when(high > low)
        def _():
            turn = notes_ref[TURN_ROW + slot]
            apart = (plan_ref[KIND_ROW + turn] > len(SWAPS)).astype(jnp.int32)

            @pl.when(plane == low)
            def _():
                plan_ref[UP_ROW + turn] = offset
                plan_ref[FINAL_ROW + offset] = GROUP + 2 * turn + apart

            @pl.when(plane == high)
            def _():
                plan_ref[UP_ROW + turn + (DOWN_ROW - UP_ROW) * apart] = there
                plan_ref[FINAL_ROW + there] = GROUP + 2 * turn


def make_plan(source, plane, member):
    smem = pl.BlockSpec(memory_space=pltpu.SMEM)
    return pl.pallas_call(
        plan_kernel,
        out_shape=jax.ShapeDtypeStruct((16,), jnp.int32),
        in_specs=[smem, smem],
        out_specs=smem,
        scratch_shapes=[pltpu.SMEM((TURN_ROW + PLANES * GROUP,), jnp.int32)],
        name="plan",
    )(jnp.stack([plane, member]), source)


def copy_all(loads, stores):
    for load in loads:
        load.start()
    for load, store in zip(loads, stores):
        load.wait()
        store.start()
    for store in stores:
        store.wait()


def cut_kernel(batches, member_ref, *refs):
    count = len(batches)
    first_ref, second_ref, outs = refs[0], refs[1], refs[2 : 2 + GROUP * count]
    staged, in_sems, out_sems = refs[2 + GROUP * count : -2], refs[-2], refs[-1]
    quarter = first_ref.shape[0] // GROUP
    loads, stores = [], []
    for which, parts in enumerate(batches):
        for offset in reversed(range(GROUP)):
            at = 0
            for part, (array, low, high) in enumerate(parts):
                begin = pl.multiple_of((member_ref[0] ^ offset) * quarter + low, 16)
                here = staged[which].at[offset, pl.ds(at, high - low)]
                out = outs[GROUP * which + offset].at[pl.ds(at, high - low)]
                source = (first_ref, second_ref)[array].at[pl.ds(begin, high - low)]
                place = (which * GROUP + offset) * 2 + part
                loads.append(pltpu.make_async_copy(source, here, in_sems.at[place]))
                stores.append(pltpu.make_async_copy(here, out, out_sems.at[place]))
                at += high - low
    copy_all(loads, stores)


def cut(first, second, batches, member):
    width = first.shape[1]
    anywhere = pl.BlockSpec(memory_space=pltpu.HBM)
    shapes = [(sum(high - low for _, low, high in parts), width) for parts in batches]
    amount = 2 * GROUP * len(batches)
    pieces = pl.pallas_call(
        functools.partial(cut_kernel, batches),
        out_shape=[jax.ShapeDtypeStruct(shape, first.dtype) for shape in shapes for _ in range(GROUP)],
        in_specs=[pl.BlockSpec(memory_space=pltpu.SMEM), anywhere, anywhere],
        out_specs=[anywhere] * (GROUP * len(batches)),
        scratch_shapes=[
            *[pltpu.VMEM((GROUP, *shape), first.dtype) for shape in shapes],
            pltpu.SemaphoreType.DMA((amount,)),
            pltpu.SemaphoreType.DMA((amount,)),
        ],
        compiler_params=pltpu.CompilerParams(vmem_limit_bytes=MOST_VMEM_BYTES),
        name="cut",
    )(member[None], first, second)
    return [list(pieces[at : at + GROUP]) for at in range(0, len(pieces), GROUP)]


def choose_kernel(counts, amounts, *refs):
    total = len(counts)
    choices, refs = refs[:total], refs[total:]
    options, refs = refs[: sum(counts)], refs[sum(counts) :]
    outs, staged = refs[: sum(amounts)], refs[sum(amounts) : -2]
    in_sems, out_sems = refs[-2:]
    tasks = []
    for which, choice in enumerate(choices):
        begin, at = sum(counts[:which]), sum(amounts[:which])
        for place in range(amounts[which]):
            tasks.append(
                (
                    choice[place],
                    options[begin : begin + counts[which]],
                    staged[which].at[place],
                    outs[at + place],
                    at + place,
                )
            )
    for named, some, here, out, place in tasks:
        for index, option in enumerate(some):

            @pl.when(named == index)
            def _():
                pltpu.make_async_copy(option, here, in_sems.at[place]).start()

    for named, some, here, out, place in tasks:

        @pl.when(named < len(some))
        def _():
            pltpu.make_async_copy(some[0], here, in_sems.at[place]).wait()
            pltpu.make_async_copy(here, out, out_sems.at[place]).start()

    for named, some, here, out, place in tasks:

        @pl.when(named < len(some))
        def _():
            pltpu.make_async_copy(here, out, out_sems.at[place]).wait()


def choose(*lists):
    anywhere = pl.BlockSpec(memory_space=pltpu.HBM)
    amounts = [choice.shape[0] for choice, _ in lists]
    counts = [len(options) for _, options in lists]
    kinds = [(options[0].shape, options[0].dtype) for _, options in lists]
    chosen = pl.pallas_call(
        functools.partial(choose_kernel, counts, amounts),
        out_shape=[
            jax.ShapeDtypeStruct(shape, dtype)
            for amount, (shape, dtype) in zip(amounts, kinds)
            for _ in range(amount)
        ],
        in_specs=[pl.BlockSpec(memory_space=pltpu.SMEM)] * len(lists) + [anywhere] * sum(counts),
        out_specs=[anywhere] * sum(amounts),
        scratch_shapes=[
            *[pltpu.VMEM((amount, *shape), dtype) for amount, (shape, dtype) in zip(amounts, kinds)],
            pltpu.SemaphoreType.DMA((sum(amounts),)),
            pltpu.SemaphoreType.DMA((sum(amounts),)),
        ],
        compiler_params=pltpu.CompilerParams(vmem_limit_bytes=MOST_VMEM_BYTES),
        name="choose",
    )(*[choice for choice, _ in lists], *[option for _, options in lists for option in options])
    ends = [sum(amounts[: which + 1]) for which in range(len(lists))]
    results = [list(chosen[end - amount : end]) for end, amount in zip(ends, amounts)]
    return results[0] if len(results) == 1 else results


def blank_kernel(*refs):
    pass


def blank(like):
    return pl.pallas_call(
        blank_kernel,
        out_shape=jax.ShapeDtypeStruct(like.shape, like.dtype),
        out_specs=pl.BlockSpec(memory_space=pltpu.HBM),
        name="blank",
    )()


def within_plane(offset):
    return [(index, index ^ offset) for index in range(PLANES * GROUP)]


def between_planes(moves):
    return [(GROUP * a + index, GROUP * b + index) for a, b in moves for index in range(GROUP)]


def turned(moves):
    return tuple((b, a) for a, b in moves)


def swap_nothing(up, down):
    return blank(up), blank(down)


def swap_together(moves, up, down):
    pairs = between_planes(moves + turned(moves))
    return lax.ppermute(up, "expert", pairs), blank(down)


def swap_apart(moves, up, down):
    return (
        lax.ppermute(up, "expert", between_planes(moves)),
        lax.ppermute(down, "expert", between_planes(turned(moves))),
    )


def hand(piece, offset):
    return lax.ppermute(piece, "expert", within_plane(offset))


def swap(turn, plan, ways, work=None, values=()):
    kinds = (
        [swap_nothing]
        + [functools.partial(swap_together, moves) for moves in SWAPS]
        + [functools.partial(swap_apart, moves) for moves in CHAINS]
    )

    def branch(kind):
        if work is None:
            return lambda up, down, values: (kind(up, down), ())
        return lambda up, down, values: (kind(up, down), work(*values))

    arrived, results = lax.switch(
        plan[KIND_ROW + turn],
        [branch(kind) for kind in kinds],
        ways[turn],
        ways[PLANES + turn],
        values,
    )
    return list(arrived) if work is None else (list(arrived), results)


def join_quarters(own):
    member = lax.axis_index("expert") % GROUP
    for bit in (1, 2):
        swap = (member & bit) != 0
        own = [jnp.where(swap, own[offset ^ bit], own[offset]) for offset in range(GROUP)]
    return own


def per_device(
    tokens, cotangent, routes, gates, source, w_gate_up, w_down, moment_first, moment_second
):
    experts = lax.axis_size("expert")
    micro_count, token_count, part_width = tokens.shape
    model_width = w_gate_up.shape[1]
    hidden_part = w_gate_up.shape[3]
    top_count = routes.shape[2]
    capacity = max(2, 3 * token_count * top_count // (2 * experts))
    per_expert = micro_count * capacity
    slots = experts * per_expert
    all_tokens = micro_count * token_count
    swaps = experts == PLANES * GROUP and lax.axis_size("dp") == 2

    pairs = token_count * top_count
    chosen = routes.reshape(micro_count, pairs)
    same = chosen[:, :, None] == chosen[:, None, :]
    order = jnp.arange(pairs, dtype=jnp.int32)
    earlier = order[None, :] < order[:, None]
    position = jnp.sum((same & earlier).astype(jnp.int32), axis=2)
    micro_ids = jnp.arange(micro_count, dtype=jnp.int32)[:, None]
    place = (chosen * per_expert + micro_ids * capacity + position).reshape(all_tokens, top_count)
    slot_ids = jnp.arange(slots, dtype=jnp.int32)
    flat_gates = gates.reshape(all_tokens, top_count)
    matches = [place[:, k][:, None] == slot_ids for k in range(top_count)]
    picks = [match.astype(jnp.bfloat16) for match in matches]
    plain = sum(picks[1:], picks[0])
    slot_gate = sum(
        jnp.sum(jnp.where(matches[k], flat_gates[:, k : k + 1], 0.0), axis=0)
        for k in range(top_count)
    )

    if swaps:
        index = lax.axis_index("expert")
        plane, member = index // GROUP, index % GROUP
        plan = make_plan(source, plane, member)
        quarter = moment_first.shape[1] // GROUP
        part = 3 * quarter // 4
        tokens, (piece_a, piece_b) = fence(
            tokens,
            cut(
                moment_first[0],
                moment_second[0],
                (((0, 0, part),), ((0, part, quarter), (1, 0, quarter))),
                member,
            ),
        )
        held_a = [piece_a[0]] + [hand(piece_a[offset], offset) for offset in range(1, GROUP)]
        near_b = hand(piece_b[1], 1)
    row_tokens = lax.dot_general(
        plain,
        tokens.reshape(all_tokens, part_width),
        contract_first,
        preferred_element_type=jnp.float32,
    ).astype(jnp.bfloat16)
    here_tokens = exchange(row_tokens.reshape(experts, per_expert, part_width))
    row_grads = (
        lax.dot_general(
            plain,
            cotangent.reshape(all_tokens, part_width),
            contract_first,
            preferred_element_type=jnp.float32,
        )
        * slot_gate[:, None]
    ).astype(jnp.bfloat16)
    gate_up = w_gate_up.reshape(model_width, 2 * hidden_part)
    down = w_down.reshape(hidden_part, model_width)

    if swaps:
        here_tokens, row_grads, gate_up, held_a, piece_b, near_b, plan = fence(
            here_tokens, row_grads, gate_up, held_a, piece_b, near_b, plan
        )
        held_b = [piece_b[0], near_b, hand(piece_b[2], 2), hand(piece_b[3], 3)]
        ways_a = choose((plan[UP_ROW:FINAL_ROW], held_a))
        arrived_a = swap(0, plan, ways_a)
    grad_blocks = row_grads.reshape(experts, per_expert, part_width)
    here_grads = exchange(grad_blocks)
    expert_in = jnp.concatenate(gather_features(here_tokens.reshape(slots, part_width)), axis=1)

    def forward(expert_in, gate_up, down):
        both = jnp.dot(expert_in, gate_up, preferred_element_type=jnp.float32)
        gate_pre = both[:, :hidden_part]
        up_pre = both[:, hidden_part:]
        hidden = (gate_pre * jax.nn.sigmoid(gate_pre) * up_pre).astype(jnp.bfloat16)
        partial_out = jnp.dot(hidden, down, preferred_element_type=jnp.float32)
        return gate_pre, up_pre, hidden, partial_out.astype(jnp.bfloat16)

    if swaps:
        expert_in, arrived_a = fence(expert_in, arrived_a)
        arrived, (gate_pre, up_pre, hidden, partial_out) = swap(
            1, plan, ways_a, forward, (expert_in, gate_up, down)
        )
        arrived_a += arrived
    else:
        gate_pre, up_pre, hidden, partial_out = forward(expert_in, gate_up, down)
    gate_sig = jax.nn.sigmoid(gate_pre)

    if swaps:
        here_grads, hidden, partial_out, ways_a, arrived_a, held_b = fence(
            here_grads, hidden, partial_out, ways_a, arrived_a, held_b
        )
        arrived_a += swap(2, plan, ways_a) + swap(3, plan, ways_a)
        ready_a, ways_b = choose(
            (plan[FINAL_ROW:], [*held_a, *arrived_a]), (plan[UP_ROW:FINAL_ROW], held_b)
        )
        home_a = [hand(ready_a[2], 2), hand(ready_a[3], 3)]
        arrived_b = swap(0, plan, ways_b)

    def going_back(keep, other, hidden):
        return jnp.concatenate([add_parts(keep, other), hidden], axis=1)

    if swaps:
        keep, send = split_parts(partial_out)
        other = lax.ppermute(send, "dp", ((0, 1), (1, 0)))
        other, arrived_b = fence(other, arrived_b)
        arrived, outgoing = swap(1, plan, ways_b, going_back, (keep, other, hidden))
        arrived_b += arrived
    else:
        outgoing = jnp.concatenate([scatter_sum(partial_out), hidden], axis=1)

    if swaps:
        outgoing, here_grads, arrived_b, ready_a, home_a, ways_b = fence(
            outgoing, here_grads, arrived_b, ready_a, home_a, ways_b
        )
        rows_a = join_quarters([ready_a[0], hand(ready_a[1], 1), *home_a])
        arrived_b += swap(2, plan, ways_b) + swap(3, plan, ways_b)
        ready_b = choose((plan[FINAL_ROW:], [*held_b, *arrived_b]))
    back = exchange(outgoing.reshape(experts, per_expert, -1))
    grad_in = jnp.concatenate(gather_features(here_grads.reshape(slots, part_width)), axis=1)
    hidden_grad = lax.dot_general(
        grad_in, down, contract_second, preferred_element_type=jnp.float32
    )
    gate_grad = hidden_grad * up_pre * gate_sig * (1.0 + gate_pre * (1.0 - gate_sig))
    up_grad = hidden_grad * gate_pre * gate_sig
    both_grad = jnp.concatenate([gate_grad, up_grad], axis=1).astype(jnp.bfloat16)
    partial_in = lax.dot_general(
        both_grad, gate_up, contract_second, preferred_element_type=jnp.float32
    ).astype(jnp.bfloat16)
    to_move = reorder([(back, part_width), (grad_blocks, 0)], source)

    if swaps:
        to_move, partial_in, rows_a, ready_b = fence(to_move, partial_in, rows_a, ready_b)
        home_b = hand(ready_b[3], 3)
    there = exchange(to_move).reshape(slots, hidden_part + part_width)
    there_hidden, there_rows = there[:, :hidden_part], there[:, hidden_part:]
    summed_in = scatter_sum(partial_in)
    back_out = back[:, :, :part_width].reshape(slots, part_width)
    layer_out = sum(
        flat_gates[:, k : k + 1] * jnp.dot(picks[k], back_out, preferred_element_type=jnp.float32)
        for k in range(top_count)
    ).astype(jnp.bfloat16)

    if swaps:
        there_hidden, there_rows, summed_in, home_b, layer_out, ready_b = fence(
            there_hidden, there_rows, summed_in, home_b, layer_out, ready_b
        )
        home_b = [ready_b[0], hand(ready_b[1], 1), hand(ready_b[2], 2), home_b]
    back_in = exchange(summed_in.reshape(experts, per_expert, part_width))
    token_grad = jnp.dot(
        plain, back_in.reshape(slots, part_width), preferred_element_type=jnp.float32
    )

    there_grads = jnp.concatenate(gather_features(there_rows), axis=1)
    if swaps:
        rows_b = join_quarters(home_b)
        old_first = jnp.concatenate(
            [rows for a, b in zip(rows_a, rows_b) for rows in (a, b[: quarter - part])]
        )
        old_second = jnp.concatenate([b[quarter - part :] for b in rows_b])
    else:
        old_first, old_second = relocate_spread((moment_first, moment_second), source, experts)
    down_grad = lax.dot_general(
        there_hidden, there_grads, contract_first, preferred_element_type=jnp.float32
    )
    first = 0.9 * old_first.astype(jnp.float32) + 0.1 * down_grad
    second = 0.999 * old_second.astype(jnp.float32) + 0.001 * down_grad * down_grad
    update = first / (jnp.sqrt(second) + 1e-08)
    shape = moment_first.shape
    return (
        layer_out.reshape(tokens.shape),
        token_grad.astype(jnp.bfloat16).reshape(tokens.shape),
        update.astype(jnp.bfloat16).reshape(shape),
        first.astype(jnp.bfloat16).reshape(shape),
        second.astype(jnp.bfloat16).reshape(shape),
    )


def solution(mesh):
    placed = (
        P(None, "expert", "dp"),
        P(None, "expert", "dp"),
        P(None, "expert", None),
        P(None, "expert", None),
        P(),
        P("expert", None, None, "dp"),
        P("expert", "dp", None),
        P("expert", "dp", None),
        P("expert", "dp", None),
    )
    return jax.shard_map(
        per_device,
        mesh=mesh,
        in_specs=placed,
        out_specs=(
            P(None, "expert", "dp"),
            P(None, "expert", "dp"),
            P("expert", "dp", None),
            P("expert", "dp", None),
            P("expert", "dp", None),
        ),
        check_vma=False,
    )
```

```python
import functools

import jax
import jax.numpy as jnp
from jax import lax
from jax.experimental import pallas as pl
from jax.experimental.pallas import tpu as pltpu
from jax.sharding import PartitionSpec as P

contract_first = (((0,), (0,)), ((), ()))
contract_second = (((1,), (1,)), ((), ()))
VMEM_BYTES = 32 * 1024 * 1024
MOST_VMEM_BYTES = 60 * 1024 * 1024


def fence(*values):
    return lax.optimization_barrier(values)


def exchange(blocks):
    return lax.all_to_all(blocks, "expert", split_axis=0, concat_axis=0, tiled=True)


def reorder_kernel(starts, order_ref, *refs):
    out_ref = refs[-1]
    for place in range(out_ref.shape[0]):
        at = 0
        for start, ref in zip(starts, refs[:-1]):
            width = ref.shape[2] - start
            out_ref[place, :, pl.ds(at, width)] = ref[order_ref[place], :, pl.ds(start, width)]
            at += width


def reorder(sources, order):
    whole = pl.BlockSpec(memory_space=pltpu.VMEM)
    blocks = [blocks for blocks, _ in sources]
    starts = [start for _, start in sources]
    width = sum(each.shape[2] - start for each, start in sources)
    return pl.pallas_call(
        functools.partial(reorder_kernel, starts),
        out_shape=jax.ShapeDtypeStruct((*blocks[0].shape[:2], width), blocks[0].dtype),
        in_specs=[pl.BlockSpec(memory_space=pltpu.SMEM)] + [whole] * len(blocks),
        out_specs=whole,
        compiler_params=pltpu.CompilerParams(vmem_limit_bytes=VMEM_BYTES),
        name="reorder",
    )(order, *blocks)


def gather_features(rows):
    parts = lax.axis_size("dp")
    if parts == 2:
        other = lax.ppermute(rows, "dp", ((0, 1), (1, 0)))
        first = lax.axis_index("dp") == 0
        return [jnp.where(first, rows, other), jnp.where(first, other, rows)]
    whole = lax.all_gather(rows, "dp", axis=0, tiled=False)
    return [whole[part] for part in range(parts)]


def split_parts(partial):
    half = partial.shape[1] // 2
    low, high = partial[:, :half], partial[:, half:]
    first = lax.axis_index("dp") == 0
    return jnp.where(first, low, high), jnp.where(first, high, low)


def add_parts(keep, other):
    return (keep.astype(jnp.float32) + other.astype(jnp.float32)).astype(jnp.bfloat16)


def scatter_sum(partial):
    if lax.axis_size("dp") == 2:
        keep, send = split_parts(partial)
        return add_parts(keep, lax.ppermute(send, "dp", ((0, 1), (1, 0))))
    return lax.psum_scatter(partial, "dp", scatter_dimension=1, tiled=True)


def relocate_spread(arrays, source, experts):
    outputs = []
    for array in arrays:
        blocks = array.reshape(experts, array.shape[1] // experts, array.shape[2])
        outputs.append(exchange(reorder([(exchange(blocks), 0)], source)).reshape(array.shape[1:]))
    return outputs


PLANES = 4
GROUP = 4
SWAPS = (((0, 1), (2, 3)), ((1, 2),), ((0, 2),), ((1, 3),), ((0, 3),))
CHAINS = (((0, 1), (1, 2), (2, 3)), ((0, 2), (2, 3)), ((0, 1), (1, 3)))
KIND_ROW, UP_ROW, DOWN_ROW, FINAL_ROW = 0, 4, 8, 12
END_ROW, PAIR_ROW, TURN_ROW = 0, 4, 8


def kind_of(pairs):
    def has(bit):
        return (pairs & (1 << bit)) != 0

    near = jnp.where(has(1), jnp.where(jnp.logical_or(has(0), has(2)), 6, 2), 1)
    kind = jnp.where(has(4), jnp.where(has(0), 8, 4), near)
    kind = jnp.where(has(3), jnp.where(has(2), 7, 3), kind)
    kind = jnp.where(has(5), 5, kind)
    return jnp.where(pairs == 0, 0, kind)


def plan_kernel(where_ref, source_ref, plan_ref, notes_ref):
    plane = where_ref[0]
    member = where_ref[1]
    for index in range(PLANES):
        plan_ref[UP_ROW + index] = GROUP
        plan_ref[DOWN_ROW + index] = GROUP
        notes_ref[END_ROW + index] = 0
        notes_ref[PAIR_ROW + index] = 0
    for slot in range(PLANES * GROUP):
        low = slot // GROUP
        high = source_ref[slot] // GROUP

        @pl.when(high > low)
        def _():
            turn = jnp.int32(PLANES - 1)
            for index in reversed(range(PLANES - 1)):
                turn = jnp.where(notes_ref[END_ROW + index] <= low, index, turn)
            notes_ref[END_ROW + turn] = high
            span = high - low
            bit = jnp.where(span == 3, 5, jnp.where(span == 2, 3 + low, low))
            notes_ref[PAIR_ROW + turn] = notes_ref[PAIR_ROW + turn] | (1 << bit)
            notes_ref[TURN_ROW + slot] = turn

    for index in range(PLANES):
        plan_ref[KIND_ROW + index] = kind_of(notes_ref[PAIR_ROW + index])
    for slot in range(PLANES * GROUP):
        low = slot // GROUP
        other = source_ref[slot]
        high = other // GROUP
        offset = (slot % GROUP) ^ member
        there = (other % GROUP) ^ member

        @pl.when(jnp.logical_and(high == low, plane == low))
        def _():
            plan_ref[FINAL_ROW + offset] = there

        @pl.when(high > low)
        def _():
            turn = notes_ref[TURN_ROW + slot]
            apart = (plan_ref[KIND_ROW + turn] > len(SWAPS)).astype(jnp.int32)

            @pl.when(plane == low)
            def _():
                plan_ref[UP_ROW + turn] = offset
                plan_ref[FINAL_ROW + offset] = GROUP + 2 * turn + apart

            @pl.when(plane == high)
            def _():
                plan_ref[UP_ROW + turn + (DOWN_ROW - UP_ROW) * apart] = there
                plan_ref[FINAL_ROW + there] = GROUP + 2 * turn


def make_plan(source, plane, member):
    smem = pl.BlockSpec(memory_space=pltpu.SMEM)
    return pl.pallas_call(
        plan_kernel,
        out_shape=jax.ShapeDtypeStruct((16,), jnp.int32),
        in_specs=[smem, smem],
        out_specs=smem,
        scratch_shapes=[pltpu.SMEM((TURN_ROW + PLANES * GROUP,), jnp.int32)],
        name="plan",
    )(jnp.stack([plane, member]), source)


def copy_all(loads, stores):
    for load in loads:
        load.start()
    for load, store in zip(loads, stores):
        load.wait()
        store.start()
    for store in stores:
        store.wait()


def cut_kernel(batches, member_ref, *refs):
    count = len(batches)
    first_ref, second_ref, outs = refs[0], refs[1], refs[2 : 2 + GROUP * count]
    staged, in_sems, out_sems = refs[2 + GROUP * count : -2], refs[-2], refs[-1]
    quarter = first_ref.shape[0] // GROUP
    loads, stores = [], []
    for which, parts in enumerate(batches):
        for offset in reversed(range(GROUP)):
            at = 0
            for part, (array, low, high) in enumerate(parts):
                begin = pl.multiple_of((member_ref[0] ^ offset) * quarter + low, 16)
                here = staged[which].at[offset, pl.ds(at, high - low)]
                out = outs[GROUP * which + offset].at[pl.ds(at, high - low)]
                source = (first_ref, second_ref)[array].at[pl.ds(begin, high - low)]
                place = (which * GROUP + offset) * 2 + part
                loads.append(pltpu.make_async_copy(source, here, in_sems.at[place]))
                stores.append(pltpu.make_async_copy(here, out, out_sems.at[place]))
                at += high - low
    copy_all(loads, stores)


def cut(first, second, batches, member):
    width = first.shape[1]
    anywhere = pl.BlockSpec(memory_space=pltpu.HBM)
    shapes = [(sum(high - low for _, low, high in parts), width) for parts in batches]
    amount = 2 * GROUP * len(batches)
    pieces = pl.pallas_call(
        functools.partial(cut_kernel, batches),
        out_shape=[jax.ShapeDtypeStruct(shape, first.dtype) for shape in shapes for _ in range(GROUP)],
        in_specs=[pl.BlockSpec(memory_space=pltpu.SMEM), anywhere, anywhere],
        out_specs=[anywhere] * (GROUP * len(batches)),
        scratch_shapes=[
            *[pltpu.VMEM((GROUP, *shape), first.dtype) for shape in shapes],
            pltpu.SemaphoreType.DMA((amount,)),
            pltpu.SemaphoreType.DMA((amount,)),
        ],
        compiler_params=pltpu.CompilerParams(vmem_limit_bytes=MOST_VMEM_BYTES),
        name="cut",
    )(member[None], first, second)
    return [list(pieces[at : at + GROUP]) for at in range(0, len(pieces), GROUP)]


def choose_kernel(counts, amounts, *refs):
    total = len(counts)
    choices, refs = refs[:total], refs[total:]
    options, refs = refs[: sum(counts)], refs[sum(counts) :]
    outs, staged = refs[: sum(amounts)], refs[sum(amounts) : -2]
    in_sems, out_sems = refs[-2:]
    tasks = []
    for which, choice in enumerate(choices):
        begin, at = sum(counts[:which]), sum(amounts[:which])
        for place in range(amounts[which]):
            tasks.append(
                (
                    choice[place],
                    options[begin : begin + counts[which]],
                    staged[which].at[place],
                    outs[at + place],
                    at + place,
                )
            )
    for named, some, here, out, place in tasks:
        for index, option in enumerate(some):

            @pl.when(named == index)
            def _():
                pltpu.make_async_copy(option, here, in_sems.at[place]).start()

    for named, some, here, out, place in tasks:

        @pl.when(named < len(some))
        def _():
            pltpu.make_async_copy(some[0], here, in_sems.at[place]).wait()
            pltpu.make_async_copy(here, out, out_sems.at[place]).start()

    for named, some, here, out, place in tasks:

        @pl.when(named < len(some))
        def _():
            pltpu.make_async_copy(here, out, out_sems.at[place]).wait()


def choose(*lists):
    anywhere = pl.BlockSpec(memory_space=pltpu.HBM)
    amounts = [choice.shape[0] for choice, _ in lists]
    counts = [len(options) for _, options in lists]
    kinds = [(options[0].shape, options[0].dtype) for _, options in lists]
    chosen = pl.pallas_call(
        functools.partial(choose_kernel, counts, amounts),
        out_shape=[
            jax.ShapeDtypeStruct(shape, dtype)
            for amount, (shape, dtype) in zip(amounts, kinds)
            for _ in range(amount)
        ],
        in_specs=[pl.BlockSpec(memory_space=pltpu.SMEM)] * len(lists) + [anywhere] * sum(counts),
        out_specs=[anywhere] * sum(amounts),
        scratch_shapes=[
            *[pltpu.VMEM((amount, *shape), dtype) for amount, (shape, dtype) in zip(amounts, kinds)],
            pltpu.SemaphoreType.DMA((sum(amounts),)),
            pltpu.SemaphoreType.DMA((sum(amounts),)),
        ],
        compiler_params=pltpu.CompilerParams(vmem_limit_bytes=MOST_VMEM_BYTES),
        name="choose",
    )(*[choice for choice, _ in lists], *[option for _, options in lists for option in options])
    ends = [sum(amounts[: which + 1]) for which in range(len(lists))]
    results = [list(chosen[end - amount : end]) for end, amount in zip(ends, amounts)]
    return results[0] if len(results) == 1 else results


def blank_kernel(*refs):
    pass


def blank(like):
    return pl.pallas_call(
        blank_kernel,
        out_shape=jax.ShapeDtypeStruct(like.shape, like.dtype),
        out_specs=pl.BlockSpec(memory_space=pltpu.HBM),
        name="blank",
    )()


def within_plane(offset):
    return [(index, index ^ offset) for index in range(PLANES * GROUP)]


def between_planes(moves):
    return [(GROUP * a + index, GROUP * b + index) for a, b in moves for index in range(GROUP)]


def turned(moves):
    return tuple((b, a) for a, b in moves)


def swap_nothing(up, down):
    return blank(up), blank(down)


def swap_together(moves, up, down):
    pairs = between_planes(moves + turned(moves))
    return lax.ppermute(up, "expert", pairs), blank(down)


def swap_apart(moves, up, down):
    return (
        lax.ppermute(up, "expert", between_planes(moves)),
        lax.ppermute(down, "expert", between_planes(turned(moves))),
    )


def hand(piece, offset):
    return lax.ppermute(piece, "expert", within_plane(offset))


def swap(turn, plan, ways, work=None, values=()):
    kinds = (
        [swap_nothing]
        + [functools.partial(swap_together, moves) for moves in SWAPS]
        + [functools.partial(swap_apart, moves) for moves in CHAINS]
    )

    def branch(kind):
        if work is None:
            return lambda up, down, values: (kind(up, down), ())
        return lambda up, down, values: (kind(up, down), work(*values))

    arrived, results = lax.switch(
        plan[KIND_ROW + turn],
        [branch(kind) for kind in kinds],
        ways[turn],
        ways[PLANES + turn],
        values,
    )
    return list(arrived) if work is None else (list(arrived), results)


def join_quarters(own):
    member = lax.axis_index("expert") % GROUP
    for bit in (1, 2):
        swap = (member & bit) != 0
        own = [jnp.where(swap, own[offset ^ bit], own[offset]) for offset in range(GROUP)]
    return own


def per_device(
    tokens, cotangent, routes, gates, source, w_gate_up, w_down, moment_first, moment_second
):
    experts = lax.axis_size("expert")
    micro_count, token_count, part_width = tokens.shape
    model_width = w_gate_up.shape[1]
    hidden_part = w_gate_up.shape[3]
    top_count = routes.shape[2]
    capacity = max(2, 3 * token_count * top_count // (2 * experts))
    per_expert = micro_count * capacity
    slots = experts * per_expert
    all_tokens = micro_count * token_count
    swaps = experts == PLANES * GROUP and lax.axis_size("dp") == 2

    pairs = token_count * top_count
    chosen = routes.reshape(micro_count, pairs)
    same = chosen[:, :, None] == chosen[:, None, :]
    order = jnp.arange(pairs, dtype=jnp.int32)
    earlier = order[None, :] < order[:, None]
    position = jnp.sum((same & earlier).astype(jnp.int32), axis=2)
    micro_ids = jnp.arange(micro_count, dtype=jnp.int32)[:, None]
    place = (chosen * per_expert + micro_ids * capacity + position).reshape(all_tokens, top_count)
    slot_ids = jnp.arange(slots, dtype=jnp.int32)
    flat_gates = gates.reshape(all_tokens, top_count)
    matches = [place[:, k][:, None] == slot_ids for k in range(top_count)]
    picks = [match.astype(jnp.bfloat16) for match in matches]
    plain = sum(picks[1:], picks[0])
    slot_gate = sum(
        jnp.sum(jnp.where(matches[k], flat_gates[:, k : k + 1], 0.0), axis=0)
        for k in range(top_count)
    )

    if swaps:
        index = lax.axis_index("expert")
        plane, member = index // GROUP, index % GROUP
        plan = make_plan(source, plane, member)
        quarter = moment_first.shape[1] // GROUP
        part = 3 * quarter // 4
        tokens, (piece_a, piece_b) = fence(
            tokens,
            cut(
                moment_first[0],
                moment_second[0],
                (((0, 0, part),), ((0, part, quarter), (1, 0, quarter))),
                member,
            ),
        )
        held_a = [piece_a[0]] + [hand(piece_a[offset], offset) for offset in range(1, GROUP)]
        near_b = hand(piece_b[1], 1)
    row_tokens = lax.dot_general(
        plain,
        tokens.reshape(all_tokens, part_width),
        contract_first,
        preferred_element_type=jnp.float32,
    ).astype(jnp.bfloat16)
    here_tokens = exchange(row_tokens.reshape(experts, per_expert, part_width))
    row_grads = (
        lax.dot_general(
            plain,
            cotangent.reshape(all_tokens, part_width),
            contract_first,
            preferred_element_type=jnp.float32,
        )
        * slot_gate[:, None]
    ).astype(jnp.bfloat16)
    gate_up = w_gate_up.reshape(model_width, 2 * hidden_part)
    down = w_down.reshape(hidden_part, model_width)

    if swaps:
        here_tokens, row_grads, gate_up, held_a, piece_b, near_b, plan = fence(
            here_tokens, row_grads, gate_up, held_a, piece_b, near_b, plan
        )
        held_b = [piece_b[0], near_b, hand(piece_b[2], 2), hand(piece_b[3], 3)]
        ways_a = choose((plan[UP_ROW:FINAL_ROW], held_a))
        arrived_a = swap(0, plan, ways_a) + swap(1, plan, ways_a)
    grad_blocks = row_grads.reshape(experts, per_expert, part_width)
    here_grads = exchange(grad_blocks)
    expert_in = jnp.concatenate(gather_features(here_tokens.reshape(slots, part_width)), axis=1)

    def forward(expert_in, gate_up, down):
        both = jnp.dot(expert_in, gate_up, preferred_element_type=jnp.float32)
        gate_pre = both[:, :hidden_part]
        up_pre = both[:, hidden_part:]
        hidden = (gate_pre * jax.nn.sigmoid(gate_pre) * up_pre).astype(jnp.bfloat16)
        partial_out = jnp.dot(hidden, down, preferred_element_type=jnp.float32)
        return gate_pre, up_pre, hidden, partial_out.astype(jnp.bfloat16)

    if swaps:
        expert_in, here_grads, arrived_a, held_b = fence(
            expert_in, here_grads, arrived_a, held_b
        )
    gate_pre, up_pre, hidden, partial_out = forward(expert_in, gate_up, down)
    gate_sig = jax.nn.sigmoid(gate_pre)

    if swaps:
        here_grads, hidden, partial_out, ways_a, arrived_a, held_b = fence(
            here_grads, hidden, partial_out, ways_a, arrived_a, held_b
        )
        arrived_a += swap(2, plan, ways_a) + swap(3, plan, ways_a)
        ready_a, ways_b = choose(
            (plan[FINAL_ROW:], [*held_a, *arrived_a]), (plan[UP_ROW:FINAL_ROW], held_b)
        )
        home_a = [hand(ready_a[2], 2), hand(ready_a[3], 3)]
        arrived_b = swap(0, plan, ways_b)

    def going_back(keep, other, hidden):
        return jnp.concatenate([add_parts(keep, other), hidden], axis=1)

    if swaps:
        keep, send = split_parts(partial_out)
        other = lax.ppermute(send, "dp", ((0, 1), (1, 0)))
        other, arrived_b = fence(other, arrived_b)
        arrived, outgoing = swap(1, plan, ways_b, going_back, (keep, other, hidden))
        arrived_b += arrived
    else:
        outgoing = jnp.concatenate([scatter_sum(partial_out), hidden], axis=1)

    if swaps:
        outgoing, here_grads, arrived_b, ready_a, home_a, ways_b = fence(
            outgoing, here_grads, arrived_b, ready_a, home_a, ways_b
        )
        rows_a = join_quarters([ready_a[0], hand(ready_a[1], 1), *home_a])
        arrived_b += swap(2, plan, ways_b) + swap(3, plan, ways_b)
        ready_b = choose((plan[FINAL_ROW:], [*held_b, *arrived_b]))
        home_b = hand(ready_b[3], 3)
    back = exchange(outgoing.reshape(experts, per_expert, -1))
    grad_in = jnp.concatenate(gather_features(here_grads.reshape(slots, part_width)), axis=1)
    hidden_grad = lax.dot_general(
        grad_in, down, contract_second, preferred_element_type=jnp.float32
    )
    gate_grad = hidden_grad * up_pre * gate_sig * (1.0 + gate_pre * (1.0 - gate_sig))
    up_grad = hidden_grad * gate_pre * gate_sig
    both_grad = jnp.concatenate([gate_grad, up_grad], axis=1).astype(jnp.bfloat16)
    partial_in = lax.dot_general(
        both_grad, gate_up, contract_second, preferred_element_type=jnp.float32
    ).astype(jnp.bfloat16)
    to_move = reorder([(back, part_width), (grad_blocks, 0)], source)

    if swaps:
        to_move, partial_in, rows_a, ready_b, home_b = fence(
            to_move, partial_in, rows_a, ready_b, home_b
        )
        home_b = [ready_b[0], hand(ready_b[1], 1), hand(ready_b[2], 2), home_b]
    there = exchange(to_move).reshape(slots, hidden_part + part_width)
    there_hidden, there_rows = there[:, :hidden_part], there[:, hidden_part:]
    summed_in = scatter_sum(partial_in)
    back_out = back[:, :, :part_width].reshape(slots, part_width)
    layer_out = sum(
        flat_gates[:, k : k + 1] * jnp.dot(picks[k], back_out, preferred_element_type=jnp.float32)
        for k in range(top_count)
    ).astype(jnp.bfloat16)

    if swaps:
        rows_b = join_quarters(home_b)
        there_hidden, there_rows, summed_in, rows_b, layer_out = fence(
            there_hidden, there_rows, summed_in, rows_b, layer_out
        )
    back_in = exchange(summed_in.reshape(experts, per_expert, part_width))
    token_grad = jnp.dot(
        plain, back_in.reshape(slots, part_width), preferred_element_type=jnp.float32
    )

    there_grads = jnp.concatenate(gather_features(there_rows), axis=1)
    if swaps:
        old_first = jnp.concatenate(
            [rows for a, b in zip(rows_a, rows_b) for rows in (a, b[: quarter - part])]
        )
        old_second = jnp.concatenate([b[quarter - part :] for b in rows_b])
    else:
        old_first, old_second = relocate_spread((moment_first, moment_second), source, experts)
    down_grad = lax.dot_general(
        there_hidden, there_grads, contract_first, preferred_element_type=jnp.float32
    )
    first = 0.9 * old_first.astype(jnp.float32) + 0.1 * down_grad
    second = 0.999 * old_second.astype(jnp.float32) + 0.001 * down_grad * down_grad
    update = first / (jnp.sqrt(second) + 1e-08)
    shape = moment_first.shape
    return (
        layer_out.reshape(tokens.shape),
        token_grad.astype(jnp.bfloat16).reshape(tokens.shape),
        update.astype(jnp.bfloat16).reshape(shape),
        first.astype(jnp.bfloat16).reshape(shape),
        second.astype(jnp.bfloat16).reshape(shape),
    )


def solution(mesh):
    placed = (
        P(None, "expert", "dp"),
        P(None, "expert", "dp"),
        P(None, "expert", None),
        P(None, "expert", None),
        P(),
        P("expert", None, None, "dp"),
        P("expert", "dp", None),
        P("expert", "dp", None),
        P("expert", "dp", None),
    )
    return jax.shard_map(
        per_device,
        mesh=mesh,
        in_specs=placed,
        out_specs=(
            P(None, "expert", "dp"),
            P(None, "expert", "dp"),
            P("expert", "dp", None),
            P("expert", "dp", None),
            P("expert", "dp", None),
        ),
        check_vma=False,
    )
```

```python
import functools

import jax
import jax.numpy as jnp
from jax import lax
from jax.experimental import pallas as pl
from jax.experimental.pallas import tpu as pltpu
from jax.sharding import PartitionSpec as P

contract_first = (((0,), (0,)), ((), ()))
contract_second = (((1,), (1,)), ((), ()))
VMEM_BYTES = 32 * 1024 * 1024
MOST_VMEM_BYTES = 60 * 1024 * 1024


def fence(*values):
    return lax.optimization_barrier(values)


def exchange(blocks):
    return lax.all_to_all(blocks, "expert", split_axis=0, concat_axis=0, tiled=True)


def reorder_kernel(starts, order_ref, *refs):
    out_ref = refs[-1]
    for place in range(out_ref.shape[0]):
        at = 0
        for start, ref in zip(starts, refs[:-1]):
            width = ref.shape[2] - start
            out_ref[place, :, pl.ds(at, width)] = ref[order_ref[place], :, pl.ds(start, width)]
            at += width


def reorder(sources, order):
    whole = pl.BlockSpec(memory_space=pltpu.VMEM)
    blocks = [blocks for blocks, _ in sources]
    starts = [start for _, start in sources]
    width = sum(each.shape[2] - start for each, start in sources)
    return pl.pallas_call(
        functools.partial(reorder_kernel, starts),
        out_shape=jax.ShapeDtypeStruct((*blocks[0].shape[:2], width), blocks[0].dtype),
        in_specs=[pl.BlockSpec(memory_space=pltpu.SMEM)] + [whole] * len(blocks),
        out_specs=whole,
        compiler_params=pltpu.CompilerParams(vmem_limit_bytes=VMEM_BYTES),
        name="reorder",
    )(order, *blocks)


def gather_features(rows):
    parts = lax.axis_size("dp")
    if parts == 2:
        other = lax.ppermute(rows, "dp", ((0, 1), (1, 0)))
        first = lax.axis_index("dp") == 0
        return [jnp.where(first, rows, other), jnp.where(first, other, rows)]
    whole = lax.all_gather(rows, "dp", axis=0, tiled=False)
    return [whole[part] for part in range(parts)]


def split_parts(partial):
    half = partial.shape[1] // 2
    low, high = partial[:, :half], partial[:, half:]
    first = lax.axis_index("dp") == 0
    return jnp.where(first, low, high), jnp.where(first, high, low)


def add_parts(keep, other):
    return (keep.astype(jnp.float32) + other.astype(jnp.float32)).astype(jnp.bfloat16)


def scatter_sum(partial):
    if lax.axis_size("dp") == 2:
        keep, send = split_parts(partial)
        return add_parts(keep, lax.ppermute(send, "dp", ((0, 1), (1, 0))))
    return lax.psum_scatter(partial, "dp", scatter_dimension=1, tiled=True)


def relocate_spread(arrays, source, experts):
    outputs = []
    for array in arrays:
        blocks = array.reshape(experts, array.shape[1] // experts, array.shape[2])
        outputs.append(exchange(reorder([(exchange(blocks), 0)], source)).reshape(array.shape[1:]))
    return outputs


PLANES = 4
GROUP = 4
SWAPS = (((0, 1), (2, 3)), ((1, 2),), ((0, 2),), ((1, 3),), ((0, 3),))
CHAINS = (((0, 1), (1, 2), (2, 3)), ((0, 2), (2, 3)), ((0, 1), (1, 3)))
KIND_ROW, UP_ROW, DOWN_ROW, FINAL_ROW = 0, 4, 8, 12
END_ROW, PAIR_ROW, TURN_ROW = 0, 4, 8


def kind_of(pairs):
    def has(bit):
        return (pairs & (1 << bit)) != 0

    near = jnp.where(has(1), jnp.where(jnp.logical_or(has(0), has(2)), 6, 2), 1)
    kind = jnp.where(has(4), jnp.where(has(0), 8, 4), near)
    kind = jnp.where(has(3), jnp.where(has(2), 7, 3), kind)
    kind = jnp.where(has(5), 5, kind)
    return jnp.where(pairs == 0, 0, kind)


def plan_kernel(where_ref, source_ref, plan_ref, notes_ref):
    plane = where_ref[0]
    member = where_ref[1]
    for index in range(PLANES):
        plan_ref[UP_ROW + index] = GROUP
        plan_ref[DOWN_ROW + index] = GROUP
        notes_ref[END_ROW + index] = 0
        notes_ref[PAIR_ROW + index] = 0
    for slot in range(PLANES * GROUP):
        low = slot // GROUP
        high = source_ref[slot] // GROUP

        @pl.when(high > low)
        def _():
            turn = jnp.int32(PLANES - 1)
            for index in reversed(range(PLANES - 1)):
                turn = jnp.where(notes_ref[END_ROW + index] <= low, index, turn)
            notes_ref[END_ROW + turn] = high
            span = high - low
            bit = jnp.where(span == 3, 5, jnp.where(span == 2, 3 + low, low))
            notes_ref[PAIR_ROW + turn] = notes_ref[PAIR_ROW + turn] | (1 << bit)
            notes_ref[TURN_ROW + slot] = turn

    for index in range(PLANES):
        plan_ref[KIND_ROW + index] = kind_of(notes_ref[PAIR_ROW + index])
    for slot in range(PLANES * GROUP):
        low = slot // GROUP
        other = source_ref[slot]
        high = other // GROUP
        offset = (slot % GROUP) ^ member
        there = (other % GROUP) ^ member

        @pl.when(jnp.logical_and(high == low, plane == low))
        def _():
            plan_ref[FINAL_ROW + offset] = there

        @pl.when(high > low)
        def _():
            turn = notes_ref[TURN_ROW + slot]
            apart = (plan_ref[KIND_ROW + turn] > len(SWAPS)).astype(jnp.int32)

            @pl.when(plane == low)
            def _():
                plan_ref[UP_ROW + turn] = offset
                plan_ref[FINAL_ROW + offset] = GROUP + 2 * turn + apart

            @pl.when(plane == high)
            def _():
                plan_ref[UP_ROW + turn + (DOWN_ROW - UP_ROW) * apart] = there
                plan_ref[FINAL_ROW + there] = GROUP + 2 * turn


def make_plan(source, plane, member):
    smem = pl.BlockSpec(memory_space=pltpu.SMEM)
    return pl.pallas_call(
        plan_kernel,
        out_shape=jax.ShapeDtypeStruct((16,), jnp.int32),
        in_specs=[smem, smem],
        out_specs=smem,
        scratch_shapes=[pltpu.SMEM((TURN_ROW + PLANES * GROUP,), jnp.int32)],
        name="plan",
    )(jnp.stack([plane, member]), source)


def copy_all(loads, stores):
    for load in loads:
        load.start()
    for load, store in zip(loads, stores):
        load.wait()
        store.start()
    for store in stores:
        store.wait()


def cut_kernel(batches, member_ref, *refs):
    count = len(batches)
    first_ref, second_ref, outs = refs[0], refs[1], refs[2 : 2 + GROUP * count]
    staged, in_sems, out_sems = refs[2 + GROUP * count : -2], refs[-2], refs[-1]
    quarter = first_ref.shape[0] // GROUP
    loads, stores = [], []
    for which, parts in enumerate(batches):
        for offset in reversed(range(GROUP)):
            at = 0
            for part, (array, low, high) in enumerate(parts):
                begin = pl.multiple_of((member_ref[0] ^ offset) * quarter + low, 16)
                here = staged[which].at[offset, pl.ds(at, high - low)]
                out = outs[GROUP * which + offset].at[pl.ds(at, high - low)]
                source = (first_ref, second_ref)[array].at[pl.ds(begin, high - low)]
                place = (which * GROUP + offset) * 2 + part
                loads.append(pltpu.make_async_copy(source, here, in_sems.at[place]))
                stores.append(pltpu.make_async_copy(here, out, out_sems.at[place]))
                at += high - low
    copy_all(loads, stores)


def cut(first, second, batches, member):
    width = first.shape[1]
    anywhere = pl.BlockSpec(memory_space=pltpu.HBM)
    shapes = [(sum(high - low for _, low, high in parts), width) for parts in batches]
    amount = 2 * GROUP * len(batches)
    pieces = pl.pallas_call(
        functools.partial(cut_kernel, batches),
        out_shape=[jax.ShapeDtypeStruct(shape, first.dtype) for shape in shapes for _ in range(GROUP)],
        in_specs=[pl.BlockSpec(memory_space=pltpu.SMEM), anywhere, anywhere],
        out_specs=[anywhere] * (GROUP * len(batches)),
        scratch_shapes=[
            *[pltpu.VMEM((GROUP, *shape), first.dtype) for shape in shapes],
            pltpu.SemaphoreType.DMA((amount,)),
            pltpu.SemaphoreType.DMA((amount,)),
        ],
        compiler_params=pltpu.CompilerParams(vmem_limit_bytes=MOST_VMEM_BYTES),
        name="cut",
    )(member[None], first, second)
    return [list(pieces[at : at + GROUP]) for at in range(0, len(pieces), GROUP)]


def choose_kernel(counts, amounts, *refs):
    total = len(counts)
    choices, refs = refs[:total], refs[total:]
    options, refs = refs[: sum(counts)], refs[sum(counts) :]
    outs, staged = refs[: sum(amounts)], refs[sum(amounts) : -2]
    in_sems, out_sems = refs[-2:]
    tasks = []
    for which, choice in enumerate(choices):
        begin, at = sum(counts[:which]), sum(amounts[:which])
        for place in range(amounts[which]):
            tasks.append(
                (
                    choice[place],
                    options[begin : begin + counts[which]],
                    staged[which].at[place],
                    outs[at + place],
                    at + place,
                )
            )
    for named, some, here, out, place in tasks:
        for index, option in enumerate(some):

            @pl.when(named == index)
            def _():
                pltpu.make_async_copy(option, here, in_sems.at[place]).start()

    for named, some, here, out, place in tasks:

        @pl.when(named < len(some))
        def _():
            pltpu.make_async_copy(some[0], here, in_sems.at[place]).wait()
            pltpu.make_async_copy(here, out, out_sems.at[place]).start()

    for named, some, here, out, place in tasks:

        @pl.when(named < len(some))
        def _():
            pltpu.make_async_copy(here, out, out_sems.at[place]).wait()


def choose(*lists):
    anywhere = pl.BlockSpec(memory_space=pltpu.HBM)
    amounts = [choice.shape[0] for choice, _ in lists]
    counts = [len(options) for _, options in lists]
    kinds = [(options[0].shape, options[0].dtype) for _, options in lists]
    chosen = pl.pallas_call(
        functools.partial(choose_kernel, counts, amounts),
        out_shape=[
            jax.ShapeDtypeStruct(shape, dtype)
            for amount, (shape, dtype) in zip(amounts, kinds)
            for _ in range(amount)
        ],
        in_specs=[pl.BlockSpec(memory_space=pltpu.SMEM)] * len(lists) + [anywhere] * sum(counts),
        out_specs=[anywhere] * sum(amounts),
        scratch_shapes=[
            *[pltpu.VMEM((amount, *shape), dtype) for amount, (shape, dtype) in zip(amounts, kinds)],
            pltpu.SemaphoreType.DMA((sum(amounts),)),
            pltpu.SemaphoreType.DMA((sum(amounts),)),
        ],
        compiler_params=pltpu.CompilerParams(vmem_limit_bytes=MOST_VMEM_BYTES),
        name="choose",
    )(*[choice for choice, _ in lists], *[option for _, options in lists for option in options])
    ends = [sum(amounts[: which + 1]) for which in range(len(lists))]
    results = [list(chosen[end - amount : end]) for end, amount in zip(ends, amounts)]
    return results[0] if len(results) == 1 else results


def blank_kernel(*refs):
    pass


def blank(like):
    return pl.pallas_call(
        blank_kernel,
        out_shape=jax.ShapeDtypeStruct(like.shape, like.dtype),
        out_specs=pl.BlockSpec(memory_space=pltpu.HBM),
        name="blank",
    )()


def within_plane(offset):
    return [(index, index ^ offset) for index in range(PLANES * GROUP)]


def between_planes(moves):
    return [(GROUP * a + index, GROUP * b + index) for a, b in moves for index in range(GROUP)]


def turned(moves):
    return tuple((b, a) for a, b in moves)


def swap_nothing(up, down):
    return blank(up), blank(down)


def swap_together(moves, up, down):
    pairs = between_planes(moves + turned(moves))
    return lax.ppermute(up, "expert", pairs), blank(down)


def swap_apart(moves, up, down):
    return (
        lax.ppermute(up, "expert", between_planes(moves)),
        lax.ppermute(down, "expert", between_planes(turned(moves))),
    )


def hand(piece, offset):
    return lax.ppermute(piece, "expert", within_plane(offset))


def swap(turn, plan, ways, work=None, values=()):
    kinds = (
        [swap_nothing]
        + [functools.partial(swap_together, moves) for moves in SWAPS]
        + [functools.partial(swap_apart, moves) for moves in CHAINS]
    )

    def branch(kind):
        if work is None:
            return lambda up, down, values: (kind(up, down), ())
        return lambda up, down, values: (kind(up, down), work(*values))

    arrived, results = lax.switch(
        plan[KIND_ROW + turn],
        [branch(kind) for kind in kinds],
        ways[turn],
        ways[PLANES + turn],
        values,
    )
    return list(arrived) if work is None else (list(arrived), results)


def join_quarters(own):
    member = lax.axis_index("expert") % GROUP
    for bit in (1, 2):
        swap = (member & bit) != 0
        own = [jnp.where(swap, own[offset ^ bit], own[offset]) for offset in range(GROUP)]
    return own


def per_device(
    tokens, cotangent, routes, gates, source, w_gate_up, w_down, moment_first, moment_second
):
    experts = lax.axis_size("expert")
    micro_count, token_count, part_width = tokens.shape
    model_width = w_gate_up.shape[1]
    hidden_part = w_gate_up.shape[3]
    top_count = routes.shape[2]
    capacity = max(2, 3 * token_count * top_count // (2 * experts))
    per_expert = micro_count * capacity
    slots = experts * per_expert
    all_tokens = micro_count * token_count
    swaps = experts == PLANES * GROUP and lax.axis_size("dp") == 2

    pairs = token_count * top_count
    chosen = routes.reshape(micro_count, pairs)
    same = chosen[:, :, None] == chosen[:, None, :]
    order = jnp.arange(pairs, dtype=jnp.int32)
    earlier = order[None, :] < order[:, None]
    position = jnp.sum((same & earlier).astype(jnp.int32), axis=2)
    micro_ids = jnp.arange(micro_count, dtype=jnp.int32)[:, None]
    place = (chosen * per_expert + micro_ids * capacity + position).reshape(all_tokens, top_count)
    slot_ids = jnp.arange(slots, dtype=jnp.int32)
    flat_gates = gates.reshape(all_tokens, top_count)
    matches = [place[:, k][:, None] == slot_ids for k in range(top_count)]
    picks = [match.astype(jnp.bfloat16) for match in matches]
    plain = sum(picks[1:], picks[0])
    slot_gate = sum(
        jnp.sum(jnp.where(matches[k], flat_gates[:, k : k + 1], 0.0), axis=0)
        for k in range(top_count)
    )

    if swaps:
        index = lax.axis_index("expert")
        plane, member = index // GROUP, index % GROUP
        plan = make_plan(source, plane, member)
        quarter = moment_first.shape[1] // GROUP
        part = 3 * quarter // 4
        tokens, (piece_a, piece_b) = fence(
            tokens,
            cut(
                moment_first[0],
                moment_second[0],
                (((0, 0, part),), ((0, part, quarter), (1, 0, quarter))),
                member,
            ),
        )
        held_a = [piece_a[0]] + [hand(piece_a[offset], offset) for offset in range(1, GROUP)]
        near_b = hand(piece_b[1], 1)
    row_tokens = lax.dot_general(
        plain,
        tokens.reshape(all_tokens, part_width),
        contract_first,
        preferred_element_type=jnp.float32,
    ).astype(jnp.bfloat16)
    here_tokens = exchange(row_tokens.reshape(experts, per_expert, part_width))
    row_grads = (
        lax.dot_general(
            plain,
            cotangent.reshape(all_tokens, part_width),
            contract_first,
            preferred_element_type=jnp.float32,
        )
        * slot_gate[:, None]
    ).astype(jnp.bfloat16)
    gate_up = w_gate_up.reshape(model_width, 2 * hidden_part)
    down = w_down.reshape(hidden_part, model_width)

    if swaps:
        here_tokens, row_grads, gate_up, held_a, piece_b, near_b, plan = fence(
            here_tokens, row_grads, gate_up, held_a, piece_b, near_b, plan
        )
        held_b = [piece_b[0], near_b, hand(piece_b[2], 2), hand(piece_b[3], 3)]
        ways_a = choose((plan[UP_ROW:FINAL_ROW], held_a))
        arrived_a = swap(0, plan, ways_a) + swap(1, plan, ways_a)
    grad_blocks = row_grads.reshape(experts, per_expert, part_width)
    here_grads = exchange(grad_blocks)
    expert_in = jnp.concatenate(gather_features(here_tokens.reshape(slots, part_width)), axis=1)

    def forward(expert_in, gate_up, down):
        both = jnp.dot(expert_in, gate_up, preferred_element_type=jnp.float32)
        gate_pre = both[:, :hidden_part]
        up_pre = both[:, hidden_part:]
        hidden = (gate_pre * jax.nn.sigmoid(gate_pre) * up_pre).astype(jnp.bfloat16)
        partial_out = jnp.dot(hidden, down, preferred_element_type=jnp.float32)
        return gate_pre, up_pre, hidden, partial_out.astype(jnp.bfloat16)

    if swaps:
        expert_in, here_grads, arrived_a, held_b = fence(
            expert_in, here_grads, arrived_a, held_b
        )
    gate_pre, up_pre, hidden, partial_out = forward(expert_in, gate_up, down)
    gate_sig = jax.nn.sigmoid(gate_pre)

    if swaps:
        here_grads, hidden, partial_out, ways_a, arrived_a, held_b = fence(
            here_grads, hidden, partial_out, ways_a, arrived_a, held_b
        )
        arrived_a += swap(2, plan, ways_a) + swap(3, plan, ways_a)
        ready_a, ways_b = choose(
            (plan[FINAL_ROW:], [*held_a, *arrived_a]), (plan[UP_ROW:FINAL_ROW], held_b)
        )
        home_a = [hand(ready_a[2], 2), hand(ready_a[3], 3)]
        arrived_b = swap(0, plan, ways_b)

    def going_back(keep, other, hidden):
        return jnp.concatenate([add_parts(keep, other), hidden], axis=1)

    if swaps:
        keep, send = split_parts(partial_out)
        other = lax.ppermute(send, "dp", ((0, 1), (1, 0)))
        other, arrived_b = fence(other, arrived_b)
        arrived, outgoing = swap(1, plan, ways_b, going_back, (keep, other, hidden))
        arrived_b += arrived
    else:
        outgoing = jnp.concatenate([scatter_sum(partial_out), hidden], axis=1)

    if swaps:
        outgoing, here_grads, arrived_b, ready_a, home_a, ways_b = fence(
            outgoing, here_grads, arrived_b, ready_a, home_a, ways_b
        )
        rows_a = join_quarters([ready_a[0], hand(ready_a[1], 1), *home_a])
        arrived_b += swap(2, plan, ways_b) + swap(3, plan, ways_b)
        ready_b = choose((plan[FINAL_ROW:], [*held_b, *arrived_b]))
        home_b = hand(ready_b[3], 3)
    back = exchange(outgoing.reshape(experts, per_expert, -1))
    grad_in = jnp.concatenate(gather_features(here_grads.reshape(slots, part_width)), axis=1)
    hidden_grad = lax.dot_general(
        grad_in, down, contract_second, preferred_element_type=jnp.float32
    )
    gate_grad = hidden_grad * up_pre * gate_sig * (1.0 + gate_pre * (1.0 - gate_sig))
    up_grad = hidden_grad * gate_pre * gate_sig
    both_grad = jnp.concatenate([gate_grad, up_grad], axis=1).astype(jnp.bfloat16)
    partial_in = lax.dot_general(
        both_grad, gate_up, contract_second, preferred_element_type=jnp.float32
    ).astype(jnp.bfloat16)
    to_move = reorder([(back, part_width), (grad_blocks, 0)], source)

    if swaps:
        to_move, partial_in, rows_a, ready_b, home_b = fence(
            to_move, partial_in, rows_a, ready_b, home_b
        )
        middle = ready_b[2].shape[0] // 2
        near_b, early_b = hand(ready_b[1], 1), hand(ready_b[2][:middle], 2)
    there = exchange(to_move).reshape(slots, hidden_part + part_width)
    there_rows = there[:, hidden_part:]
    summed_in = scatter_sum(partial_in)
    back_out = back[:, :, :part_width].reshape(slots, part_width)
    layer_out = sum(
        flat_gates[:, k : k + 1] * jnp.dot(picks[k], back_out, preferred_element_type=jnp.float32)
        for k in range(top_count)
    ).astype(jnp.bfloat16)

    if swaps:
        there, there_rows, summed_in, near_b, early_b, ready_b, layer_out = fence(
            there, there_rows, summed_in, near_b, early_b, ready_b, layer_out
        )
        late_b = hand(ready_b[2][middle:], 2)
    back_in = exchange(summed_in.reshape(experts, per_expert, part_width))
    token_grad = jnp.dot(
        plain, back_in.reshape(slots, part_width), preferred_element_type=jnp.float32
    )

    there_grads = jnp.concatenate(gather_features(there_rows), axis=1)
    if swaps:
        home_b = [ready_b[0], near_b, jnp.concatenate([early_b, late_b]), home_b]
        rows_b = join_quarters(home_b)
        old_first = jnp.concatenate(
            [rows for a, b in zip(rows_a, rows_b) for rows in (a, b[: quarter - part])]
        )
        old_second = jnp.concatenate([b[quarter - part :] for b in rows_b])
    else:
        old_first, old_second = relocate_spread((moment_first, moment_second), source, experts)
    down_grad = lax.dot_general(
        there[:, :hidden_part], there_grads, contract_first, preferred_element_type=jnp.float32
    )
    first = 0.9 * old_first.astype(jnp.float32) + 0.1 * down_grad
    second = 0.999 * old_second.astype(jnp.float32) + 0.001 * down_grad * down_grad
    update = first / (jnp.sqrt(second) + 1e-08)
    shape = moment_first.shape
    return (
        layer_out.reshape(tokens.shape),
        token_grad.astype(jnp.bfloat16).reshape(tokens.shape),
        update.astype(jnp.bfloat16).reshape(shape),
        first.astype(jnp.bfloat16).reshape(shape),
        second.astype(jnp.bfloat16).reshape(shape),
    )


def solution(mesh):
    placed = (
        P(None, "expert", "dp"),
        P(None, "expert", "dp"),
        P(None, "expert", None),
        P(None, "expert", None),
        P(),
        P("expert", None, None, "dp"),
        P("expert", "dp", None),
        P("expert", "dp", None),
        P("expert", "dp", None),
    )
    return jax.shard_map(
        per_device,
        mesh=mesh,
        in_specs=placed,
        out_specs=(
            P(None, "expert", "dp"),
            P(None, "expert", "dp"),
            P("expert", "dp", None),
            P("expert", "dp", None),
            P("expert", "dp", None),
        ),
        check_vma=False,
    )
```

```python
import functools

import jax
import jax.numpy as jnp
from jax import lax
from jax.experimental import pallas as pl
from jax.experimental.pallas import tpu as pltpu
from jax.sharding import PartitionSpec as P

contract_first = (((0,), (0,)), ((), ()))
contract_second = (((1,), (1,)), ((), ()))
VMEM_BYTES = 32 * 1024 * 1024
MOST_VMEM_BYTES = 60 * 1024 * 1024


def fence(*values):
    return lax.optimization_barrier(values)


def exchange(blocks):
    return lax.all_to_all(blocks, "expert", split_axis=0, concat_axis=0, tiled=True)


def reorder_kernel(starts, order_ref, *refs):
    out_ref = refs[-1]
    for place in range(out_ref.shape[0]):
        at = 0
        for start, ref in zip(starts, refs[:-1]):
            width = ref.shape[2] - start
            out_ref[place, :, pl.ds(at, width)] = ref[order_ref[place], :, pl.ds(start, width)]
            at += width


def reorder(sources, order):
    whole = pl.BlockSpec(memory_space=pltpu.VMEM)
    blocks = [blocks for blocks, _ in sources]
    starts = [start for _, start in sources]
    width = sum(each.shape[2] - start for each, start in sources)
    return pl.pallas_call(
        functools.partial(reorder_kernel, starts),
        out_shape=jax.ShapeDtypeStruct((*blocks[0].shape[:2], width), blocks[0].dtype),
        in_specs=[pl.BlockSpec(memory_space=pltpu.SMEM)] + [whole] * len(blocks),
        out_specs=whole,
        compiler_params=pltpu.CompilerParams(vmem_limit_bytes=VMEM_BYTES),
        name="reorder",
    )(order, *blocks)


def gather_features(rows):
    parts = lax.axis_size("dp")
    if parts == 2:
        other = lax.ppermute(rows, "dp", ((0, 1), (1, 0)))
        first = lax.axis_index("dp") == 0
        return [jnp.where(first, rows, other), jnp.where(first, other, rows)]
    whole = lax.all_gather(rows, "dp", axis=0, tiled=False)
    return [whole[part] for part in range(parts)]


def split_parts(partial):
    half = partial.shape[1] // 2
    low, high = partial[:, :half], partial[:, half:]
    first = lax.axis_index("dp") == 0
    return jnp.where(first, low, high), jnp.where(first, high, low)


def add_parts(keep, other):
    return (keep.astype(jnp.float32) + other.astype(jnp.float32)).astype(jnp.bfloat16)


def scatter_sum(partial):
    if lax.axis_size("dp") == 2:
        keep, send = split_parts(partial)
        return add_parts(keep, lax.ppermute(send, "dp", ((0, 1), (1, 0))))
    return lax.psum_scatter(partial, "dp", scatter_dimension=1, tiled=True)


def relocate_spread(arrays, source, experts):
    outputs = []
    for array in arrays:
        blocks = array.reshape(experts, array.shape[1] // experts, array.shape[2])
        outputs.append(exchange(reorder([(exchange(blocks), 0)], source)).reshape(array.shape[1:]))
    return outputs


PLANES = 4
GROUP = 4
SWAPS = (((0, 1), (2, 3)), ((1, 2),), ((0, 2),), ((1, 3),), ((0, 3),))
CHAINS = (((0, 1), (1, 2), (2, 3)), ((0, 2), (2, 3)), ((0, 1), (1, 3)))
KIND_ROW, UP_ROW, DOWN_ROW, FINAL_ROW = 0, 4, 8, 12
END_ROW, PAIR_ROW, TURN_ROW = 0, 4, 8


def kind_of(pairs):
    def has(bit):
        return (pairs & (1 << bit)) != 0

    near = jnp.where(has(1), jnp.where(jnp.logical_or(has(0), has(2)), 6, 2), 1)
    kind = jnp.where(has(4), jnp.where(has(0), 8, 4), near)
    kind = jnp.where(has(3), jnp.where(has(2), 7, 3), kind)
    kind = jnp.where(has(5), 5, kind)
    return jnp.where(pairs == 0, 0, kind)


def plan_kernel(where_ref, source_ref, plan_ref, notes_ref):
    plane = where_ref[0]
    member = where_ref[1]
    for index in range(PLANES):
        plan_ref[UP_ROW + index] = GROUP
        plan_ref[DOWN_ROW + index] = GROUP
        notes_ref[END_ROW + index] = 0
        notes_ref[PAIR_ROW + index] = 0
    for slot in range(PLANES * GROUP):
        low = slot // GROUP
        high = source_ref[slot] // GROUP

        @pl.when(high > low)
        def _():
            turn = jnp.int32(PLANES - 1)
            for index in reversed(range(PLANES - 1)):
                turn = jnp.where(notes_ref[END_ROW + index] <= low, index, turn)
            notes_ref[END_ROW + turn] = high
            span = high - low
            bit = jnp.where(span == 3, 5, jnp.where(span == 2, 3 + low, low))
            notes_ref[PAIR_ROW + turn] = notes_ref[PAIR_ROW + turn] | (1 << bit)
            notes_ref[TURN_ROW + slot] = turn

    for index in range(PLANES):
        plan_ref[KIND_ROW + index] = kind_of(notes_ref[PAIR_ROW + index])
    for slot in range(PLANES * GROUP):
        low = slot // GROUP
        other = source_ref[slot]
        high = other // GROUP
        offset = (slot % GROUP) ^ member
        there = (other % GROUP) ^ member

        @pl.when(jnp.logical_and(high == low, plane == low))
        def _():
            plan_ref[FINAL_ROW + offset] = there

        @pl.when(high > low)
        def _():
            turn = notes_ref[TURN_ROW + slot]
            apart = (plan_ref[KIND_ROW + turn] > len(SWAPS)).astype(jnp.int32)

            @pl.when(plane == low)
            def _():
                plan_ref[UP_ROW + turn] = offset
                plan_ref[FINAL_ROW + offset] = GROUP + 2 * turn + apart

            @pl.when(plane == high)
            def _():
                plan_ref[UP_ROW + turn + (DOWN_ROW - UP_ROW) * apart] = there
                plan_ref[FINAL_ROW + there] = GROUP + 2 * turn


def make_plan(source, plane, member):
    smem = pl.BlockSpec(memory_space=pltpu.SMEM)
    return pl.pallas_call(
        plan_kernel,
        out_shape=jax.ShapeDtypeStruct((16,), jnp.int32),
        in_specs=[smem, smem],
        out_specs=smem,
        scratch_shapes=[pltpu.SMEM((TURN_ROW + PLANES * GROUP,), jnp.int32)],
        name="plan",
    )(jnp.stack([plane, member]), source)


def copy_all(loads, stores):
    for load in loads:
        load.start()
    for load, store in zip(loads, stores):
        load.wait()
        store.start()
    for store in stores:
        store.wait()


def cut_kernel(batches, member_ref, *refs):
    count = len(batches)
    first_ref, second_ref, outs = refs[0], refs[1], refs[2 : 2 + GROUP * count]
    staged, in_sems, out_sems = refs[2 + GROUP * count : -2], refs[-2], refs[-1]
    quarter = first_ref.shape[0] // GROUP
    loads, stores = [], []
    for which, parts in enumerate(batches):
        for offset in reversed(range(GROUP)):
            at = 0
            for part, (array, low, high) in enumerate(parts):
                begin = pl.multiple_of((member_ref[0] ^ offset) * quarter + low, 16)
                here = staged[which].at[offset, pl.ds(at, high - low)]
                out = outs[GROUP * which + offset].at[pl.ds(at, high - low)]
                source = (first_ref, second_ref)[array].at[pl.ds(begin, high - low)]
                place = (which * GROUP + offset) * 2 + part
                loads.append(pltpu.make_async_copy(source, here, in_sems.at[place]))
                stores.append(pltpu.make_async_copy(here, out, out_sems.at[place]))
                at += high - low
    copy_all(loads, stores)


def cut(first, second, batches, member):
    width = first.shape[1]
    anywhere = pl.BlockSpec(memory_space=pltpu.HBM)
    shapes = [(sum(high - low for _, low, high in parts), width) for parts in batches]
    amount = 2 * GROUP * len(batches)
    pieces = pl.pallas_call(
        functools.partial(cut_kernel, batches),
        out_shape=[jax.ShapeDtypeStruct(shape, first.dtype) for shape in shapes for _ in range(GROUP)],
        in_specs=[pl.BlockSpec(memory_space=pltpu.SMEM), anywhere, anywhere],
        out_specs=[anywhere] * (GROUP * len(batches)),
        scratch_shapes=[
            *[pltpu.VMEM((GROUP, *shape), first.dtype) for shape in shapes],
            pltpu.SemaphoreType.DMA((amount,)),
            pltpu.SemaphoreType.DMA((amount,)),
        ],
        compiler_params=pltpu.CompilerParams(vmem_limit_bytes=MOST_VMEM_BYTES),
        name="cut",
    )(member[None], first, second)
    return [list(pieces[at : at + GROUP]) for at in range(0, len(pieces), GROUP)]


def choose_kernel(counts, amounts, *refs):
    total = len(counts)
    choices, refs = refs[:total], refs[total:]
    options, refs = refs[: sum(counts)], refs[sum(counts) :]
    outs, staged = refs[: sum(amounts)], refs[sum(amounts) : -2]
    in_sems, out_sems = refs[-2:]
    tasks = []
    for which, choice in enumerate(choices):
        begin, at = sum(counts[:which]), sum(amounts[:which])
        for place in range(amounts[which]):
            tasks.append(
                (
                    choice[place],
                    options[begin : begin + counts[which]],
                    staged[which].at[place],
                    outs[at + place],
                    at + place,
                )
            )
    for named, some, here, out, place in tasks:
        for index, option in enumerate(some):

            @pl.when(named == index)
            def _():
                pltpu.make_async_copy(option, here, in_sems.at[place]).start()

    for named, some, here, out, place in tasks:

        @pl.when(named < len(some))
        def _():
            pltpu.make_async_copy(some[0], here, in_sems.at[place]).wait()
            pltpu.make_async_copy(here, out, out_sems.at[place]).start()

    for named, some, here, out, place in tasks:

        @pl.when(named < len(some))
        def _():
            pltpu.make_async_copy(here, out, out_sems.at[place]).wait()


def choose(*lists):
    anywhere = pl.BlockSpec(memory_space=pltpu.HBM)
    amounts = [choice.shape[0] for choice, _ in lists]
    counts = [len(options) for _, options in lists]
    kinds = [(options[0].shape, options[0].dtype) for _, options in lists]
    chosen = pl.pallas_call(
        functools.partial(choose_kernel, counts, amounts),
        out_shape=[
            jax.ShapeDtypeStruct(shape, dtype)
            for amount, (shape, dtype) in zip(amounts, kinds)
            for _ in range(amount)
        ],
        in_specs=[pl.BlockSpec(memory_space=pltpu.SMEM)] * len(lists) + [anywhere] * sum(counts),
        out_specs=[anywhere] * sum(amounts),
        scratch_shapes=[
            *[pltpu.VMEM((amount, *shape), dtype) for amount, (shape, dtype) in zip(amounts, kinds)],
            pltpu.SemaphoreType.DMA((sum(amounts),)),
            pltpu.SemaphoreType.DMA((sum(amounts),)),
        ],
        compiler_params=pltpu.CompilerParams(vmem_limit_bytes=MOST_VMEM_BYTES),
        name="choose",
    )(*[choice for choice, _ in lists], *[option for _, options in lists for option in options])
    ends = [sum(amounts[: which + 1]) for which in range(len(lists))]
    results = [list(chosen[end - amount : end]) for end, amount in zip(ends, amounts)]
    return results[0] if len(results) == 1 else results


def blank_kernel(*refs):
    pass


def blank(like):
    return pl.pallas_call(
        blank_kernel,
        out_shape=jax.ShapeDtypeStruct(like.shape, like.dtype),
        out_specs=pl.BlockSpec(memory_space=pltpu.HBM),
        name="blank",
    )()


def within_plane(offset):
    return [(index, index ^ offset) for index in range(PLANES * GROUP)]


def between_planes(moves):
    return [(GROUP * a + index, GROUP * b + index) for a, b in moves for index in range(GROUP)]


def turned(moves):
    return tuple((b, a) for a, b in moves)


def swap_nothing(up, down):
    return blank(up), blank(down)


def swap_together(moves, up, down):
    pairs = between_planes(moves + turned(moves))
    return lax.ppermute(up, "expert", pairs), blank(down)


def swap_apart(moves, up, down):
    return (
        lax.ppermute(up, "expert", between_planes(moves)),
        lax.ppermute(down, "expert", between_planes(turned(moves))),
    )


def hand(piece, offset):
    return lax.ppermute(piece, "expert", within_plane(offset))


def swap(turn, plan, ways, work=None, values=()):
    kinds = (
        [swap_nothing]
        + [functools.partial(swap_together, moves) for moves in SWAPS]
        + [functools.partial(swap_apart, moves) for moves in CHAINS]
    )

    def branch(kind):
        if work is None:
            return lambda up, down, values: (kind(up, down), ())
        return lambda up, down, values: (kind(up, down), work(*values))

    arrived, results = lax.switch(
        plan[KIND_ROW + turn],
        [branch(kind) for kind in kinds],
        ways[turn],
        ways[PLANES + turn],
        values,
    )
    return list(arrived) if work is None else (list(arrived), results)


def join_quarters(own):
    member = lax.axis_index("expert") % GROUP
    for bit in (1, 2):
        swap = (member & bit) != 0
        own = [jnp.where(swap, own[offset ^ bit], own[offset]) for offset in range(GROUP)]
    return own


def per_device(
    tokens, cotangent, routes, gates, source, w_gate_up, w_down, moment_first, moment_second
):
    experts = lax.axis_size("expert")
    micro_count, token_count, part_width = tokens.shape
    model_width = w_gate_up.shape[1]
    hidden_part = w_gate_up.shape[3]
    top_count = routes.shape[2]
    capacity = max(2, 3 * token_count * top_count // (2 * experts))
    per_expert = micro_count * capacity
    slots = experts * per_expert
    all_tokens = micro_count * token_count
    swaps = experts == PLANES * GROUP and lax.axis_size("dp") == 2

    pairs = token_count * top_count
    chosen = routes.reshape(micro_count, pairs)
    same = chosen[:, :, None] == chosen[:, None, :]
    order = jnp.arange(pairs, dtype=jnp.int32)
    earlier = order[None, :] < order[:, None]
    position = jnp.sum((same & earlier).astype(jnp.int32), axis=2)
    micro_ids = jnp.arange(micro_count, dtype=jnp.int32)[:, None]
    place = (chosen * per_expert + micro_ids * capacity + position).reshape(all_tokens, top_count)
    slot_ids = jnp.arange(slots, dtype=jnp.int32)
    flat_gates = gates.reshape(all_tokens, top_count)
    matches = [place[:, k][:, None] == slot_ids for k in range(top_count)]
    picks = [match.astype(jnp.bfloat16) for match in matches]
    plain = sum(picks[1:], picks[0])
    slot_gate = sum(
        jnp.sum(jnp.where(matches[k], flat_gates[:, k : k + 1], 0.0), axis=0)
        for k in range(top_count)
    )

    if swaps:
        index = lax.axis_index("expert")
        plane, member = index // GROUP, index % GROUP
        quarter = moment_first.shape[1] // GROUP
        part = 3 * quarter // 4
        tokens, (piece_a, piece_b) = fence(
            tokens,
            cut(
                moment_first[0],
                moment_second[0],
                (((0, 0, part),), ((0, part, quarter), (1, 0, quarter))),
                member,
            ),
        )
        held_a = [piece_a[0]] + [hand(piece_a[offset], offset) for offset in range(1, GROUP)]
        near_b = hand(piece_b[1], 1)
        held_a, plan_source = fence(held_a, source)
        plan = make_plan(plan_source, plane, member)
    row_tokens = lax.dot_general(
        plain,
        tokens.reshape(all_tokens, part_width),
        contract_first,
        preferred_element_type=jnp.float32,
    ).astype(jnp.bfloat16)
    here_tokens = exchange(row_tokens.reshape(experts, per_expert, part_width))
    row_grads = (
        lax.dot_general(
            plain,
            cotangent.reshape(all_tokens, part_width),
            contract_first,
            preferred_element_type=jnp.float32,
        )
        * slot_gate[:, None]
    ).astype(jnp.bfloat16)
    gate_up = w_gate_up.reshape(model_width, 2 * hidden_part)
    down = w_down.reshape(hidden_part, model_width)

    if swaps:
        here_tokens, row_grads, gate_up, held_a, piece_b, near_b, plan = fence(
            here_tokens, row_grads, gate_up, held_a, piece_b, near_b, plan
        )
        held_b = [piece_b[0], near_b, hand(piece_b[2], 2), hand(piece_b[3], 3)]
        ways_a = choose((plan[UP_ROW:FINAL_ROW], held_a))
        arrived_a = swap(0, plan, ways_a) + swap(1, plan, ways_a)
    grad_blocks = row_grads.reshape(experts, per_expert, part_width)
    here_grads = exchange(grad_blocks)
    expert_in = jnp.concatenate(gather_features(here_tokens.reshape(slots, part_width)), axis=1)

    def forward(expert_in, gate_up, down):
        both = jnp.dot(expert_in, gate_up, preferred_element_type=jnp.float32)
        gate_pre = both[:, :hidden_part]
        up_pre = both[:, hidden_part:]
        hidden = (gate_pre * jax.nn.sigmoid(gate_pre) * up_pre).astype(jnp.bfloat16)
        partial_out = jnp.dot(hidden, down, preferred_element_type=jnp.float32)
        return gate_pre, up_pre, hidden, partial_out.astype(jnp.bfloat16)

    if swaps:
        expert_in, here_grads, arrived_a, held_b = fence(
            expert_in, here_grads, arrived_a, held_b
        )
    gate_pre, up_pre, hidden, partial_out = forward(expert_in, gate_up, down)
    gate_sig = jax.nn.sigmoid(gate_pre)

    if swaps:
        here_grads, hidden, partial_out, ways_a, arrived_a, held_b = fence(
            here_grads, hidden, partial_out, ways_a, arrived_a, held_b
        )
        arrived_a += swap(2, plan, ways_a) + swap(3, plan, ways_a)
        ready_a, ways_b = choose(
            (plan[FINAL_ROW:], [*held_a, *arrived_a]), (plan[UP_ROW:FINAL_ROW], held_b)
        )
        home_a = [hand(ready_a[2], 2), hand(ready_a[3], 3)]
        arrived_b = swap(0, plan, ways_b)

    def going_back(keep, other, hidden):
        return jnp.concatenate([add_parts(keep, other), hidden], axis=1)

    if swaps:
        keep, send = split_parts(partial_out)
        other = lax.ppermute(send, "dp", ((0, 1), (1, 0)))
        other, arrived_b = fence(other, arrived_b)
        arrived, outgoing = swap(1, plan, ways_b, going_back, (keep, other, hidden))
        arrived_b += arrived
    else:
        outgoing = jnp.concatenate([scatter_sum(partial_out), hidden], axis=1)

    if swaps:
        outgoing, here_grads, arrived_b, ready_a, home_a, ways_b = fence(
            outgoing, here_grads, arrived_b, ready_a, home_a, ways_b
        )
        rows_a = join_quarters([ready_a[0], hand(ready_a[1], 1), *home_a])
        arrived_b += swap(2, plan, ways_b) + swap(3, plan, ways_b)
        ready_b = choose((plan[FINAL_ROW:], [*held_b, *arrived_b]))
        home_b = hand(ready_b[3], 3)
    back = exchange(outgoing.reshape(experts, per_expert, -1))
    grad_in = jnp.concatenate(gather_features(here_grads.reshape(slots, part_width)), axis=1)
    hidden_grad = lax.dot_general(
        grad_in, down, contract_second, preferred_element_type=jnp.float32
    )
    gate_grad = hidden_grad * up_pre * gate_sig * (1.0 + gate_pre * (1.0 - gate_sig))
    up_grad = hidden_grad * gate_pre * gate_sig
    both_grad = jnp.concatenate([gate_grad, up_grad], axis=1).astype(jnp.bfloat16)
    partial_in = lax.dot_general(
        both_grad, gate_up, contract_second, preferred_element_type=jnp.float32
    ).astype(jnp.bfloat16)
    to_move = reorder([(back, part_width), (grad_blocks, 0)], source)

    if swaps:
        to_move, partial_in, rows_a, ready_b, home_b = fence(
            to_move, partial_in, rows_a, ready_b, home_b
        )
        middle = ready_b[2].shape[0] // 2
        near_b, early_b = hand(ready_b[1], 1), hand(ready_b[2][:middle], 2)
    there = exchange(to_move).reshape(slots, hidden_part + part_width)
    there_rows = there[:, hidden_part:]
    summed_in = scatter_sum(partial_in)
    back_out = back[:, :, :part_width].reshape(slots, part_width)
    layer_out = sum(
        flat_gates[:, k : k + 1] * jnp.dot(picks[k], back_out, preferred_element_type=jnp.float32)
        for k in range(top_count)
    ).astype(jnp.bfloat16)

    if swaps:
        there, there_rows, summed_in, near_b, early_b, ready_b, layer_out = fence(
            there, there_rows, summed_in, near_b, early_b, ready_b, layer_out
        )
        late_b = hand(ready_b[2][middle:], 2)
    back_in = exchange(summed_in.reshape(experts, per_expert, part_width))
    token_grad = jnp.dot(
        plain, back_in.reshape(slots, part_width), preferred_element_type=jnp.float32
    )

    there_grads = jnp.concatenate(gather_features(there_rows), axis=1)
    if swaps:
        home_b = [ready_b[0], near_b, jnp.concatenate([early_b, late_b]), home_b]
        rows_b = join_quarters(home_b)
        old_first = jnp.concatenate(
            [rows for a, b in zip(rows_a, rows_b) for rows in (a, b[: quarter - part])]
        )
        old_second = jnp.concatenate([b[quarter - part :] for b in rows_b])
    else:
        old_first, old_second = relocate_spread((moment_first, moment_second), source, experts)
    down_grad = lax.dot_general(
        there[:, :hidden_part], there_grads, contract_first, preferred_element_type=jnp.float32
    )
    first = 0.9 * old_first.astype(jnp.float32) + 0.1 * down_grad
    second = 0.999 * old_second.astype(jnp.float32) + 0.001 * down_grad * down_grad
    update = first / (jnp.sqrt(second) + 1e-08)
    shape = moment_first.shape
    return (
        layer_out.reshape(tokens.shape),
        token_grad.astype(jnp.bfloat16).reshape(tokens.shape),
        update.astype(jnp.bfloat16).reshape(shape),
        first.astype(jnp.bfloat16).reshape(shape),
        second.astype(jnp.bfloat16).reshape(shape),
    )


def solution(mesh):
    placed = (
        P(None, "expert", "dp"),
        P(None, "expert", "dp"),
        P(None, "expert", None),
        P(None, "expert", None),
        P(),
        P("expert", None, None, "dp"),
        P("expert", "dp", None),
        P("expert", "dp", None),
        P("expert", "dp", None),
    )
    return jax.shard_map(
        per_device,
        mesh=mesh,
        in_specs=placed,
        out_specs=(
            P(None, "expert", "dp"),
            P(None, "expert", "dp"),
            P("expert", "dp", None),
            P("expert", "dp", None),
            P("expert", "dp", None),
        ),
        check_vma=False,
    )
```
